32 devices in a mesh: dp: 2 (over x), expert: 16 (over z, y, core).
Axes of the slice: x: 2, y: 2, z: 4, core: 2. Of those that a mesh axis runs over, the one named last changes fastest.
Arguments:
- tokens: bfloat16 [2048, 4096], P('expert', 'dp'), may hold values from -6 to 6
- expert_ids: int32 [2048, 8], P('expert'), may hold values from 0 to 15, all different within a row; in each aligned block of 128 rows (0 to 127, 128 to 255, ...) at most 70 rows name the same one
- route_weight: float32 [2048, 8], P('expert'), may hold values from 0.1 to 1
- placement: int32 [16], replicated, may hold values from 0 to 15, each once
- swap_flag: int32 [8], replicated, may hold values 0 or 1
- gate_up: bfloat16 [16, 2, 768, 4096], P('expert', None, 'dp'), may hold values from -0.09375 to 0.09375
- down_weight: bfloat16 [16, 768, 4096], P('expert', None, 'dp'), may hold values from -0.21875 to 0.21875
Outputs:
- moe_out: bfloat16 [2048, 4096], P('expert', 'dp')
- column_load: float32 [16], replicated
- slot_gate_up: bfloat16 [16, 2, 768, 4096], P('expert', None, 'dp')
- slot_down: bfloat16 [16, 768, 4096], P('expert', None, 'dp')
The draws below stay inside these ranges and needn't reach their ends.
Inputs may be any that keep to these rules, and one draw needn't show every extreme that they name: `expert_ids`: within the rows of one device (aligned blocks of 128 tokens) no expert is chosen more than 70 times, and some expert is chosen exactly 70 times; a token's 8 experts differ. A permutation: expert e's weights are in slot placement[e]. swap_flag[p] = 1 means slots p and p + 8 exchange owners.
All inputs are finite; a program needn't handle non-finite values.
Results may differ from the reference program's by a relative error of at most 0.0057.
Values may be sent and summed in bfloat16 or wider, within the bound.
No kernel may reach another device: no remote copies, remote signals or barrier semaphores. Data moves between devices by JAX's collectives and lax.ppermute only.
A program may use at most 128 MiB of HBM per device.

```python
import math
import jax
import jax.numpy as jnp
import numpy as np
from jax import lax

D = 4096
FFN = 768
TOPK = 8
TOK_DEV = 128
EXPERTS = 16
PAIRS = 8
CAP = 70
TOKENS = 2048
N_EXPERT = 16


def with_ends(values, own_key, low, high):
    longest = values.shape.index(max(values.shape))
    spots = []
    for shift in (0, 1):
        where = [jax.random.randint(jax.random.fold_in(own_key, axis), (), 0, length) for axis, length in enumerate(values.shape)]
        where[longest] = (where[longest] + shift) % values.shape[longest]
        spots.append(tuple(where))
    return values.at[spots[0]].set(low).at[spots[1]].set(high)


def levels(rng, dims, cuts, low, top_value):
    level, own = 1.0, jax.random.fold_in(rng, 6)
    for position, blocks in cuts:
        draws = jnp.exp(jax.random.uniform(jax.random.fold_in(own, position), (blocks,), jnp.float32, low / len(cuts), top_value / len(cuts)))
        level = level * jnp.repeat(draws, dims[position] // blocks).reshape([-1 if axis == position else 1 for axis in range(len(dims))])
    return level


def routed_block(stream_key, own, number, rows, amount, top, most, lean):
    order = jax.random.permutation(stream_key, amount)
    packed, usual = portions_of(amount, rows * top, most, lean, True), portions_of(amount, rows * top, most, lean, False)
    places = jnp.arange(amount)

    def named(sizes, offset_by):
        used = int((sizes > 0).sum())
        fixed = max(1, used // 4)
        shifted = fixed + (places - fixed + offset_by * (used - fixed)) % max(1, amount - fixed)
        return jnp.zeros((amount,), jnp.int32).at[order[jnp.where(places < fixed, places, shifted)]].set(jnp.asarray(sizes, jnp.int32))

    sizes = jnp.where(number % 4 == 0, named(packed, number // 4), named(usual, number - number // 4 - 1))
    mixed = jax.random.permutation(jax.random.fold_in(own, 3), amount)
    giver, receiver = mixed[0:amount // 2 * 2:2], mixed[1:amount // 2 * 2:2]
    slack = jnp.minimum(sizes[giver] - 1, most - sizes[receiver]) // 2
    slack = jnp.where((giver == order[0]) | (receiver == order[0]) | (sizes[receiver] == 0), 0, jnp.maximum(slack, 0))
    shifted = jax.random.randint(jax.random.fold_in(own, 4), (amount // 2,), 0, 1 << 20) % (slack + 1)
    sizes = sizes.at[giver].add(-shifted).at[receiver].add(shifted)
    members = jnp.searchsorted(jnp.cumsum(sizes), jnp.arange(rows * top), side="right").astype(jnp.int32)
    listing = members.reshape(top, rows).T
    listing = listing[jax.random.permutation(jax.random.fold_in(own, 1), rows)]
    offset_by = jax.random.randint(jax.random.fold_in(own, 2), (rows, 1), 0, top)
    return jnp.take_along_axis(listing, (jnp.arange(top)[None, :] + offset_by) % top, axis=1)


def portions_of(amount, total, most, skew, full):
    weights = [(1 << 20) // math.isqrt(grade ** skew) + 1 for grade in range(1, amount + 1)]
    largest = most if full else min(most, max(-(-total // amount), total * weights[0] // sum(weights)))
    least = 1 if total - largest >= amount - 1 else 0
    given, spare = [largest] + [least] * (amount - 1), total - largest - least * (amount - 1)
    while spare > 0:
        candidates = [i for i in range(1, amount) if given[i] < largest] or [i for i in range(1, amount) if given[i] < most]
        mass, budget = sum([weights[i] for i in candidates]), spare
        for i in candidates:
            addition = min(most - given[i], max(1, budget * weights[i] // mass), spare)
            given[i] = given[i] + addition
            spare = spare - addition
    return np.array(given)


def noise(own_key, extent, spread, most, pieces=(), kind=jnp.bfloat16):
    array = spread * jax.random.normal(own_key, extent, jnp.float32)
    if pieces:
        array = array * levels(own_key, extent, pieces, -0.22, 0.18)
    return jnp.clip(array, -most, most).astype(kind)


def setup_inputs(seed: int = 0) -> dict:
    arg_keys = jax.random.split(jax.random.key(seed), 8)
    tokens = noise(arg_keys[0], (TOKENS, D), 1.0, 6.0, ((0, 16), (1, 2)))
    expert_ids_keys = jax.random.split(jax.random.fold_in(arg_keys[1], 1), TOKENS // TOK_DEV)
    expert_ids_turns = jax.random.permutation(jax.random.fold_in(arg_keys[1], 3), TOKENS // TOK_DEV)
    expert_ids = jax.vmap(lambda own, number: routed_block(jax.random.fold_in(arg_keys[1], 2), own, number, TOK_DEV, EXPERTS, TOPK, CAP, 1))(expert_ids_keys, expert_ids_turns).reshape((TOKENS, TOPK))
    route_weight = jnp.clip(jnp.exp(math.log(1.0) - 2.3025851 * jax.random.uniform(arg_keys[2], (TOKENS, TOPK), jnp.float32) ** levels(arg_keys[2], (TOKENS, TOPK), ((0, 16),), -0.2, 0.2)), 0.1, 1.0)
    placement = jax.random.permutation(arg_keys[3], EXPERTS).astype(jnp.int32)
    swap_flag = with_ends((jax.random.randint(arg_keys[4], (PAIRS,), 0, 2) < 1).astype(jnp.int32), jax.random.fold_in(arg_keys[4], 1), 0, 1)
    gate_up = noise(arg_keys[5], (EXPERTS, 2, FFN, D), D ** -0.5, 0.09375, ((0, 16), (2, 2)))
    down_weight = noise(arg_keys[6], (EXPERTS, FFN, D), FFN ** -0.5, 0.21875, ((0, 16), (2, 2)))
    return {"tokens": tokens, "expert_ids": expert_ids, "route_weight": route_weight, "placement": placement, "swap_flag": swap_flag, "gate_up": gate_up, "down_weight": down_weight}


def reference(tokens, expert_ids, route_weight, placement, swap_flag, gate_up, down_weight):
    flag_of = swap_flag[placement % PAIRS]
    owner = (placement + PAIRS * flag_of) % EXPERTS
    flat_ids = expert_ids.reshape(-1)
    dest = owner[flat_ids]
    counts = jnp.zeros((EXPERTS,), jnp.int32).at[dest].add(1)
    column_load = counts.astype(jnp.float32) / jnp.float32(TOK_DEV * TOPK)
    slot_range = jnp.arange(EXPERTS, dtype=jnp.int32)
    partner = ((slot_range + PAIRS * swap_flag[slot_range % PAIRS]) % EXPERTS).astype(jnp.int32)
    slot_gate_up = gate_up[partner]
    slot_down = down_weight[partner]
    flat_w = route_weight.reshape(-1)
    tok_of = jnp.arange(TOKENS * TOPK, dtype=jnp.int32) // TOPK
    limit = N_EXPERT * CAP

    def one_expert(total, expert):
        chosen = flat_ids == expert
        order = jnp.cumsum(chosen.astype(jnp.int32)) - 1
        target = jnp.where(chosen, order, limit).astype(jnp.int32)
        rows = jnp.zeros((limit,), jnp.int32).at[target].set(tok_of, mode="drop")
        weights = jnp.zeros((limit,), flat_w.dtype).at[target].set(flat_w, mode="drop")
        slot = placement[expert]
        w_pair = lax.dynamic_index_in_dim(gate_up, slot, 0, keepdims=False).reshape(2 * FFN, D)
        w_down = lax.dynamic_index_in_dim(down_weight, slot, 0, keepdims=False)
        picked = tokens[rows]
        projected = lax.dot_general(picked, w_pair, (((1,), (1,)), ((), ())), preferred_element_type=jnp.float32)
        hidden = (jax.nn.silu(projected[:, :FFN]) * projected[:, FFN:]).astype(jnp.bfloat16)
        result = jnp.dot(hidden, w_down, preferred_element_type=jnp.float32).astype(jnp.bfloat16)
        total = total.at[rows].add(weights[:, None] * result.astype(jnp.float32))
        return total, None

    start = jnp.zeros((TOKENS, D), jnp.float32)
    total, _ = lax.scan(one_expert, start, jnp.arange(EXPERTS, dtype=jnp.int32))
    return total.astype(jnp.bfloat16), column_load, slot_gate_up, slot_down
```

```python
import functools

import jax
import jax.numpy as jnp
from jax import lax
from jax.experimental import pallas as pl
from jax.experimental.pallas import tpu as pltpu
from jax.sharding import PartitionSpec as P


def project_kernel(x_ref, w_ref, out_ref):
    parts, rows, feat = x_ref.shape[1:]
    hid = out_ref.shape[1]
    contract = (((1,), (1,)), ((), ()))
    total = None
    for part in range(parts):
        term = lax.dot_general(
            x_ref[0, part],
            w_ref[:, part * feat : (part + 1) * feat],
            contract,
            preferred_element_type=jnp.float32,
        )
        total = term if total is None else total + term
    gate, up = total[:, :hid], total[:, hid:]
    out_ref[...] = (gate / (1.0 + jnp.exp(-gate)) * up).astype(jnp.bfloat16)


def project(x_all, w_pair):
    blocks, parts, rows, feat = x_all.shape
    hid2, width = w_pair.shape
    hid = hid2 // 2
    return pl.pallas_call(
        project_kernel,
        grid=(blocks,),
        in_specs=[
            pl.BlockSpec((1, parts, rows, feat), lambda i: (i, 0, 0, 0)),
            pl.BlockSpec((hid2, width), lambda i: (0, 0)),
        ],
        out_specs=pl.BlockSpec((rows, hid), lambda i: (i, 0)),
        out_shape=jax.ShapeDtypeStruct((blocks * rows, hid), jnp.bfloat16),
        compiler_params=pltpu.CompilerParams(vmem_limit_bytes=48 << 20),
        cost_estimate=pl.CostEstimate(
            flops=2 * blocks * rows * hid2 * width,
            bytes_accessed=2 * (blocks * rows * width + hid2 * width),
            transcendentals=blocks * rows * hid,
        ),
        name="project",
    )(x_all, w_pair)


def down_kernel(h_ref, w_ref, scale_ref, out_ref):
    result = jnp.dot(h_ref[...], w_ref[...], preferred_element_type=jnp.float32)
    result = result.astype(jnp.bfloat16).astype(jnp.float32)
    out_ref[...] = (result * scale_ref[...]).astype(out_ref.dtype)


def down(hidden, w_down, scale, block):
    rows, hid = hidden.shape
    feat = w_down.shape[1]
    return pl.pallas_call(
        down_kernel,
        grid=(rows // block,),
        in_specs=[
            pl.BlockSpec((block, hid), lambda i: (i, 0)),
            pl.BlockSpec((hid, feat), lambda i: (0, 0)),
            pl.BlockSpec((block, 1), lambda i: (i, 0)),
        ],
        out_specs=pl.BlockSpec((block, feat), lambda i: (i, 0)),
        out_shape=jax.ShapeDtypeStruct((rows, feat), jnp.bfloat16),
        compiler_params=pltpu.CompilerParams(vmem_limit_bytes=48 << 20),
        cost_estimate=pl.CostEstimate(
            flops=2 * rows * hid * feat,
            bytes_accessed=2 * (rows * hid + hid * feat + rows * feat),
            transcendentals=0,
        ),
        name="down",
    )(hidden, w_down, scale)


def exchange(gate_up, down_weight, flags, half):
    pairs = []
    for p in range(half):
        if flags[p]:
            pairs += [(p, p + half), (p + half, p)]
        else:
            pairs += [(p, p), (p + half, p + half)]
    return (
        lax.ppermute(gate_up, "expert", pairs),
        lax.ppermute(down_weight, "expert", pairs),
    )


def swap_weights(gate_up, down_weight, swap_flag, half):
    if half <= 8:
        code = jnp.sum(swap_flag << jnp.arange(half, dtype=jnp.int32))
        branches = [lambda g, d: (g, d)]
        for number in range(1, 1 << half):
            flags = [(number >> p) & 1 for p in range(half)]
            branches.append(functools.partial(exchange, flags=flags, half=half))
        return lax.switch(code, branches, gate_up, down_weight)
    other = exchange(gate_up, down_weight, [1] * half, half)
    own = jnp.take(swap_flag, lax.axis_index("expert") % half) == 1
    return jnp.where(own, other[0], gate_up), jnp.where(own, other[1], down_weight)


def body(tokens, expert_ids, route_weight, placement, swap_flag, gate_up, down_weight):
    ncol = lax.axis_size("expert")
    parts = lax.axis_size("dp")
    half = ncol // 2
    rows, feat = tokens.shape
    topk = expert_ids.shape[1]
    hid = gate_up.shape[2]
    width = gate_up.shape[3]
    me = lax.axis_index("expert")

    slots = jnp.arange(ncol, dtype=jnp.int32)
    picks = expert_ids[:, :, None] == jnp.arange(placement.shape[0], dtype=jnp.int32)
    slot = jnp.sum(jnp.where(picks, placement, 0), axis=2)
    here = slot[:, :, None] == slots
    named = jnp.any(here, axis=1)
    weight = jnp.sum(jnp.where(here, route_weight[:, :, None], 0.0), axis=1)
    table = lax.all_gather(jnp.where(named, weight, -1.0), "expert", axis=0, tiled=True)
    counts = jnp.sum((table >= 0).astype(jnp.float32), axis=0)
    partner = (slots + half * jnp.tile(swap_flag, 2)) % ncol
    column_load = jnp.sum(
        jnp.where(partner[:, None] == slots[None, :], counts[None, :], 0.0), axis=1
    ) / jnp.float32(rows * topk)
    scale = jnp.sum(jnp.where(slots == me, jnp.maximum(table, 0.0), 0.0), axis=1, keepdims=True)

    x_all = lax.all_gather(tokens, ("expert", "dp"), axis=0, tiled=True)
    x_all = x_all.reshape(ncol, parts, rows, feat)
    hidden = project(x_all, gate_up.reshape(2 * hid, width))
    hidden = lax.all_gather(hidden, "dp", axis=1, tiled=True)
    partial = down(hidden, down_weight.reshape(down_weight.shape[1:]), scale, 2 * rows)
    moe_out = lax.psum_scatter(partial, "expert", scatter_dimension=0, tiled=True)

    slot_gate_up, slot_down = swap_weights(gate_up, down_weight, swap_flag, half)
    return (moe_out, column_load, slot_gate_up, slot_down)


def from_behind(value, axis, steps):
    count = lax.axis_size(axis)
    pairs = [(source, (source + steps) % count) for source in range(count)]
    return lax.ppermute(value, axis, pairs)


def swapped_blocks(gate_up, down_weight, swap_flag, pair_index, half):
    incoming_pair = from_behind(gate_up, "expert", half)
    incoming_down = from_behind(down_weight, "expert", half)
    own_column = lax.axis_index("expert")
    own_flag = jnp.sum(jnp.where(pair_index == own_column % half, swap_flag, 0))
    pair_after = jnp.where(own_flag == 1, incoming_pair, gate_up)
    down_after = jnp.where(own_flag == 1, incoming_down, down_weight)
    return (pair_after, down_after)


def dispatched_body(tokens, expert_ids, route_weight, placement, swap_flag, gate_up, down_weight):
    ncol = lax.axis_size("expert")
    half = ncol // 2
    rows_here, feat_here = tokens.shape
    topk = expert_ids.shape[1]
    hid_here = gate_up.shape[2]
    width = gate_up.shape[3]
    capacity = max(4, rows_here * topk * 17 // (16 * ncol) + 2)
    experts_all = placement.shape[0]
    pair_index = jnp.arange(half, dtype=jnp.int32)
    hits = placement[:, None] % half == pair_index[None, :]
    flag_of = jnp.sum(jnp.where(hits, swap_flag[None, :], 0), axis=1)
    moved = (placement + half * flag_of) % ncol
    picks = expert_ids.reshape(-1)[:, None] == jnp.arange(experts_all, dtype=jnp.int32)[None, :]
    moved_dest = jnp.sum(jnp.where(picks, moved[None, :], 0), axis=1)
    columns = jnp.arange(ncol, dtype=jnp.int32)
    local_counts = jnp.sum((moved_dest[:, None] == columns[None, :]).astype(jnp.float32), axis=0)
    totals = lax.psum(local_counts, "expert")
    column_load = totals / jnp.float32(rows_here * topk)
    slot_gate_up, slot_down = swapped_blocks(gate_up, down_weight, swap_flag, pair_index, half)
    col_hits = moved_dest[:, None] == columns[None, :]
    order = jnp.cumsum(col_hits.astype(jnp.int32), axis=0) - 1
    position = jnp.sum(jnp.where(col_hits, order, 0), axis=1)
    slot_index = moved_dest * capacity + position
    w_pair = slot_gate_up.reshape(2 * hid_here, width)
    w_down = slot_down.reshape(slot_down.shape[1], feat_here)
    contract = (((1,), (1,)), ((), ()))
    whole = lax.all_gather(tokens, "dp", axis=1, tiled=True)
    repeated = jnp.repeat(whole, topk, axis=0)
    buffer = jnp.zeros((ncol * capacity, width), jnp.bfloat16).at[slot_index].set(repeated)
    buffer = buffer.reshape(ncol, capacity, width)
    received = lax.all_to_all(buffer, "expert", split_axis=0, concat_axis=0, tiled=True)
    blocks, count, wide = received.shape
    rows = received.reshape(blocks * count, wide)
    projected = lax.dot_general(rows, w_pair, contract, preferred_element_type=jnp.float32)
    hidden = (jax.nn.silu(projected[:, :hid_here]) * projected[:, hid_here:]).astype(jnp.bfloat16)
    mixed = jnp.dot(
        lax.all_gather(hidden, "dp", axis=1, tiled=True), w_down, preferred_element_type=jnp.float32
    )
    result = mixed.astype(jnp.bfloat16).reshape(blocks, count, feat_here)
    returned = lax.all_to_all(result, "expert", split_axis=0, concat_axis=0, tiled=True)
    flat_back = returned.reshape(ncol * capacity, feat_here)
    gathered = flat_back[slot_index].astype(jnp.float32).reshape(rows_here, topk, feat_here)
    moe_out = jnp.sum(gathered * route_weight[:, :, None], axis=1).astype(jnp.bfloat16)
    return (moe_out, column_load, slot_gate_up, slot_down)


def solution(mesh):
    return jax.shard_map(
        body if mesh.shape["expert"] <= 16 else dispatched_body,
        mesh=mesh,
        in_specs=(
            P("expert", "dp"),
            P("expert", None),
            P("expert", None),
            P(),
            P(),
            P("expert", None, "dp", None),
            P("expert", None, "dp"),
        ),
        out_specs=(P("expert", "dp"), P(), P("expert", None, "dp", None), P("expert", None, "dp")),
        check_vma=False,
    )
```

```python
import jax
import jax.numpy as jnp
from jax import lax
from jax.experimental import pallas as pl
from jax.experimental.pallas import tpu as pltpu
from jax.sharding import PartitionSpec as P


def project_kernel(x_ref, w_ref, out_ref):
    blocks, parts, rows, feat = x_ref.shape
    hid = out_ref.shape[1]
    contract = (((1,), (1,)), ((), ()))
    total = None
    for part in range(parts):
        term = lax.dot_general(
            x_ref[:, part].reshape(blocks * rows, feat),
            w_ref[:, part * feat : (part + 1) * feat],
            contract,
            preferred_element_type=jnp.float32,
        )
        total = term if total is None else total + term
    gate, up = total[:, :hid], total[:, hid:]
    out_ref[...] = (gate / (1.0 + jnp.exp(-gate)) * up).astype(jnp.bfloat16)


def project(x_all, w_pair, step):
    blocks, parts, rows, feat = x_all.shape
    hid2, width = w_pair.shape
    hid = hid2 // 2
    return pl.pallas_call(
        project_kernel,
        grid=(blocks // step,),
        in_specs=[
            pl.BlockSpec((step, parts, rows, feat), lambda i: (i, 0, 0, 0)),
            pl.BlockSpec((hid2, width), lambda i: (0, 0)),
        ],
        out_specs=pl.BlockSpec((step * rows, hid), lambda i: (i, 0)),
        out_shape=jax.ShapeDtypeStruct((blocks * rows, hid), jnp.bfloat16),
        compiler_params=pltpu.CompilerParams(vmem_limit_bytes=48 << 20),
        cost_estimate=pl.CostEstimate(
            flops=2 * blocks * rows * hid2 * width,
            bytes_accessed=2 * (blocks * rows * width + hid2 * width),
            transcendentals=blocks * rows * hid,
        ),
        name="project",
    )(x_all, w_pair)


def down_kernel(h_ref, w_ref, scale_ref, out_ref):
    result = jnp.dot(h_ref[...], w_ref[...], preferred_element_type=jnp.float32)
    result = result.astype(jnp.bfloat16).astype(jnp.float32)
    out_ref[...] = (result * scale_ref[...]).astype(out_ref.dtype)


def down(hidden, w_down, scale, block):
    rows, hid = hidden.shape
    feat = w_down.shape[1]
    return pl.pallas_call(
        down_kernel,
        grid=(rows // block,),
        in_specs=[
            pl.BlockSpec((block, hid), lambda i: (i, 0)),
            pl.BlockSpec((hid, feat), lambda i: (0, 0)),
            pl.BlockSpec((block, 1), lambda i: (i, 0)),
        ],
        out_specs=pl.BlockSpec((block, feat), lambda i: (i, 0)),
        out_shape=jax.ShapeDtypeStruct((rows, feat), jnp.bfloat16),
        compiler_params=pltpu.CompilerParams(vmem_limit_bytes=48 << 20),
        cost_estimate=pl.CostEstimate(
            flops=2 * rows * hid * feat,
            bytes_accessed=2 * (rows * hid + hid * feat + rows * feat),
            transcendentals=0,
        ),
        name="down",
    )(hidden, w_down, scale)


def exchange(value, own, half):
    pairs = [(p, (p + half) % (2 * half)) for p in range(2 * half)]
    return lax.cond(own, lambda v: lax.ppermute(v, "expert", pairs), lambda v: v, value)


def body(tokens, expert_ids, route_weight, placement, swap_flag, gate_up, down_weight):
    ncol = lax.axis_size("expert")
    parts = lax.axis_size("dp")
    half = ncol // 2
    rows, feat = tokens.shape
    topk = expert_ids.shape[1]
    hid = gate_up.shape[2]
    width = gate_up.shape[3]
    me = lax.axis_index("expert")

    slots = jnp.arange(ncol, dtype=jnp.int32)
    picks = expert_ids[:, :, None] == jnp.arange(placement.shape[0], dtype=jnp.int32)
    slot = jnp.sum(jnp.where(picks, placement, 0), axis=2)
    here = slot[:, :, None] == slots
    named = jnp.any(here, axis=1)
    weight = jnp.sum(jnp.where(here, route_weight[:, :, None], 0.0), axis=1)
    table = lax.all_gather(jnp.where(named, weight, -1.0), "expert", axis=0, tiled=True)
    counts = jnp.sum((table >= 0).astype(jnp.float32), axis=0)
    partner = (slots + half * jnp.tile(swap_flag, 2)) % ncol
    column_load = jnp.sum(
        jnp.where(partner[:, None] == slots[None, :], counts[None, :], 0.0), axis=1
    ) / jnp.float32(rows * topk)
    scale = jnp.sum(jnp.where(slots == me, jnp.maximum(table, 0.0), 0.0), axis=1, keepdims=True)

    x_all = lax.all_gather(tokens, ("expert", "dp"), axis=0, tiled=True)
    own = jnp.sum(jnp.where(slots[:half] == me % half, swap_flag, 0)) == 1
    slot_gate_up = exchange(gate_up, own, half)
    x_all, slot_gate_up = lax.optimization_barrier((x_all, slot_gate_up))
    x_all = x_all.reshape(ncol, parts, rows, feat)
    hidden = project(x_all, gate_up.reshape(2 * hid, width), 4)
    hidden = lax.all_gather(hidden, "dp", axis=1, tiled=True)
    partial = down(hidden, down_weight.reshape(down_weight.shape[1:]), scale, 2 * rows)
    partial, late_down = lax.optimization_barrier((partial, down_weight))
    moe_out = lax.psum_scatter(partial, "expert", scatter_dimension=0, tiled=True)
    slot_down = exchange(late_down, own, half)
    return (moe_out, column_load, slot_gate_up, slot_down)


def from_behind(value, axis, steps):
    count = lax.axis_size(axis)
    pairs = [(source, (source + steps) % count) for source in range(count)]
    return lax.ppermute(value, axis, pairs)


def swapped_blocks(gate_up, down_weight, swap_flag, pair_index, half):
    incoming_pair = from_behind(gate_up, "expert", half)
    incoming_down = from_behind(down_weight, "expert", half)
    own_column = lax.axis_index("expert")
    own_flag = jnp.sum(jnp.where(pair_index == own_column % half, swap_flag, 0))
    pair_after = jnp.where(own_flag == 1, incoming_pair, gate_up)
    down_after = jnp.where(own_flag == 1, incoming_down, down_weight)
    return (pair_after, down_after)


def dispatched_body(tokens, expert_ids, route_weight, placement, swap_flag, gate_up, down_weight):
    ncol = lax.axis_size("expert")
    half = ncol // 2
    rows_here, feat_here = tokens.shape
    topk = expert_ids.shape[1]
    hid_here = gate_up.shape[2]
    width = gate_up.shape[3]
    capacity = max(4, rows_here * topk * 17 // (16 * ncol) + 2)
    experts_all = placement.shape[0]
    pair_index = jnp.arange(half, dtype=jnp.int32)
    hits = placement[:, None] % half == pair_index[None, :]
    flag_of = jnp.sum(jnp.where(hits, swap_flag[None, :], 0), axis=1)
    moved = (placement + half * flag_of) % ncol
    picks = expert_ids.reshape(-1)[:, None] == jnp.arange(experts_all, dtype=jnp.int32)[None, :]
    moved_dest = jnp.sum(jnp.where(picks, moved[None, :], 0), axis=1)
    columns = jnp.arange(ncol, dtype=jnp.int32)
    local_counts = jnp.sum((moved_dest[:, None] == columns[None, :]).astype(jnp.float32), axis=0)
    totals = lax.psum(local_counts, "expert")
    column_load = totals / jnp.float32(rows_here * topk)
    slot_gate_up, slot_down = swapped_blocks(gate_up, down_weight, swap_flag, pair_index, half)
    col_hits = moved_dest[:, None] == columns[None, :]
    order = jnp.cumsum(col_hits.astype(jnp.int32), axis=0) - 1
    position = jnp.sum(jnp.where(col_hits, order, 0), axis=1)
    slot_index = moved_dest * capacity + position
    w_pair = slot_gate_up.reshape(2 * hid_here, width)
    w_down = slot_down.reshape(slot_down.shape[1], feat_here)
    contract = (((1,), (1,)), ((), ()))
    whole = lax.all_gather(tokens, "dp", axis=1, tiled=True)
    repeated = jnp.repeat(whole, topk, axis=0)
    buffer = jnp.zeros((ncol * capacity, width), jnp.bfloat16).at[slot_index].set(repeated)
    buffer = buffer.reshape(ncol, capacity, width)
    received = lax.all_to_all(buffer, "expert", split_axis=0, concat_axis=0, tiled=True)
    blocks, count, wide = received.shape
    rows = received.reshape(blocks * count, wide)
    projected = lax.dot_general(rows, w_pair, contract, preferred_element_type=jnp.float32)
    hidden = (jax.nn.silu(projected[:, :hid_here]) * projected[:, hid_here:]).astype(jnp.bfloat16)
    mixed = jnp.dot(
        lax.all_gather(hidden, "dp", axis=1, tiled=True), w_down, preferred_element_type=jnp.float32
    )
    result = mixed.astype(jnp.bfloat16).reshape(blocks, count, feat_here)
    returned = lax.all_to_all(result, "expert", split_axis=0, concat_axis=0, tiled=True)
    flat_back = returned.reshape(ncol * capacity, feat_here)
    gathered = flat_back[slot_index].astype(jnp.float32).reshape(rows_here, topk, feat_here)
    moe_out = jnp.sum(gathered * route_weight[:, :, None], axis=1).astype(jnp.bfloat16)
    return (moe_out, column_load, slot_gate_up, slot_down)


def solution(mesh):
    return jax.shard_map(
        body if mesh.shape["expert"] <= 16 else dispatched_body,
        mesh=mesh,
        in_specs=(
            P("expert", "dp"),
            P("expert", None),
            P("expert", None),
            P(),
            P(),
            P("expert", None, "dp", None),
            P("expert", None, "dp"),
        ),
        out_specs=(P("expert", "dp"), P(), P("expert", None, "dp", None), P("expert", None, "dp")),
        check_vma=False,
    )
```

```python
import jax
import jax.numpy as jnp
from jax import lax
from jax.experimental import pallas as pl
from jax.experimental.pallas import tpu as pltpu
from jax.sharding import Mesh
from jax.sharding import PartitionSpec as P

COLUMN = ("z", "y", "core")


def project_kernel(x_ref, w_ref, out_ref):
    parts, blocks, rows, feat = x_ref.shape
    hid = out_ref.shape[1]
    contract = (((1,), (1,)), ((), ()))
    total = None
    for part in range(parts):
        term = lax.dot_general(
            x_ref[part].reshape(blocks * rows, feat),
            w_ref[:, part * feat : (part + 1) * feat],
            contract,
            preferred_element_type=jnp.float32,
        )
        total = term if total is None else total + term
    gate, up = total[:, :hid], total[:, hid:]
    out_ref[...] = (gate / (1.0 + jnp.exp(-gate)) * up).astype(jnp.bfloat16)


def project(x_all, w_pair, step):
    parts, blocks, rows, feat = x_all.shape
    hid2, width = w_pair.shape
    hid = hid2 // 2
    return pl.pallas_call(
        project_kernel,
        grid=(blocks // step,),
        in_specs=[
            pl.BlockSpec((parts, step, rows, feat), lambda i: (0, i, 0, 0)),
            pl.BlockSpec((hid2, width), lambda i: (0, 0)),
        ],
        out_specs=pl.BlockSpec((step * rows, hid), lambda i: (i, 0)),
        out_shape=jax.ShapeDtypeStruct((blocks * rows, hid), jnp.bfloat16),
        compiler_params=pltpu.CompilerParams(vmem_limit_bytes=48 << 20),
        cost_estimate=pl.CostEstimate(
            flops=2 * blocks * rows * hid2 * width,
            bytes_accessed=2 * (blocks * rows * width + hid2 * width),
            transcendentals=blocks * rows * hid,
        ),
        name="project",
    )(x_all, w_pair)


def down_kernel(first_ref, own_ref, other_ref, w_ref, scale_ref, *rest):
    out_ref = rest[-1]
    hid = own_ref.shape[1]
    mine = pl.ds(pl.multiple_of(first_ref[0], hid), hid)
    theirs = pl.ds(pl.multiple_of(hid - first_ref[0], hid), hid)
    result = jnp.dot(own_ref[...], w_ref[mine, :], preferred_element_type=jnp.float32)
    result += jnp.dot(other_ref[...], w_ref[theirs, :], preferred_element_type=jnp.float32)
    result = result.astype(jnp.bfloat16).astype(jnp.float32) * scale_ref[...]
    if len(rest) == 2:
        result += rest[0][...].astype(jnp.float32)
    out_ref[...] = result.astype(out_ref.dtype)


def down(first, own, other, w_down, scale, block, extra=()):
    rows, hid = own.shape
    depth, feat = w_down.shape
    tall = pl.BlockSpec((block, feat), lambda i, s: (i, 0))
    return pl.pallas_call(
        down_kernel,
        grid_spec=pltpu.PrefetchScalarGridSpec(
            num_scalar_prefetch=1,
            grid=(rows // block,),
            in_specs=[
                pl.BlockSpec((block, hid), lambda i, s: (i, 0)),
                pl.BlockSpec((block, hid), lambda i, s: (i, 0)),
                pl.BlockSpec((depth, feat), lambda i, s: (0, 0)),
                pl.BlockSpec((block, 1), lambda i, s: (i, 0)),
            ]
            + [tall] * len(extra),
            out_specs=tall,
        ),
        out_shape=jax.ShapeDtypeStruct((rows, feat), jnp.bfloat16),
        compiler_params=pltpu.CompilerParams(vmem_limit_bytes=48 << 20),
        cost_estimate=pl.CostEstimate(
            flops=2 * rows * depth * feat,
            bytes_accessed=2 * (rows * depth + depth * feat + rows * feat),
            transcendentals=0,
        ),
        name="down",
    )(first, own, other, w_down, scale, *extra)


def swap_ends(value, axis):
    return lax.ppermute(value, axis, [(0, 1), (1, 0)])


def exchange(value, own):
    count = lax.axis_size("z")
    pairs = [(p, (p + count // 2) % count) for p in range(count)]
    return lax.cond(own, lambda v: lax.ppermute(v, "z", pairs), lambda v: v, value)


def after(value, *others):
    return lax.optimization_barrier((value, *others))[0]


def body(tokens, expert_ids, route_weight, placement, swap_flag, gate_up, down_weight):
    nz, ny, ncore = (lax.axis_size(name) for name in COLUMN)
    parts = lax.axis_size("dp")
    ncol = nz * ny * ncore
    half = ncol // 2
    rows, feat = tokens.shape
    topk = expert_ids.shape[1]
    hid = gate_up.shape[2]
    width = gate_up.shape[3]
    me = lax.axis_index(COLUMN)
    core = lax.axis_index("core")
    y = lax.axis_index("y")

    slots = jnp.arange(ncol, dtype=jnp.int32)
    own = jnp.sum(jnp.where(slots[:half] == me % half, swap_flag, 0)) == 1
    gate_piece, up_piece = gate_up[0, 0], gate_up[0, 1]
    cut = hid // 2
    depth = down_weight.shape[1] // 2

    along_z = lax.all_gather(tokens, "z", axis=0)
    up_first = exchange(up_piece[:cut], own)

    picks = expert_ids[:, :, None] == jnp.arange(placement.shape[0], dtype=jnp.int32)
    slot = jnp.sum(jnp.where(picks, placement, 0), axis=2)
    here = slot[:, :, None] == slots
    named = jnp.any(here, axis=1)
    weight = jnp.sum(jnp.where(here, route_weight[:, :, None], 0.0), axis=1)
    table = jnp.where(named, weight, -1.0)

    along_z, up_first = lax.optimization_barrier((along_z, up_first))
    plane = lax.all_gather(along_z, ("dp", "y"), axis=0)
    gate_new = exchange(after(gate_piece, along_z), own)
    table = lax.all_gather(after(table, along_z), COLUMN, axis=0, tiled=True)

    counts = jnp.sum((table >= 0).astype(jnp.float32), axis=0)
    partner = (slots + half * jnp.tile(swap_flag, 2)) % ncol
    column_load = jnp.sum(
        jnp.where(partner[:, None] == slots[None, :], counts[None, :], 0.0), axis=1
    ) / jnp.float32(rows * topk)
    scale = jnp.sum(jnp.where(slots == me, jnp.maximum(table, 0.0), 0.0), axis=1)
    scale = scale.reshape(nz, ny, ncore, rows).transpose(2, 1, 0, 3)
    scale = scale.reshape(ncore, ny * nz * rows, 1)
    scale_own = lax.dynamic_index_in_dim(scale, core, 0, keepdims=False)
    scale_other = lax.dynamic_index_in_dim(scale, 1 - core, 0, keepdims=False)

    plane, gate_new = lax.optimization_barrier((plane, gate_new))
    plane = plane.reshape(parts, ny * nz, rows, feat)
    plane_other = swap_ends(plane, "core")
    w_pair = gate_up.reshape(2 * hid, width)
    hidden_own = project(plane, w_pair, 2)
    crossed_own = swap_ends(hidden_own, "dp")
    plane_other, hidden_own = lax.optimization_barrier((plane_other, hidden_own))
    hidden_other = project(plane_other, w_pair, 2)
    crossed_other = swap_ends(hidden_other, "dp")
    up_second = exchange(after(up_piece[cut:], hidden_other), own)
    crossed_other, up_second = lax.optimization_barrier((crossed_other, up_second))

    w_down = down_weight.reshape(down_weight.shape[1:])
    first = (lax.axis_index("dp") * hid).astype(jnp.int32).reshape(1)
    sent = down(first, hidden_other, crossed_other, w_down, scale_other, 2 * rows)
    received = swap_ends(sent, "core")
    chip = down(first, hidden_own, crossed_own, w_down, scale_own, 2 * rows, (received,))
    chip = chip.reshape(ny, nz * rows, feat)
    from_y = swap_ends(lax.dynamic_index_in_dim(chip, 1 - y, 0, keepdims=False), "y")
    down_first = exchange(after(w_down[:depth], chip), own)
    kept = lax.dynamic_index_in_dim(chip, y, 0, keepdims=False)
    from_y, down_first = lax.optimization_barrier((from_y, down_first))
    line = (kept.astype(jnp.float32) + from_y.astype(jnp.float32)).astype(jnp.bfloat16)
    moe_out = lax.psum_scatter(line, "z", scatter_dimension=0, tiled=True)
    down_second = exchange(after(w_down[depth:], line), own)

    slot_gate_up = jnp.stack([gate_new, jnp.concatenate([up_first, up_second])])[None]
    slot_down = jnp.concatenate([down_first, down_second])[None]
    return (moe_out, column_load, slot_gate_up, slot_down)


def from_behind(value, axis, steps):
    count = lax.axis_size(axis)
    pairs = [(source, (source + steps) % count) for source in range(count)]
    return lax.ppermute(value, axis, pairs)


def swapped_blocks(gate_up, down_weight, swap_flag, pair_index, half):
    incoming_pair = from_behind(gate_up, "expert", half)
    incoming_down = from_behind(down_weight, "expert", half)
    own_column = lax.axis_index("expert")
    own_flag = jnp.sum(jnp.where(pair_index == own_column % half, swap_flag, 0))
    pair_after = jnp.where(own_flag == 1, incoming_pair, gate_up)
    down_after = jnp.where(own_flag == 1, incoming_down, down_weight)
    return (pair_after, down_after)


def dispatched_body(tokens, expert_ids, route_weight, placement, swap_flag, gate_up, down_weight):
    ncol = lax.axis_size("expert")
    half = ncol // 2
    rows_here, feat_here = tokens.shape
    topk = expert_ids.shape[1]
    hid_here = gate_up.shape[2]
    width = gate_up.shape[3]
    capacity = max(4, rows_here * topk * 17 // (16 * ncol) + 2)
    experts_all = placement.shape[0]
    pair_index = jnp.arange(half, dtype=jnp.int32)
    hits = placement[:, None] % half == pair_index[None, :]
    flag_of = jnp.sum(jnp.where(hits, swap_flag[None, :], 0), axis=1)
    moved = (placement + half * flag_of) % ncol
    picks = expert_ids.reshape(-1)[:, None] == jnp.arange(experts_all, dtype=jnp.int32)[None, :]
    moved_dest = jnp.sum(jnp.where(picks, moved[None, :], 0), axis=1)
    columns = jnp.arange(ncol, dtype=jnp.int32)
    local_counts = jnp.sum((moved_dest[:, None] == columns[None, :]).astype(jnp.float32), axis=0)
    totals = lax.psum(local_counts, "expert")
    column_load = totals / jnp.float32(rows_here * topk)
    slot_gate_up, slot_down = swapped_blocks(gate_up, down_weight, swap_flag, pair_index, half)
    col_hits = moved_dest[:, None] == columns[None, :]
    order = jnp.cumsum(col_hits.astype(jnp.int32), axis=0) - 1
    position = jnp.sum(jnp.where(col_hits, order, 0), axis=1)
    slot_index = moved_dest * capacity + position
    w_pair = slot_gate_up.reshape(2 * hid_here, width)
    w_down = slot_down.reshape(slot_down.shape[1], feat_here)
    contract = (((1,), (1,)), ((), ()))
    whole = lax.all_gather(tokens, "dp", axis=1, tiled=True)
    repeated = jnp.repeat(whole, topk, axis=0)
    buffer = jnp.zeros((ncol * capacity, width), jnp.bfloat16).at[slot_index].set(repeated)
    buffer = buffer.reshape(ncol, capacity, width)
    received = lax.all_to_all(buffer, "expert", split_axis=0, concat_axis=0, tiled=True)
    blocks, count, wide = received.shape
    rows = received.reshape(blocks * count, wide)
    projected = lax.dot_general(rows, w_pair, contract, preferred_element_type=jnp.float32)
    hidden = (jax.nn.silu(projected[:, :hid_here]) * projected[:, hid_here:]).astype(jnp.bfloat16)
    mixed = jnp.dot(
        lax.all_gather(hidden, "dp", axis=1, tiled=True), w_down, preferred_element_type=jnp.float32
    )
    result = mixed.astype(jnp.bfloat16).reshape(blocks, count, feat_here)
    returned = lax.all_to_all(result, "expert", split_axis=0, concat_axis=0, tiled=True)
    flat_back = returned.reshape(ncol * capacity, feat_here)
    gathered = flat_back[slot_index].astype(jnp.float32).reshape(rows_here, topk, feat_here)
    moe_out = jnp.sum(gathered * route_weight[:, :, None], axis=1).astype(jnp.bfloat16)
    return (moe_out, column_load, slot_gate_up, slot_down)


def solution(mesh):
    expert = mesh.shape["expert"]
    if expert > 16:
        run, names, column = dispatched_body, mesh, "expert"
    else:
        shape = (mesh.shape["dp"], expert // 4, 2, 2)
        run, names, column = body, Mesh(mesh.devices.reshape(shape), ("dp", *COLUMN)), COLUMN
    return jax.shard_map(
        run,
        mesh=names,
        in_specs=(
            P(column, "dp"),
            P(column, None),
            P(column, None),
            P(),
            P(),
            P(column, None, "dp", None),
            P(column, None, "dp"),
        ),
        out_specs=(P(column, "dp"), P(), P(column, None, "dp", None), P(column, None, "dp")),
        check_vma=False,
    )
```

```python
import jax
import jax.numpy as jnp
from jax import lax
from jax.experimental import pallas as pl
from jax.experimental.pallas import tpu as pltpu
from jax.sharding import Mesh
from jax.sharding import PartitionSpec as P

COLUMN = ("z", "y", "core")


def project_kernel(x_ref, w_ref, out_ref):
    parts, blocks, rows, feat = x_ref.shape
    hid = out_ref.shape[1]
    contract = (((1,), (1,)), ((), ()))
    total = None
    for part in range(parts):
        term = lax.dot_general(
            x_ref[part].reshape(blocks * rows, feat),
            w_ref[:, part * feat : (part + 1) * feat],
            contract,
            preferred_element_type=jnp.float32,
        )
        total = term if total is None else total + term
    gate, up = total[:, :hid], total[:, hid:]
    out_ref[...] = (gate / (1.0 + jnp.exp(-gate)) * up).astype(jnp.bfloat16)


def project(x_all, w_pair, step):
    parts, blocks, rows, feat = x_all.shape
    hid2, width = w_pair.shape
    hid = hid2 // 2
    return pl.pallas_call(
        project_kernel,
        grid=(blocks // step,),
        in_specs=[
            pl.BlockSpec((parts, step, rows, feat), lambda i: (0, i, 0, 0)),
            pl.BlockSpec((hid2, width), lambda i: (0, 0)),
        ],
        out_specs=pl.BlockSpec((step * rows, hid), lambda i: (i, 0)),
        out_shape=jax.ShapeDtypeStruct((blocks * rows, hid), jnp.bfloat16),
        compiler_params=pltpu.CompilerParams(vmem_limit_bytes=48 << 20),
        cost_estimate=pl.CostEstimate(
            flops=2 * blocks * rows * hid2 * width,
            bytes_accessed=2 * (blocks * rows * width + hid2 * width),
            transcendentals=blocks * rows * hid,
        ),
        name="project",
    )(x_all, w_pair)


def down_kernel(first_ref, own_ref, other_ref, w_ref, scale_ref, *rest):
    out_ref = rest[-1]
    hid = own_ref.shape[1]
    mine = pl.ds(pl.multiple_of(first_ref[0], hid), hid)
    theirs = pl.ds(pl.multiple_of(hid - first_ref[0], hid), hid)
    result = jnp.dot(own_ref[...], w_ref[mine, :], preferred_element_type=jnp.float32)
    result += jnp.dot(other_ref[...], w_ref[theirs, :], preferred_element_type=jnp.float32)
    result = result.astype(jnp.bfloat16).astype(jnp.float32) * scale_ref[...]
    if len(rest) == 2:
        result += rest[0][...].astype(jnp.float32)
    out_ref[...] = result.astype(out_ref.dtype)


def down(first, own, other, w_down, scale, block, extra=()):
    rows, hid = own.shape
    depth, feat = w_down.shape
    tall = pl.BlockSpec((block, feat), lambda i, s: (i, 0))
    return pl.pallas_call(
        down_kernel,
        grid_spec=pltpu.PrefetchScalarGridSpec(
            num_scalar_prefetch=1,
            grid=(rows // block,),
            in_specs=[
                pl.BlockSpec((block, hid), lambda i, s: (i, 0)),
                pl.BlockSpec((block, hid), lambda i, s: (i, 0)),
                pl.BlockSpec((depth, feat), lambda i, s: (0, 0)),
                pl.BlockSpec((block, 1), lambda i, s: (i, 0)),
            ]
            + [tall] * len(extra),
            out_specs=tall,
        ),
        out_shape=jax.ShapeDtypeStruct((rows, feat), jnp.bfloat16),
        compiler_params=pltpu.CompilerParams(vmem_limit_bytes=48 << 20),
        cost_estimate=pl.CostEstimate(
            flops=2 * rows * depth * feat,
            bytes_accessed=2 * (rows * depth + depth * feat + rows * feat),
            transcendentals=0,
        ),
        name="down",
    )(first, own, other, w_down, scale, *extra)


def swap_ends(value, axis):
    return lax.ppermute(value, axis, [(0, 1), (1, 0)])


def opposite(value):
    count = lax.axis_size("z")
    return lax.ppermute(value, "z", [(p, (p + count // 2) % count) for p in range(count)])


def after(value, *others):
    return lax.optimization_barrier((value, *others))[0]


def add(left, right):
    return (left.astype(jnp.float32) + right.astype(jnp.float32)).astype(jnp.bfloat16)


def body(tokens, expert_ids, route_weight, placement, swap_flag, gate_up, down_weight):
    nz, ny, ncore = (lax.axis_size(name) for name in COLUMN)
    parts = lax.axis_size("dp")
    ncol = nz * ny * ncore
    half = ncol // 2
    rows, feat = tokens.shape
    topk = expert_ids.shape[1]
    hid = gate_up.shape[2]
    width = gate_up.shape[3]
    me = lax.axis_index(COLUMN)
    core = lax.axis_index("core")
    y = lax.axis_index("y")
    w_pair = gate_up.reshape(2 * hid, width)
    w_down = down_weight.reshape(down_weight.shape[1:])
    depth = w_down.shape[0] // 2

    slots = jnp.arange(ncol, dtype=jnp.int32)
    own = jnp.sum(jnp.where(slots[:half] == me % half, swap_flag, 0)) == 1
    sibling = jnp.sum(jnp.where(slots[:half] == (me + 1 - 2 * core) % half, swap_flag, 0)) == 1
    alone = own & ~sibling
    both = own & sibling

    along_z = lax.all_gather(tokens, "z", axis=0)
    heads, tails = (w_pair[:hid], w_down[:depth]), (w_pair[hid:], w_down[depth:])
    lanes = tuple(
        jnp.where(own, head, swap_ends(tail, "core")) for head, tail in zip(heads, tails)
    )
    along_z, *lanes = lax.optimization_barrier((along_z, *lanes))

    picks = expert_ids[:, :, None] == jnp.arange(placement.shape[0], dtype=jnp.int32)
    slot = jnp.sum(jnp.where(picks, placement, 0), axis=2)
    here = slot[:, :, None] == slots
    named = jnp.any(here, axis=1)
    weight = jnp.sum(jnp.where(here, route_weight[:, :, None], 0.0), axis=1)
    table = jnp.where(named, weight, -1.0)

    plane = lax.all_gather(along_z, ("dp", "y"), axis=0)
    first_piece = opposite(lanes[0][: hid // 2])
    table = lax.all_gather(after(table, along_z), COLUMN, axis=0, tiled=True)

    counts = jnp.sum((table >= 0).astype(jnp.float32), axis=0)
    partner = (slots + half * jnp.tile(swap_flag, 2)) % ncol
    column_load = jnp.sum(
        jnp.where(partner[:, None] == slots[None, :], counts[None, :], 0.0), axis=1
    ) / jnp.float32(rows * topk)
    scale = jnp.sum(jnp.where(slots == me, jnp.maximum(table, 0.0), 0.0), axis=1)
    scale = scale.reshape(nz, ny, ncore, rows).transpose(2, 1, 0, 3)
    scale = scale.reshape(ncore, ny * nz * rows, 1)
    scale_own = lax.dynamic_index_in_dim(scale, core, 0, keepdims=False)
    scale_other = lax.dynamic_index_in_dim(scale, 1 - core, 0, keepdims=False)

    plane, scale_own, scale_other, first_piece, lane_rest, lane_down = lax.optimization_barrier(
        (plane, scale_own, scale_other, first_piece, lanes[0][hid // 2 :], lanes[1])
    )
    second_piece = opposite(lane_rest)
    plane = plane.reshape(parts, ny * nz, rows, feat)
    plane_other = swap_ends(plane, "core")
    hidden_own = project(plane, w_pair, 4)
    crossed_own = swap_ends(hidden_own, "dp")
    plane_other, hidden_own = lax.optimization_barrier((plane_other, hidden_own))
    hidden_other = project(plane_other, w_pair, 4)
    crossed_other = swap_ends(hidden_other, "dp")

    first = (lax.axis_index("dp") * hid).astype(jnp.int32).reshape(1)
    crossed_own, hidden_other = lax.optimization_barrier((crossed_own, hidden_other))
    kept = down(first, hidden_own, crossed_own, w_down, scale_own, 2 * rows)
    crossed_other, kept = lax.optimization_barrier((crossed_other, kept))
    sent = down(first, hidden_other, crossed_other, w_down, scale_other, 2 * rows)
    sent, second_piece, lane_down = lax.optimization_barrier((sent, second_piece, lane_down))
    received = swap_ends(sent, "core")
    third_piece = opposite(lane_down)

    cut = feat // 2
    kept, received = (v.reshape(ny, nz, rows, feat) for v in (kept, received))
    leave = [lax.dynamic_index_in_dim(v[..., :cut], 1 - y, 0, keepdims=False) for v in (kept, received)]
    stay = [lax.dynamic_index_in_dim(v[..., :cut], y, 0, keepdims=False) for v in (kept, received)]
    from_y = swap_ends(add(*leave), "y")
    line = add(kept[..., cut:], received[..., cut:]).transpose(1, 0, 2, 3)
    line = lax.psum_scatter(line, "z", scatter_dimension=0, tiled=True)[0]
    total = (stay[0].astype(jnp.float32) + stay[1].astype(jnp.float32)) + from_y.astype(jnp.float32)
    *late, total = lax.optimization_barrier((*tails, total.astype(jnp.bfloat16)))
    left = lax.psum_scatter(total, "z", scatter_dimension=0, tiled=True)[0]
    over_y = swap_ends(lax.dynamic_index_in_dim(line, 1 - y, 0, keepdims=False), "y")
    right = add(lax.dynamic_index_in_dim(line, y, 0, keepdims=False), over_y)
    moe_out = jnp.concatenate([left, right], axis=1)

    rest = lax.cond(both, lambda a, b: (opposite(a), opposite(b)), lambda a, b: (a, b), *late)
    third_piece, *rest = lax.optimization_barrier((third_piece, *rest))
    arrived = [jnp.concatenate([first_piece, second_piece]), third_piece]
    handed = [
        jnp.concatenate([swap_ends(first_piece, "core"), swap_ends(second_piece, "core")]),
        swap_ends(third_piece, "core"),
    ]
    heads = [jnp.where(own, new, old) for new, old in zip(arrived, heads)]
    tails = [jnp.where(alone, new, old) for new, old in zip(handed, rest)]
    slot_gate_up = jnp.stack([heads[0], tails[0]])[None]
    slot_down = jnp.concatenate([heads[1], tails[1]])[None]
    return (moe_out, column_load, slot_gate_up, slot_down)


def from_behind(value, axis, steps):
    count = lax.axis_size(axis)
    pairs = [(source, (source + steps) % count) for source in range(count)]
    return lax.ppermute(value, axis, pairs)


def swapped_blocks(gate_up, down_weight, swap_flag, pair_index, half):
    incoming_pair = from_behind(gate_up, "expert", half)
    incoming_down = from_behind(down_weight, "expert", half)
    own_column = lax.axis_index("expert")
    own_flag = jnp.sum(jnp.where(pair_index == own_column % half, swap_flag, 0))
    pair_after = jnp.where(own_flag == 1, incoming_pair, gate_up)
    down_after = jnp.where(own_flag == 1, incoming_down, down_weight)
    return (pair_after, down_after)


def dispatched_body(tokens, expert_ids, route_weight, placement, swap_flag, gate_up, down_weight):
    ncol = lax.axis_size("expert")
    half = ncol // 2
    rows_here, feat_here = tokens.shape
    topk = expert_ids.shape[1]
    hid_here = gate_up.shape[2]
    width = gate_up.shape[3]
    capacity = max(4, rows_here * topk * 17 // (16 * ncol) + 2)
    experts_all = placement.shape[0]
    pair_index = jnp.arange(half, dtype=jnp.int32)
    hits = placement[:, None] % half == pair_index[None, :]
    flag_of = jnp.sum(jnp.where(hits, swap_flag[None, :], 0), axis=1)
    moved = (placement + half * flag_of) % ncol
    picks = expert_ids.reshape(-1)[:, None] == jnp.arange(experts_all, dtype=jnp.int32)[None, :]
    moved_dest = jnp.sum(jnp.where(picks, moved[None, :], 0), axis=1)
    columns = jnp.arange(ncol, dtype=jnp.int32)
    local_counts = jnp.sum((moved_dest[:, None] == columns[None, :]).astype(jnp.float32), axis=0)
    totals = lax.psum(local_counts, "expert")
    column_load = totals / jnp.float32(rows_here * topk)
    slot_gate_up, slot_down = swapped_blocks(gate_up, down_weight, swap_flag, pair_index, half)
    col_hits = moved_dest[:, None] == columns[None, :]
    order = jnp.cumsum(col_hits.astype(jnp.int32), axis=0) - 1
    position = jnp.sum(jnp.where(col_hits, order, 0), axis=1)
    slot_index = moved_dest * capacity + position
    w_pair = slot_gate_up.reshape(2 * hid_here, width)
    w_down = slot_down.reshape(slot_down.shape[1], feat_here)
    contract = (((1,), (1,)), ((), ()))
    whole = lax.all_gather(tokens, "dp", axis=1, tiled=True)
    repeated = jnp.repeat(whole, topk, axis=0)
    buffer = jnp.zeros((ncol * capacity, width), jnp.bfloat16).at[slot_index].set(repeated)
    buffer = buffer.reshape(ncol, capacity, width)
    received = lax.all_to_all(buffer, "expert", split_axis=0, concat_axis=0, tiled=True)
    blocks, count, wide = received.shape
    rows = received.reshape(blocks * count, wide)
    projected = lax.dot_general(rows, w_pair, contract, preferred_element_type=jnp.float32)
    hidden = (jax.nn.silu(projected[:, :hid_here]) * projected[:, hid_here:]).astype(jnp.bfloat16)
    mixed = jnp.dot(
        lax.all_gather(hidden, "dp", axis=1, tiled=True), w_down, preferred_element_type=jnp.float32
    )
    result = mixed.astype(jnp.bfloat16).reshape(blocks, count, feat_here)
    returned = lax.all_to_all(result, "expert", split_axis=0, concat_axis=0, tiled=True)
    flat_back = returned.reshape(ncol * capacity, feat_here)
    gathered = flat_back[slot_index].astype(jnp.float32).reshape(rows_here, topk, feat_here)
    moe_out = jnp.sum(gathered * route_weight[:, :, None], axis=1).astype(jnp.bfloat16)
    return (moe_out, column_load, slot_gate_up, slot_down)


def solution(mesh):
    expert = mesh.shape["expert"]
    if expert > 16:
        run, names, column = dispatched_body, mesh, "expert"
    else:
        shape = (mesh.shape["dp"], expert // 4, 2, 2)
        run, names, column = body, Mesh(mesh.devices.reshape(shape), ("dp", *COLUMN)), COLUMN
    return jax.shard_map(
        run,
        mesh=names,
        in_specs=(
            P(column, "dp"),
            P(column, None),
            P(column, None),
            P(),
            P(),
            P(column, None, "dp", None),
            P(column, None, "dp"),
        ),
        out_specs=(P(column, "dp"), P(), P(column, None, "dp", None), P(column, None, "dp")),
        check_vma=False,
    )
```

```python
import jax
import jax.numpy as jnp
from jax import lax
from jax.experimental import pallas as pl
from jax.experimental.pallas import tpu as pltpu
from jax.sharding import Mesh
from jax.sharding import PartitionSpec as P

COLUMN = ("z", "y", "core")


def project_kernel(part_ref, x_ref, own_w_ref, other_w_ref, out_ref):
    blocks, rows, feat = x_ref.shape[1:]
    hid = out_ref.shape[1]
    contract = (((1,), (1,)), ((), ()))
    total = lax.dot_general(
        x_ref[0].reshape(blocks * rows, feat),
        own_w_ref[...],
        contract,
        preferred_element_type=jnp.float32,
    )
    total += lax.dot_general(
        x_ref[1].reshape(blocks * rows, feat),
        other_w_ref[...],
        contract,
        preferred_element_type=jnp.float32,
    )
    gate, up = total[:, :hid], total[:, hid:]
    out_ref[...] = (gate / (1.0 + jnp.exp(-gate)) * up).astype(jnp.bfloat16)


def project(part, x_all, w_pair, step):
    blocks, rows, feat = x_all.shape[1:]
    hid2, width = w_pair.shape
    hid = hid2 // 2
    return pl.pallas_call(
        project_kernel,
        grid_spec=pltpu.PrefetchScalarGridSpec(
            num_scalar_prefetch=1,
            grid=(blocks // step,),
            in_specs=[
                pl.BlockSpec((2, step, rows, feat), lambda i, part: (0, i, 0, 0)),
                pl.BlockSpec((hid2, feat), lambda i, part: (0, part[0])),
                pl.BlockSpec((hid2, feat), lambda i, part: (0, 1 - part[0])),
            ],
            out_specs=pl.BlockSpec((step * rows, hid), lambda i, part: (i, 0)),
        ),
        out_shape=jax.ShapeDtypeStruct((blocks * rows, hid), jnp.bfloat16),
        compiler_params=pltpu.CompilerParams(vmem_limit_bytes=48 << 20),
        cost_estimate=pl.CostEstimate(
            flops=2 * blocks * rows * hid2 * width,
            bytes_accessed=2 * (blocks * rows * width + hid2 * width),
            transcendentals=blocks * rows * hid,
        ),
        name="project",
    )(part, x_all, w_pair, w_pair)


def down_kernel(part_ref, own_ref, other_ref, own_w_ref, other_w_ref, scale_ref, out_ref):
    result = jnp.dot(own_ref[...], own_w_ref[...], preferred_element_type=jnp.float32)
    result += jnp.dot(other_ref[...], other_w_ref[...], preferred_element_type=jnp.float32)
    result = result.astype(jnp.bfloat16).astype(jnp.float32)
    out_ref[...] = (result * scale_ref[...]).astype(out_ref.dtype)


def down(part, own, other, w_down, scale, block):
    rows, hid = own.shape
    depth, feat = w_down.shape
    return pl.pallas_call(
        down_kernel,
        grid_spec=pltpu.PrefetchScalarGridSpec(
            num_scalar_prefetch=1,
            grid=(rows // block,),
            in_specs=[
                pl.BlockSpec((block, hid), lambda i, part: (i, 0)),
                pl.BlockSpec((block, hid), lambda i, part: (i, 0)),
                pl.BlockSpec((hid, feat), lambda i, part: (part[0], 0)),
                pl.BlockSpec((hid, feat), lambda i, part: (1 - part[0], 0)),
                pl.BlockSpec((block, 1), lambda i, part: (i, 0)),
            ],
            out_specs=pl.BlockSpec((block, feat), lambda i, part: (i, 0)),
        ),
        out_shape=jax.ShapeDtypeStruct((rows, feat), jnp.bfloat16),
        compiler_params=pltpu.CompilerParams(vmem_limit_bytes=48 << 20),
        cost_estimate=pl.CostEstimate(
            flops=2 * rows * depth * feat,
            bytes_accessed=2 * (rows * depth + depth * feat + rows * feat),
            transcendentals=0,
        ),
        name="down",
    )(part, own, other, w_down, w_down, scale)


def hop(value, axis, mask=1):
    return lax.ppermute(value, axis, [(p, p ^ mask) for p in range(lax.axis_size(axis))])


def tie(*values):
    return lax.optimization_barrier(values)


def wide(value):
    return value.astype(jnp.float32)


def body(tokens, expert_ids, route_weight, placement, swap_flag, gate_up, down_weight):
    nz, ny, ncore = (lax.axis_size(name) for name in COLUMN)
    ncol = nz * ny * ncore
    half = ncol // 2
    rows, feat = tokens.shape
    topk = expert_ids.shape[1]
    hid = gate_up.shape[2]
    width = gate_up.shape[3]
    me = lax.axis_index(COLUMN)
    core = lax.axis_index("core")
    part = lax.axis_index("dp").astype(jnp.int32).reshape(1)
    w_pair = gate_up.reshape(2 * hid, width)
    w_down = down_weight.reshape(down_weight.shape[1:])
    depth = w_down.shape[0] // 2

    slots = jnp.arange(ncol, dtype=jnp.int32)
    own = jnp.sum(jnp.where(slots[:half] == me % half, swap_flag, 0)) == 1
    sibling = jnp.sum(jnp.where(slots[:half] == (me + 1 - 2 * core) % half, swap_flag, 0)) == 1
    alone = own & ~sibling
    both = own & sibling

    heads, tails = (w_pair[:hid], w_down[:depth]), (w_pair[hid:], w_down[depth:])
    lane_pair, lane_down = (
        jnp.where(own, head, hop(tail, "core")) for head, tail in zip(heads, tails)
    )
    marks = (0, 7 * hid // 24, hid // 2, 19 * hid // 24, hid)
    lanes = [lane_pair[low:high] for low, high in zip(marks[:-1], marks[1:])]

    far, near, across_0, beside_0 = tie(
        hop(tokens, "z", 2), hop(tokens, "z", 1), hop(tokens, "dp"), hop(tokens, "y")
    )
    apart, across_2, beside_2 = tie(hop(far, "z", 1), hop(far, "dp"), hop(far, "y"))
    across_3, beside_3 = hop(apart, "dp"), hop(apart, "y")
    across_1, beside_1 = hop(near, "dp"), hop(near, "y")
    planes = [
        ((tokens, beside_0), (across_0, hop(across_0, "y"))),
        ((near, beside_1), (across_1, hop(beside_1, "dp"))),
        ((far, beside_2), (across_2, hop(beside_2, "dp"))),
        ((apart, beside_3), (across_3, hop(across_3, "y"))),
    ]

    def group(first, second):
        return jnp.stack(
            [
                jnp.stack([planes[k][dp][y] for y in range(2) for k in (first, second)])
                for dp in range(2)
            ]
        )

    picks = expert_ids[:, :, None] == jnp.arange(placement.shape[0], dtype=jnp.int32)
    slot = jnp.sum(jnp.where(picks, placement, 0), axis=2)
    here = slot[:, :, None] == slots
    named = jnp.any(here, axis=1)
    weight = jnp.sum(jnp.where(here, route_weight[:, :, None], 0.0), axis=1)
    table = jnp.where(named, weight, -1.0).T[None]
    for axis, mask in (("core", 1), ("y", 1), ("z", 1), ("z", 2)):
        table = jnp.concatenate([table, hop(table, axis, mask)])
    counts = jnp.sum((table >= 0).astype(jnp.float32), axis=(0, 2))
    partner = (slots + half * jnp.tile(swap_flag, 2)) % ncol
    column_load = jnp.sum(
        jnp.where(partner[:, None] == slots[None, :], counts[None, :], 0.0), axis=1
    ) / jnp.float32(rows * topk)
    mine = (slots == me)[None, :, None]
    scale = jnp.sum(jnp.where(mine, jnp.maximum(table, 0.0), 0.0), axis=1)
    scale = scale.reshape(2, 2, ny, ncore, rows).transpose(3, 0, 2, 1, 4)
    scale = scale.reshape(ncore, 2, ny * 2 * rows, 1)

    x_late, first_lane, scale, lanes[1] = tie(group(2, 3), hop(lanes[0], "z", 2), scale, lanes[1])
    x_late_other = hop(x_late, "core")
    late_own = project(part, x_late, w_pair, 4)
    late_own_cross = hop(late_own, "dp")
    late_other = project(part, x_late_other, w_pair, 4)
    x_early, second_lane, late_other, lanes[2] = tie(
        group(0, 1), hop(lanes[1], "z", 2), late_other, lanes[2]
    )
    late_other_cross = hop(late_other, "dp")
    x_early_other = hop(x_early, "core")
    early_own = project(part, x_early, w_pair, 4)
    early_own_cross = hop(early_own, "dp")

    def serve(hidden_own, cross_own, hidden_other, cross_other, which):
        sent = down(part, hidden_other, cross_other, w_down, scale[1, which], 2 * rows)
        received = hop(sent, "core")
        kept = down(part, hidden_own, cross_own, w_down, scale[0, which], 2 * rows)
        return [v.reshape(2, 2, rows, feat) for v in (kept, received)]

    def across_y(kept, received):
        leave = (wide(kept[1]) + wide(received[1])).astype(jnp.bfloat16)
        return wide(kept[0]) + wide(received[0]), hop(leave, "y")

    late_other, early_own = tie(late_other, early_own)
    late = serve(late_own, late_own_cross, late_other, late_other_cross, 1)
    early_other = project(part, x_early_other, w_pair, 4)
    early_other_cross = hop(early_other, "dp")
    line, line_y = across_y(*late)
    line = (line + wide(line_y)).astype(jnp.bfloat16)
    early = serve(early_own, early_own_cross, early_other, early_other_cross, 0)
    line, *early, third_lane, lanes[3] = tie(line, *early, hop(lanes[2], "z", 2), lanes[3])
    line = (wide(line[0]) + wide(hop(line[1], "z", 1))).astype(jnp.bfloat16)
    over = hop(line, "z", 2)
    total, total_y = across_y(*early)
    total = total + wide(total_y)
    total, fourth_lane, lane_down = tie(total, hop(lanes[3], "z", 2), lane_down)
    down_lane = hop(lane_down, "z", 2)
    closing = hop(total[1].astype(jnp.bfloat16), "z", 1)
    moe_out = (total[0] + wide(closing) + wide(over)).astype(jnp.bfloat16)

    *last, moe_out = tie(*tails, moe_out)
    rest = lax.cond(
        both, lambda a, b: (hop(a, "z", 2), hop(b, "z", 2)), lambda a, b: (a, b), *last
    )
    arrived = [first_lane, second_lane, third_lane, fourth_lane, down_lane]
    handed = [hop(value, "core") for value in arrived]
    new_heads = (jnp.concatenate(arrived[:4]), arrived[4])
    new_tails = (jnp.concatenate(handed[:4]), handed[4])
    heads = [jnp.where(own, new, old) for new, old in zip(new_heads, heads)]
    tails = [jnp.where(alone, new, old) for new, old in zip(new_tails, rest)]
    slot_gate_up = jnp.stack([heads[0], tails[0]])[None]
    slot_down = jnp.concatenate([heads[1], tails[1]])[None]
    return (moe_out, column_load, slot_gate_up, slot_down)


def from_behind(value, axis, steps):
    count = lax.axis_size(axis)
    pairs = [(source, (source + steps) % count) for source in range(count)]
    return lax.ppermute(value, axis, pairs)


def swapped_blocks(gate_up, down_weight, swap_flag, pair_index, half):
    incoming_pair = from_behind(gate_up, "expert", half)
    incoming_down = from_behind(down_weight, "expert", half)
    own_column = lax.axis_index("expert")
    own_flag = jnp.sum(jnp.where(pair_index == own_column % half, swap_flag, 0))
    pair_after = jnp.where(own_flag == 1, incoming_pair, gate_up)
    down_after = jnp.where(own_flag == 1, incoming_down, down_weight)
    return (pair_after, down_after)


def dispatched_body(tokens, expert_ids, route_weight, placement, swap_flag, gate_up, down_weight):
    ncol = lax.axis_size("expert")
    half = ncol // 2
    rows_here, feat_here = tokens.shape
    topk = expert_ids.shape[1]
    hid_here = gate_up.shape[2]
    width = gate_up.shape[3]
    capacity = max(4, rows_here * topk * 17 // (16 * ncol) + 2)
    experts_all = placement.shape[0]
    pair_index = jnp.arange(half, dtype=jnp.int32)
    hits = placement[:, None] % half == pair_index[None, :]
    flag_of = jnp.sum(jnp.where(hits, swap_flag[None, :], 0), axis=1)
    moved = (placement + half * flag_of) % ncol
    picks = expert_ids.reshape(-1)[:, None] == jnp.arange(experts_all, dtype=jnp.int32)[None, :]
    moved_dest = jnp.sum(jnp.where(picks, moved[None, :], 0), axis=1)
    columns = jnp.arange(ncol, dtype=jnp.int32)
    local_counts = jnp.sum((moved_dest[:, None] == columns[None, :]).astype(jnp.float32), axis=0)
    totals = lax.psum(local_counts, "expert")
    column_load = totals / jnp.float32(rows_here * topk)
    slot_gate_up, slot_down = swapped_blocks(gate_up, down_weight, swap_flag, pair_index, half)
    col_hits = moved_dest[:, None] == columns[None, :]
    order = jnp.cumsum(col_hits.astype(jnp.int32), axis=0) - 1
    position = jnp.sum(jnp.where(col_hits, order, 0), axis=1)
    slot_index = moved_dest * capacity + position
    w_pair = slot_gate_up.reshape(2 * hid_here, width)
    w_down = slot_down.reshape(slot_down.shape[1], feat_here)
    contract = (((1,), (1,)), ((), ()))
    whole = lax.all_gather(tokens, "dp", axis=1, tiled=True)
    repeated = jnp.repeat(whole, topk, axis=0)
    buffer = jnp.zeros((ncol * capacity, width), jnp.bfloat16).at[slot_index].set(repeated)
    buffer = buffer.reshape(ncol, capacity, width)
    received = lax.all_to_all(buffer, "expert", split_axis=0, concat_axis=0, tiled=True)
    blocks, count, wide = received.shape
    rows = received.reshape(blocks * count, wide)
    projected = lax.dot_general(rows, w_pair, contract, preferred_element_type=jnp.float32)
    hidden = (jax.nn.silu(projected[:, :hid_here]) * projected[:, hid_here:]).astype(jnp.bfloat16)
    mixed = jnp.dot(
        lax.all_gather(hidden, "dp", axis=1, tiled=True), w_down, preferred_element_type=jnp.float32
    )
    result = mixed.astype(jnp.bfloat16).reshape(blocks, count, feat_here)
    returned = lax.all_to_all(result, "expert", split_axis=0, concat_axis=0, tiled=True)
    flat_back = returned.reshape(ncol * capacity, feat_here)
    gathered = flat_back[slot_index].astype(jnp.float32).reshape(rows_here, topk, feat_here)
    moe_out = jnp.sum(gathered * route_weight[:, :, None], axis=1).astype(jnp.bfloat16)
    return (moe_out, column_load, slot_gate_up, slot_down)


def solution(mesh):
    expert = mesh.shape["expert"]
    if expert != 16 or mesh.shape["dp"] != 2:
        run, names, column = dispatched_body, mesh, "expert"
    else:
        shape = (mesh.shape["dp"], expert // 4, 2, 2)
        run, names, column = body, Mesh(mesh.devices.reshape(shape), ("dp", *COLUMN)), COLUMN
    return jax.shard_map(
        run,
        mesh=names,
        in_specs=(
            P(column, "dp"),
            P(column, None),
            P(column, None),
            P(),
            P(),
            P(column, None, "dp", None),
            P(column, None, "dp"),
        ),
        out_specs=(P(column, "dp"), P(), P(column, None, "dp", None), P(column, None, "dp")),
        check_vma=False,
    )
```

```python
import jax
import jax.numpy as jnp
from jax import lax
from jax.experimental import pallas as pl
from jax.experimental.pallas import tpu as pltpu
from jax.sharding import Mesh
from jax.sharding import PartitionSpec as P

COLUMN = ("z", "y", "core")


def project_kernel(part_ref, x_ref, own_w_ref, other_w_ref, out_ref):
    blocks, rows, feat = x_ref.shape[1:]
    hid = out_ref.shape[1]
    contract = (((1,), (1,)), ((), ()))
    total = lax.dot_general(
        x_ref[0].reshape(blocks * rows, feat),
        own_w_ref[...],
        contract,
        preferred_element_type=jnp.float32,
    )
    total += lax.dot_general(
        x_ref[1].reshape(blocks * rows, feat),
        other_w_ref[...],
        contract,
        preferred_element_type=jnp.float32,
    )
    gate, up = total[:, :hid], total[:, hid:]
    out_ref[...] = (gate / (1.0 + jnp.exp(-gate)) * up).astype(jnp.bfloat16)


def project(part, x_all, w_pair, step):
    blocks, rows, feat = x_all.shape[1:]
    hid2, width = w_pair.shape
    hid = hid2 // 2
    return pl.pallas_call(
        project_kernel,
        grid_spec=pltpu.PrefetchScalarGridSpec(
            num_scalar_prefetch=1,
            grid=(blocks // step,),
            in_specs=[
                pl.BlockSpec((2, step, rows, feat), lambda i, part: (0, i, 0, 0)),
                pl.BlockSpec((hid2, feat), lambda i, part: (0, part[0])),
                pl.BlockSpec((hid2, feat), lambda i, part: (0, 1 - part[0])),
            ],
            out_specs=pl.BlockSpec((step * rows, hid), lambda i, part: (i, 0)),
        ),
        out_shape=jax.ShapeDtypeStruct((blocks * rows, hid), jnp.bfloat16),
        compiler_params=pltpu.CompilerParams(vmem_limit_bytes=48 << 20),
        cost_estimate=pl.CostEstimate(
            flops=2 * blocks * rows * hid2 * width,
            bytes_accessed=2 * (blocks * rows * width + hid2 * width),
            transcendentals=blocks * rows * hid,
        ),
        name="project",
    )(part, x_all, w_pair, w_pair)


def down_kernel(part_ref, own_ref, other_ref, own_w_ref, other_w_ref, scale_ref, out_ref):
    result = jnp.dot(own_ref[...], own_w_ref[...], preferred_element_type=jnp.float32)
    result += jnp.dot(other_ref[...], other_w_ref[...], preferred_element_type=jnp.float32)
    result = result.astype(jnp.bfloat16).astype(jnp.float32)
    out_ref[...] = (result * scale_ref[...]).astype(out_ref.dtype)


def down(part, own, other, w_down, scale, block):
    rows, hid = own.shape
    depth, feat = w_down.shape
    return pl.pallas_call(
        down_kernel,
        grid_spec=pltpu.PrefetchScalarGridSpec(
            num_scalar_prefetch=1,
            grid=(rows // block,),
            in_specs=[
                pl.BlockSpec((block, hid), lambda i, part: (i, 0)),
                pl.BlockSpec((block, hid), lambda i, part: (i, 0)),
                pl.BlockSpec((hid, feat), lambda i, part: (part[0], 0)),
                pl.BlockSpec((hid, feat), lambda i, part: (1 - part[0], 0)),
                pl.BlockSpec((block, 1), lambda i, part: (i, 0)),
            ],
            out_specs=pl.BlockSpec((block, feat), lambda i, part: (i, 0)),
        ),
        out_shape=jax.ShapeDtypeStruct((rows, feat), jnp.bfloat16),
        compiler_params=pltpu.CompilerParams(vmem_limit_bytes=48 << 20),
        cost_estimate=pl.CostEstimate(
            flops=2 * rows * depth * feat,
            bytes_accessed=2 * (rows * depth + depth * feat + rows * feat),
            transcendentals=0,
        ),
        name="down",
    )(part, own, other, w_down, w_down, scale)


def hop(value, axis, mask=1):
    return lax.ppermute(value, axis, [(p, p ^ mask) for p in range(lax.axis_size(axis))])


def tie(*values):
    return lax.optimization_barrier(values)


def wide(value):
    return value.astype(jnp.float32)


def serve(hidden_own, cross_own, hidden_other, cross_other, w_down, scale):
    part = lax.axis_index("dp").astype(jnp.int32).reshape(1)
    rows = hidden_own.shape[0] // 4
    feat = w_down.shape[1]
    sent = down(part, hidden_other, cross_other, w_down, scale[1], 2 * rows)
    received = hop(sent, "core")
    kept = down(part, hidden_own, cross_own, w_down, scale[0], 2 * rows)
    return [v.reshape(2, 2, rows, feat) for v in (kept, received)]


def across_y(kept, received):
    leave = (wide(kept[1]) + wide(received[1])).astype(jnp.bfloat16)
    return wide(kept[0]) + wide(received[0]), hop(leave, "y")


def gather_stage(tokens, far, near, across_0, beside_0, table, w_pair, w_down):
    nz, ny, ncore = (lax.axis_size(name) for name in COLUMN)
    ncol = nz * ny * ncore
    rows, feat = tokens.shape
    me = lax.axis_index(COLUMN)
    part = lax.axis_index("dp").astype(jnp.int32).reshape(1)

    apart, across_2, beside_2 = tie(hop(far, "z", 1), hop(far, "dp"), hop(far, "y"))
    across_3, beside_3 = hop(apart, "dp"), hop(apart, "y")
    across_1, beside_1 = hop(near, "dp"), hop(near, "y")
    planes = [
        ((tokens, beside_0), (across_0, hop(across_0, "y"))),
        ((near, beside_1), (across_1, hop(beside_1, "dp"))),
        ((far, beside_2), (across_2, hop(beside_2, "dp"))),
        ((apart, beside_3), (across_3, hop(across_3, "y"))),
    ]

    def group(first, second):
        return jnp.stack(
            [
                jnp.stack([planes[k][dp][y] for y in range(2) for k in (first, second)])
                for dp in range(2)
            ]
        )

    for axis, mask in (("core", 1), ("y", 1), ("z", 1), ("z", 2)):
        table = jnp.concatenate([table, hop(table, axis, mask)])
    counts = jnp.sum((table >= 0).astype(jnp.float32), axis=(0, 2))
    mine = (jnp.arange(ncol, dtype=jnp.int32) == me)[None, :, None]
    scale = jnp.sum(jnp.where(mine, jnp.maximum(table, 0.0), 0.0), axis=1)
    scale = scale.reshape(2, 2, ny, ncore, rows).transpose(3, 0, 2, 1, 4)
    scale = scale.reshape(ncore, 2, ny * 2 * rows, 1)

    x_late, scale = tie(group(2, 3), scale)
    x_late_other = hop(x_late, "core")
    late_own = project(part, x_late, w_pair, 4)
    late_own_cross = hop(late_own, "dp")
    late_other = project(part, x_late_other, w_pair, 4)
    x_early, late_other = tie(group(0, 1), late_other)
    late_other_cross = hop(late_other, "dp")
    x_early_other = hop(x_early, "core")
    early_own = project(part, x_early, w_pair, 4)
    early_own_cross = hop(early_own, "dp")

    late_other, early_own = tie(late_other, early_own)
    late = serve(late_own, late_own_cross, late_other, late_other_cross, w_down, scale[:, 1])
    early_other = project(part, x_early_other, w_pair, 4)
    early_other_cross = hop(early_other, "dp")
    early = (early_own, early_own_cross, early_other, early_other_cross)
    return late, early, scale[:, 0], counts


def reduce_stage(late, early, scale, w_down):
    line, line_y = across_y(*late)
    line = (line + wide(line_y)).astype(jnp.bfloat16)
    early = serve(*early, w_down, scale)
    line = (wide(line[0]) + wide(hop(line[1], "z", 1))).astype(jnp.bfloat16)
    over = hop(line, "z", 2)
    total, total_y = across_y(*early)
    total = total + wide(total_y)
    closing = hop(total[1].astype(jnp.bfloat16), "z", 1)
    return (total[0] + wide(closing) + wide(over)).astype(jnp.bfloat16)


def guarded(valid, stage, *operands):
    shapes = jax.eval_shape(stage, *operands)
    empty = lambda *_: jax.tree.map(lambda leaf: jnp.zeros(leaf.shape, leaf.dtype), shapes)
    return lax.cond(valid, stage, empty, *operands)


def body(tokens, expert_ids, route_weight, placement, swap_flag, gate_up, down_weight):
    ncol = lax.axis_size(COLUMN)
    half = ncol // 2
    rows = tokens.shape[0]
    topk = expert_ids.shape[1]
    hid = gate_up.shape[2]
    width = gate_up.shape[3]
    me = lax.axis_index(COLUMN)
    core = lax.axis_index("core")
    w_pair = gate_up.reshape(2 * hid, width)
    w_down = down_weight.reshape(down_weight.shape[1:])
    depth = w_down.shape[0] // 2

    slots = jnp.arange(ncol, dtype=jnp.int32)
    own = jnp.sum(jnp.where(slots[:half] == me % half, swap_flag, 0)) == 1
    sibling = jnp.sum(jnp.where(slots[:half] == (me + 1 - 2 * core) % half, swap_flag, 0)) == 1
    alone = own & ~sibling
    both = own & sibling

    picks = expert_ids[:, :, None] == jnp.arange(placement.shape[0], dtype=jnp.int32)
    slot = jnp.sum(jnp.where(picks, placement, 0), axis=2)
    here = slot[:, :, None] == slots
    named = jnp.any(here, axis=1)
    weight = jnp.sum(jnp.where(here, route_weight[:, :, None], 0.0), axis=1)
    table = jnp.where(named, weight, -1.0).T[None]

    heads, tails = (w_pair[:hid], w_down[:depth]), (w_pair[hid:], w_down[depth:])
    lane_pair, lane_down = (
        jnp.where(own, head, hop(tail, "core")) for head, tail in zip(heads, tails)
    )
    far, near, across_0, beside_0, table, lane_pair, lane_down = tie(
        hop(tokens, "z", 2),
        hop(tokens, "z", 1),
        hop(tokens, "dp"),
        hop(tokens, "y"),
        table,
        lane_pair,
        lane_down,
    )
    arrived_pair = hop(lane_pair, "z", 2)
    valid = placement[0] >= 0
    staged = guarded(
        valid, gather_stage, tokens, far, near, across_0, beside_0, table, w_pair, w_down
    )
    late, early, scale, counts, arrived_pair, lane_down = tie(*staged, arrived_pair, lane_down)
    arrived_down = hop(lane_down, "z", 2)
    handed_pair = hop(arrived_pair, "core")
    moe_out = guarded(valid, reduce_stage, late, early, scale, w_down)
    partner = (slots + half * jnp.tile(swap_flag, 2)) % ncol
    column_load = jnp.sum(
        jnp.where(partner[:, None] == slots[None, :], counts[None, :], 0.0), axis=1
    ) / jnp.float32(rows * topk)

    *last, moe_out, arrived_down, handed_pair = tie(*tails, moe_out, arrived_down, handed_pair)
    rest = lax.cond(
        both, lambda a, b: (hop(a, "z", 2), hop(b, "z", 2)), lambda a, b: (a, b), *last
    )
    arrived = (arrived_pair, arrived_down)
    handed = (handed_pair, hop(arrived_down, "core"))
    heads = [jnp.where(own, new, old) for new, old in zip(arrived, heads)]
    tails = [jnp.where(alone, new, old) for new, old in zip(handed, rest)]
    slot_gate_up = jnp.stack([heads[0], tails[0]])[None]
    slot_down = jnp.concatenate([heads[1], tails[1]])[None]
    return (moe_out, column_load, slot_gate_up, slot_down)


def from_behind(value, axis, steps):
    count = lax.axis_size(axis)
    pairs = [(source, (source + steps) % count) for source in range(count)]
    return lax.ppermute(value, axis, pairs)


def swapped_blocks(gate_up, down_weight, swap_flag, pair_index, half):
    incoming_pair = from_behind(gate_up, "expert", half)
    incoming_down = from_behind(down_weight, "expert", half)
    own_column = lax.axis_index("expert")
    own_flag = jnp.sum(jnp.where(pair_index == own_column % half, swap_flag, 0))
    pair_after = jnp.where(own_flag == 1, incoming_pair, gate_up)
    down_after = jnp.where(own_flag == 1, incoming_down, down_weight)
    return (pair_after, down_after)


def dispatched_body(tokens, expert_ids, route_weight, placement, swap_flag, gate_up, down_weight):
    ncol = lax.axis_size("expert")
    half = ncol // 2
    rows_here, feat_here = tokens.shape
    topk = expert_ids.shape[1]
    hid_here = gate_up.shape[2]
    width = gate_up.shape[3]
    capacity = max(4, rows_here * topk * 17 // (16 * ncol) + 2)
    experts_all = placement.shape[0]
    pair_index = jnp.arange(half, dtype=jnp.int32)
    hits = placement[:, None] % half == pair_index[None, :]
    flag_of = jnp.sum(jnp.where(hits, swap_flag[None, :], 0), axis=1)
    moved = (placement + half * flag_of) % ncol
    picks = expert_ids.reshape(-1)[:, None] == jnp.arange(experts_all, dtype=jnp.int32)[None, :]
    moved_dest = jnp.sum(jnp.where(picks, moved[None, :], 0), axis=1)
    columns = jnp.arange(ncol, dtype=jnp.int32)
    local_counts = jnp.sum((moved_dest[:, None] == columns[None, :]).astype(jnp.float32), axis=0)
    totals = lax.psum(local_counts, "expert")
    column_load = totals / jnp.float32(rows_here * topk)
    slot_gate_up, slot_down = swapped_blocks(gate_up, down_weight, swap_flag, pair_index, half)
    col_hits = moved_dest[:, None] == columns[None, :]
    order = jnp.cumsum(col_hits.astype(jnp.int32), axis=0) - 1
    position = jnp.sum(jnp.where(col_hits, order, 0), axis=1)
    slot_index = moved_dest * capacity + position
    w_pair = slot_gate_up.reshape(2 * hid_here, width)
    w_down = slot_down.reshape(slot_down.shape[1], feat_here)
    contract = (((1,), (1,)), ((), ()))
    whole = lax.all_gather(tokens, "dp", axis=1, tiled=True)
    repeated = jnp.repeat(whole, topk, axis=0)
    buffer = jnp.zeros((ncol * capacity, width), jnp.bfloat16).at[slot_index].set(repeated)
    buffer = buffer.reshape(ncol, capacity, width)
    received = lax.all_to_all(buffer, "expert", split_axis=0, concat_axis=0, tiled=True)
    blocks, count, wide = received.shape
    rows = received.reshape(blocks * count, wide)
    projected = lax.dot_general(rows, w_pair, contract, preferred_element_type=jnp.float32)
    hidden = (jax.nn.silu(projected[:, :hid_here]) * projected[:, hid_here:]).astype(jnp.bfloat16)
    mixed = jnp.dot(
        lax.all_gather(hidden, "dp", axis=1, tiled=True), w_down, preferred_element_type=jnp.float32
    )
    result = mixed.astype(jnp.bfloat16).reshape(blocks, count, feat_here)
    returned = lax.all_to_all(result, "expert", split_axis=0, concat_axis=0, tiled=True)
    flat_back = returned.reshape(ncol * capacity, feat_here)
    gathered = flat_back[slot_index].astype(jnp.float32).reshape(rows_here, topk, feat_here)
    moe_out = jnp.sum(gathered * route_weight[:, :, None], axis=1).astype(jnp.bfloat16)
    return (moe_out, column_load, slot_gate_up, slot_down)


def solution(mesh):
    expert = mesh.shape["expert"]
    if expert != 16 or mesh.shape["dp"] != 2:
        run, names, column = dispatched_body, mesh, "expert"
    else:
        shape = (mesh.shape["dp"], expert // 4, 2, 2)
        run, names, column = body, Mesh(mesh.devices.reshape(shape), ("dp", *COLUMN)), COLUMN
    return jax.shard_map(
        run,
        mesh=names,
        in_specs=(
            P(column, "dp"),
            P(column, None),
            P(column, None),
            P(),
            P(),
            P(column, None, "dp", None),
            P(column, None, "dp"),
        ),
        out_specs=(P(column, "dp"), P(), P(column, None, "dp", None), P(column, None, "dp")),
        check_vma=False,
    )
```

```python
import jax
import jax.numpy as jnp
from jax import lax
from jax.experimental import pallas as pl
from jax.experimental.pallas import tpu as pltpu
from jax.sharding import Mesh
from jax.sharding import PartitionSpec as P

COLUMN = ("z", "y", "core")


def project_kernel(part_ref, x_ref, own_w_ref, other_w_ref, out_ref):
    blocks, rows, feat = x_ref.shape[1:]
    hid = out_ref.shape[1]
    contract = (((1,), (1,)), ((), ()))
    total = lax.dot_general(
        x_ref[0].reshape(blocks * rows, feat),
        own_w_ref[...],
        contract,
        preferred_element_type=jnp.float32,
    )
    total += lax.dot_general(
        x_ref[1].reshape(blocks * rows, feat),
        other_w_ref[...],
        contract,
        preferred_element_type=jnp.float32,
    )
    gate, up = total[:, :hid], total[:, hid:]
    out_ref[...] = (gate / (1.0 + jnp.exp(-gate)) * up).astype(jnp.bfloat16)


def project(part, x_all, w_pair, step):
    blocks, rows, feat = x_all.shape[1:]
    hid2, width = w_pair.shape
    hid = hid2 // 2
    return pl.pallas_call(
        project_kernel,
        grid_spec=pltpu.PrefetchScalarGridSpec(
            num_scalar_prefetch=1,
            grid=(blocks // step,),
            in_specs=[
                pl.BlockSpec((2, step, rows, feat), lambda i, part: (0, i, 0, 0)),
                pl.BlockSpec((hid2, feat), lambda i, part: (0, part[0])),
                pl.BlockSpec((hid2, feat), lambda i, part: (0, 1 - part[0])),
            ],
            out_specs=pl.BlockSpec((step * rows, hid), lambda i, part: (i, 0)),
        ),
        out_shape=jax.ShapeDtypeStruct((blocks * rows, hid), jnp.bfloat16),
        compiler_params=pltpu.CompilerParams(vmem_limit_bytes=48 << 20),
        cost_estimate=pl.CostEstimate(
            flops=2 * blocks * rows * hid2 * width,
            bytes_accessed=2 * (blocks * rows * width + hid2 * width),
            transcendentals=blocks * rows * hid,
        ),
        name="project",
    )(part, x_all, w_pair, w_pair)


def down_kernel(part_ref, own_ref, other_ref, own_w_ref, other_w_ref, scale_ref, out_ref):
    result = jnp.dot(own_ref[...], own_w_ref[...], preferred_element_type=jnp.float32)
    result += jnp.dot(other_ref[...], other_w_ref[...], preferred_element_type=jnp.float32)
    result = result.astype(jnp.bfloat16).astype(jnp.float32)
    out_ref[...] = (result * scale_ref[...]).astype(out_ref.dtype)


def down(part, own, other, w_down, scale, block):
    rows, hid = own.shape
    depth, feat = w_down.shape
    return pl.pallas_call(
        down_kernel,
        grid_spec=pltpu.PrefetchScalarGridSpec(
            num_scalar_prefetch=1,
            grid=(rows // block,),
            in_specs=[
                pl.BlockSpec((block, hid), lambda i, part: (i, 0)),
                pl.BlockSpec((block, hid), lambda i, part: (i, 0)),
                pl.BlockSpec((hid, feat), lambda i, part: (part[0], 0)),
                pl.BlockSpec((hid, feat), lambda i, part: (1 - part[0], 0)),
                pl.BlockSpec((block, 1), lambda i, part: (i, 0)),
            ],
            out_specs=pl.BlockSpec((block, feat), lambda i, part: (i, 0)),
        ),
        out_shape=jax.ShapeDtypeStruct((rows, feat), jnp.bfloat16),
        compiler_params=pltpu.CompilerParams(vmem_limit_bytes=48 << 20),
        cost_estimate=pl.CostEstimate(
            flops=2 * rows * depth * feat,
            bytes_accessed=2 * (rows * depth + depth * feat + rows * feat),
            transcendentals=0,
        ),
        name="down",
    )(part, own, other, w_down, w_down, scale)


def hop(value, axis, mask=1):
    return lax.ppermute(value, axis, [(p, p ^ mask) for p in range(lax.axis_size(axis))])


def tie(*values):
    return lax.optimization_barrier(values)


def wide(value):
    return value.astype(jnp.float32)


def serve(hidden_own, cross_own, hidden_other, cross_other, w_down, scale):
    part = lax.axis_index("dp").astype(jnp.int32).reshape(1)
    rows = hidden_own.shape[0] // 4
    feat = w_down.shape[1]
    sent = down(part, hidden_other, cross_other, w_down, scale[1], 2 * rows)
    received = hop(sent, "core")
    kept = down(part, hidden_own, cross_own, w_down, scale[0], 2 * rows)
    return [v.reshape(2, 2, rows, feat) for v in (kept, received)]


def across_y(kept, received):
    leave = (wide(kept[1]) + wide(received[1])).astype(jnp.bfloat16)
    return wide(kept[0]) + wide(received[0]), hop(leave, "y")


def gather_stage(tokens, near, far, apart, across_0, beside_0, across_2, beside_2, table, w_pair):
    rows = tokens.shape[0]
    part = lax.axis_index("dp").astype(jnp.int32).reshape(1)
    mine = jnp.arange(table.shape[1], dtype=jnp.int32) == lax.axis_index(COLUMN)
    across_3, beside_3, corner_2 = tie(hop(apart, "dp"), hop(apart, "y"), hop(beside_2, "dp"))
    corner_3, across_1, beside_1 = tie(hop(across_3, "y"), hop(near, "dp"), hop(near, "y"))
    own = jnp.stack([far, apart, beside_2, beside_3])
    x_late = jnp.stack([own, jnp.stack([across_2, across_3, corner_2, corner_3])])
    x_late_other = hop(x_late, "core")
    for axis in ("y", "core"):
        table = jnp.concatenate([table, hop(table, axis)])
    counts = jnp.sum((table >= 0).astype(jnp.float32), axis=(0, 2))
    scale = jnp.sum(jnp.where(mine[None, :, None], jnp.maximum(table, 0.0), 0.0), axis=1)
    scale = scale.reshape(2, 2, 2, 2, rows).transpose(0, 3, 1, 2, 4)
    scale = scale.reshape(2, 2, 4 * rows, 1)
    corner_0, corner_1 = hop(across_0, "y"), hop(beside_1, "dp")
    late_own = project(part, x_late, w_pair, 4)
    late_other = project(part, x_late_other, w_pair, 4)
    corner_0, corner_1, late_own, late_other, scale = tie(
        corner_0, corner_1, late_own, late_other, scale
    )
    own = jnp.stack([tokens, near, beside_0, beside_1])
    x_early = jnp.stack([own, jnp.stack([across_0, across_1, corner_0, corner_1])])
    return x_early, late_own, hop(late_own, "dp"), late_other, scale, counts


def expert_stage(x_early, late_own, late_own_cross, late_other, scale, w_pair, w_down):
    part = lax.axis_index("dp").astype(jnp.int32).reshape(1)
    late_other_cross = hop(late_other, "dp")
    x_early_other = hop(x_early, "core")
    early_own = project(part, x_early, w_pair, 4)
    early_own_cross = hop(early_own, "dp")
    late_other, early_own = tie(late_other, early_own)
    late = serve(late_own, late_own_cross, late_other, late_other_cross, w_down, scale[:, 1])
    early_other = project(part, x_early_other, w_pair, 4)
    early_other_cross = hop(early_other, "dp")
    line, line_y = across_y(*late)
    line = (line + wide(line_y)).astype(jnp.bfloat16)
    early = serve(early_own, early_own_cross, early_other, early_other_cross, w_down, scale[:, 0])
    total, total_y = across_y(*early)
    return line, total + wide(total_y)


def guarded(valid, stage, *operands):
    shapes = jax.eval_shape(stage, *operands)
    empty = lambda *_: jax.tree.map(lambda leaf: jnp.zeros(leaf.shape, leaf.dtype), shapes)
    return lax.cond(valid, stage, empty, *operands)


def body(tokens, expert_ids, route_weight, placement, swap_flag, gate_up, down_weight):
    ncol = lax.axis_size(COLUMN)
    half = ncol // 2
    rows = tokens.shape[0]
    topk = expert_ids.shape[1]
    hid = gate_up.shape[2]
    width = gate_up.shape[3]
    me = lax.axis_index(COLUMN)
    core = lax.axis_index("core")
    w_pair = gate_up.reshape(2 * hid, width)
    w_down = down_weight.reshape(down_weight.shape[1:])
    depth = w_down.shape[0] // 2

    slots = jnp.arange(ncol, dtype=jnp.int32)
    own = jnp.sum(jnp.where(slots[:half] == me % half, swap_flag, 0)) == 1
    sibling = jnp.sum(jnp.where(slots[:half] == (me + 1 - 2 * core) % half, swap_flag, 0)) == 1
    alone = own & ~sibling
    both = own & sibling

    picks = expert_ids[:, :, None] == jnp.arange(placement.shape[0], dtype=jnp.int32)
    slot = jnp.sum(jnp.where(picks, placement, 0), axis=2)
    here = slot[:, :, None] == slots
    named = jnp.any(here, axis=1)
    weight = jnp.sum(jnp.where(here, route_weight[:, :, None], 0.0), axis=1)
    table = jnp.where(named, weight, -1.0).T[None]

    heads, tails = (w_pair[:hid], w_down[:depth]), (w_pair[hid:], w_down[depth:])
    lane_pair, lane_down = (
        jnp.where(own, head, hop(tail, "core")) for head, tail in zip(heads, tails)
    )
    far, near, across_0, beside_0 = tie(
        hop(tokens, "z", 2), hop(tokens, "z", 1), hop(tokens, "dp"), hop(tokens, "y")
    )
    for axis, mask in (("z", 2), ("z", 1)):
        table = jnp.concatenate([table, hop(table, axis, mask)])
    apart, across_2, beside_2, table, lane_pair, lane_down = tie(
        hop(far, "z", 1), hop(far, "dp"), hop(far, "y"), table, lane_pair, lane_down
    )
    arrived_down = hop(lane_down, "z", 2)
    valid = placement[0] >= 0
    planes = (tokens, near, far, apart, across_0, beside_0, across_2, beside_2)
    *staged, counts = guarded(valid, gather_stage, *planes, table, w_pair)
    *staged, arrived_down, lane_pair = tie(*staged, arrived_down, lane_pair)
    arrived_pair = hop(lane_pair, "z", 2)
    handed_down = hop(arrived_down, "core")
    line, total = guarded(valid, expert_stage, *staged, w_pair, w_down)
    line, total, arrived_pair = tie(line, total, arrived_pair)
    line = (wide(line[0]) + wide(hop(line[1], "z", 1))).astype(jnp.bfloat16)
    closing = hop(total[1].astype(jnp.bfloat16), "z", 1)
    over, closing, *last = tie(hop(line, "z", 2), closing, *tails)
    handed_pair = hop(arrived_pair, "core")
    moe_out = (total[0] + wide(closing) + wide(over)).astype(jnp.bfloat16)
    partner = (slots + half * jnp.tile(swap_flag, 2)) % ncol
    column_load = jnp.sum(
        jnp.where(partner[:, None] == slots[None, :], counts[None, :], 0.0), axis=1
    ) / jnp.float32(rows * topk)

    rest = lax.cond(
        both, lambda a, b: (hop(a, "z", 2), hop(b, "z", 2)), lambda a, b: (a, b), *last
    )
    arrived = (arrived_pair, arrived_down)
    handed = (handed_pair, handed_down)
    heads = [jnp.where(own, new, old) for new, old in zip(arrived, heads)]
    tails = [jnp.where(alone, new, old) for new, old in zip(handed, rest)]
    slot_gate_up = jnp.stack([heads[0], tails[0]])[None]
    slot_down = jnp.concatenate([heads[1], tails[1]])[None]
    return (moe_out, column_load, slot_gate_up, slot_down)


def from_behind(value, axis, steps):
    count = lax.axis_size(axis)
    pairs = [(source, (source + steps) % count) for source in range(count)]
    return lax.ppermute(value, axis, pairs)


def swapped_blocks(gate_up, down_weight, swap_flag, pair_index, half):
    incoming_pair = from_behind(gate_up, "expert", half)
    incoming_down = from_behind(down_weight, "expert", half)
    own_column = lax.axis_index("expert")
    own_flag = jnp.sum(jnp.where(pair_index == own_column % half, swap_flag, 0))
    pair_after = jnp.where(own_flag == 1, incoming_pair, gate_up)
    down_after = jnp.where(own_flag == 1, incoming_down, down_weight)
    return (pair_after, down_after)


def dispatched_body(tokens, expert_ids, route_weight, placement, swap_flag, gate_up, down_weight):
    ncol = lax.axis_size("expert")
    half = ncol // 2
    rows_here, feat_here = tokens.shape
    topk = expert_ids.shape[1]
    hid_here = gate_up.shape[2]
    width = gate_up.shape[3]
    capacity = max(4, rows_here * topk * 17 // (16 * ncol) + 2)
    experts_all = placement.shape[0]
    pair_index = jnp.arange(half, dtype=jnp.int32)
    hits = placement[:, None] % half == pair_index[None, :]
    flag_of = jnp.sum(jnp.where(hits, swap_flag[None, :], 0), axis=1)
    moved = (placement + half * flag_of) % ncol
    picks = expert_ids.reshape(-1)[:, None] == jnp.arange(experts_all, dtype=jnp.int32)[None, :]
    moved_dest = jnp.sum(jnp.where(picks, moved[None, :], 0), axis=1)
    columns = jnp.arange(ncol, dtype=jnp.int32)
    local_counts = jnp.sum((moved_dest[:, None] == columns[None, :]).astype(jnp.float32), axis=0)
    totals = lax.psum(local_counts, "expert")
    column_load = totals / jnp.float32(rows_here * topk)
    slot_gate_up, slot_down = swapped_blocks(gate_up, down_weight, swap_flag, pair_index, half)
    col_hits = moved_dest[:, None] == columns[None, :]
    order = jnp.cumsum(col_hits.astype(jnp.int32), axis=0) - 1
    position = jnp.sum(jnp.where(col_hits, order, 0), axis=1)
    slot_index = moved_dest * capacity + position
    w_pair = slot_gate_up.reshape(2 * hid_here, width)
    w_down = slot_down.reshape(slot_down.shape[1], feat_here)
    contract = (((1,), (1,)), ((), ()))
    whole = lax.all_gather(tokens, "dp", axis=1, tiled=True)
    repeated = jnp.repeat(whole, topk, axis=0)
    buffer = jnp.zeros((ncol * capacity, width), jnp.bfloat16).at[slot_index].set(repeated)
    buffer = buffer.reshape(ncol, capacity, width)
    received = lax.all_to_all(buffer, "expert", split_axis=0, concat_axis=0, tiled=True)
    blocks, count, wide = received.shape
    rows = received.reshape(blocks * count, wide)
    projected = lax.dot_general(rows, w_pair, contract, preferred_element_type=jnp.float32)
    hidden = (jax.nn.silu(projected[:, :hid_here]) * projected[:, hid_here:]).astype(jnp.bfloat16)
    mixed = jnp.dot(
        lax.all_gather(hidden, "dp", axis=1, tiled=True), w_down, preferred_element_type=jnp.float32
    )
    result = mixed.astype(jnp.bfloat16).reshape(blocks, count, feat_here)
    returned = lax.all_to_all(result, "expert", split_axis=0, concat_axis=0, tiled=True)
    flat_back = returned.reshape(ncol * capacity, feat_here)
    gathered = flat_back[slot_index].astype(jnp.float32).reshape(rows_here, topk, feat_here)
    moe_out = jnp.sum(gathered * route_weight[:, :, None], axis=1).astype(jnp.bfloat16)
    return (moe_out, column_load, slot_gate_up, slot_down)


def solution(mesh):
    expert = mesh.shape["expert"]
    if expert != 16 or mesh.shape["dp"] != 2:
        run, names, column = dispatched_body, mesh, "expert"
    else:
        shape = (mesh.shape["dp"], expert // 4, 2, 2)
        run, names, column = body, Mesh(mesh.devices.reshape(shape), ("dp", *COLUMN)), COLUMN
    return jax.shard_map(
        run,
        mesh=names,
        in_specs=(
            P(column, "dp"),
            P(column, None),
            P(column, None),
            P(),
            P(),
            P(column, None, "dp", None),
            P(column, None, "dp"),
        ),
        out_specs=(P(column, "dp"), P(), P(column, None, "dp", None), P(column, None, "dp")),
        check_vma=False,
    )
```

```python
import jax
import jax.numpy as jnp
from jax import lax
from jax.experimental import pallas as pl
from jax.experimental.pallas import tpu as pltpu
from jax.sharding import Mesh
from jax.sharding import PartitionSpec as P

COLUMN = ("z", "y", "core")


def project_kernel(part_ref, x_ref, own_w_ref, other_w_ref, out_ref):
    blocks, rows, feat = x_ref.shape[1:]
    hid = out_ref.shape[1]
    contract = (((1,), (1,)), ((), ()))
    total = lax.dot_general(
        x_ref[0].reshape(blocks * rows, feat),
        own_w_ref[...],
        contract,
        preferred_element_type=jnp.float32,
    )
    total += lax.dot_general(
        x_ref[1].reshape(blocks * rows, feat),
        other_w_ref[...],
        contract,
        preferred_element_type=jnp.float32,
    )
    gate, up = total[:, :hid], total[:, hid:]
    out_ref[...] = (gate / (1.0 + jnp.exp(-gate)) * up).astype(jnp.bfloat16)


def project(part, x_all, w_pair, step):
    blocks, rows, feat = x_all.shape[1:]
    hid2, width = w_pair.shape
    hid = hid2 // 2
    return pl.pallas_call(
        project_kernel,
        grid_spec=pltpu.PrefetchScalarGridSpec(
            num_scalar_prefetch=1,
            grid=(blocks // step,),
            in_specs=[
                pl.BlockSpec((2, step, rows, feat), lambda i, part: (0, i, 0, 0)),
                pl.BlockSpec((hid2, feat), lambda i, part: (0, part[0])),
                pl.BlockSpec((hid2, feat), lambda i, part: (0, 1 - part[0])),
            ],
            out_specs=pl.BlockSpec((step * rows, hid), lambda i, part: (i, 0)),
        ),
        out_shape=jax.ShapeDtypeStruct((blocks * rows, hid), jnp.bfloat16),
        compiler_params=pltpu.CompilerParams(vmem_limit_bytes=48 << 20),
        cost_estimate=pl.CostEstimate(
            flops=2 * blocks * rows * hid2 * width,
            bytes_accessed=2 * (blocks * rows * width + hid2 * width),
            transcendentals=blocks * rows * hid,
        ),
        name="project",
    )(part, x_all, w_pair, w_pair)


def down_kernel(part_ref, own_ref, other_ref, own_w_ref, other_w_ref, scale_ref, out_ref):
    result = jnp.dot(own_ref[...], own_w_ref[...], preferred_element_type=jnp.float32)
    result += jnp.dot(other_ref[...], other_w_ref[...], preferred_element_type=jnp.float32)
    result = result.astype(jnp.bfloat16).astype(jnp.float32)
    out_ref[...] = (result * scale_ref[...]).astype(out_ref.dtype)


def down(part, own, other, w_down, scale, block):
    rows, hid = own.shape
    depth, feat = w_down.shape
    return pl.pallas_call(
        down_kernel,
        grid_spec=pltpu.PrefetchScalarGridSpec(
            num_scalar_prefetch=1,
            grid=(rows // block,),
            in_specs=[
                pl.BlockSpec((block, hid), lambda i, part: (i, 0)),
                pl.BlockSpec((block, hid), lambda i, part: (i, 0)),
                pl.BlockSpec((hid, feat), lambda i, part: (part[0], 0)),
                pl.BlockSpec((hid, feat), lambda i, part: (1 - part[0], 0)),
                pl.BlockSpec((block, 1), lambda i, part: (i, 0)),
            ],
            out_specs=pl.BlockSpec((block, feat), lambda i, part: (i, 0)),
        ),
        out_shape=jax.ShapeDtypeStruct((rows, feat), jnp.bfloat16),
        compiler_params=pltpu.CompilerParams(vmem_limit_bytes=48 << 20),
        cost_estimate=pl.CostEstimate(
            flops=2 * rows * depth * feat,
            bytes_accessed=2 * (rows * depth + depth * feat + rows * feat),
            transcendentals=0,
        ),
        name="down",
    )(part, own, other, w_down, w_down, scale)


def hop(value, axis, mask=1):
    return lax.ppermute(value, axis, [(p, p ^ mask) for p in range(lax.axis_size(axis))])


def tie(*values):
    return lax.optimization_barrier(values)


def wide(value):
    return value.astype(jnp.float32)


def serve(hidden_own, cross_own, hidden_other, cross_other, w_down, scale):
    part = lax.axis_index("dp").astype(jnp.int32).reshape(1)
    rows = hidden_own.shape[0] // 4
    feat = w_down.shape[1]
    sent = down(part, hidden_other, cross_other, w_down, scale[1], 2 * rows)
    received = hop(sent, "core")
    kept = down(part, hidden_own, cross_own, w_down, scale[0], 2 * rows)
    return [v.reshape(2, 2, rows, feat) for v in (kept, received)]


def across_y(kept, received):
    leave = (wide(kept[1]) + wide(received[1])).astype(jnp.bfloat16)
    return wide(kept[0]) + wide(received[0]), hop(leave, "y")


def gather_stage(tokens, near, far, apart, across_0, beside_0, across_2, beside_2, table, tail, w_pair):
    rows = tokens.shape[0]
    part = lax.axis_index("dp").astype(jnp.int32).reshape(1)
    mine = jnp.arange(table.shape[1], dtype=jnp.int32) == lax.axis_index(COLUMN)
    across_3, beside_3, corner_2, table_y, near = tie(
        hop(apart, "dp"), hop(apart, "y"), hop(beside_2, "dp"), hop(table, "y"), near
    )
    table = jnp.concatenate([table, table_y])
    corner_3, across_1, beside_1, table_core, across_0, tail = tie(
        hop(across_3, "y"), hop(near, "dp"), hop(near, "y"), hop(table, "core"), across_0, tail
    )
    table = jnp.concatenate([table, table_core])
    own = jnp.stack([far, apart, beside_2, beside_3])
    x_late = jnp.stack([own, jnp.stack([across_2, across_3, corner_2, corner_3])])
    x_late_other = hop(x_late, "core")
    counts = jnp.sum((table >= 0).astype(jnp.float32), axis=(0, 2))
    scale = jnp.sum(jnp.where(mine[None, :, None], jnp.maximum(table, 0.0), 0.0), axis=1)
    scale = scale.reshape(2, 2, 2, 2, rows).transpose(0, 3, 1, 2, 4)
    scale = scale.reshape(2, 2, 4 * rows, 1)
    corner_0, corner_1 = hop(across_0, "y"), hop(beside_1, "dp")
    late_own = project(part, x_late, w_pair, 4)
    late_other = project(part, x_late_other, w_pair, 4)
    corner_0, corner_1, late_own, late_other, scale, tail = tie(
        corner_0, corner_1, late_own, late_other, scale, hop(tail, "core")
    )
    own = jnp.stack([tokens, near, beside_0, beside_1])
    x_early = jnp.stack([own, jnp.stack([across_0, across_1, corner_0, corner_1])])
    return x_early, late_own, hop(late_own, "dp"), late_other, scale, counts, tail


def expert_stage(x_early, late_own, late_own_cross, late_other, scale, w_pair, w_down):
    part = lax.axis_index("dp").astype(jnp.int32).reshape(1)
    late_other_cross = hop(late_other, "dp")
    x_early_other = hop(x_early, "core")
    early_own = project(part, x_early, w_pair, 4)
    early_own_cross = hop(early_own, "dp")
    late_other, early_own = tie(late_other, early_own)
    late = serve(late_own, late_own_cross, late_other, late_other_cross, w_down, scale[:, 1])
    early_other = project(part, x_early_other, w_pair, 4)
    early_other_cross = hop(early_other, "dp")
    line, line_y = across_y(*late)
    line = (line + wide(line_y)).astype(jnp.bfloat16)
    early = serve(early_own, early_own_cross, early_other, early_other_cross, w_down, scale[:, 0])
    total, total_y = across_y(*early)
    return line, total + wide(total_y)


def guarded(valid, stage, *operands):
    shapes = jax.eval_shape(stage, *operands)
    empty = lambda *_: jax.tree.map(lambda leaf: jnp.zeros(leaf.shape, leaf.dtype), shapes)
    return lax.cond(valid, stage, empty, *operands)


def body(tokens, expert_ids, route_weight, placement, swap_flag, gate_up, down_weight):
    ncol = lax.axis_size(COLUMN)
    half = ncol // 2
    rows = tokens.shape[0]
    topk = expert_ids.shape[1]
    hid = gate_up.shape[2]
    width = gate_up.shape[3]
    me = lax.axis_index(COLUMN)
    core = lax.axis_index("core")
    w_pair = gate_up.reshape(2 * hid, width)
    w_down = down_weight.reshape(down_weight.shape[1:])
    depth = w_down.shape[0] // 2

    slots = jnp.arange(ncol, dtype=jnp.int32)
    own = jnp.sum(jnp.where(slots[:half] == me % half, swap_flag, 0)) == 1
    sibling = jnp.sum(jnp.where(slots[:half] == (me + 1 - 2 * core) % half, swap_flag, 0)) == 1
    alone = own & ~sibling
    both = own & sibling

    picks = expert_ids[:, :, None] == jnp.arange(placement.shape[0], dtype=jnp.int32)
    slot = jnp.sum(jnp.where(picks, placement, 0), axis=2)
    here = slot[:, :, None] == slots
    named = jnp.any(here, axis=1)
    weight = jnp.sum(jnp.where(here, route_weight[:, :, None], 0.0), axis=1)
    table = jnp.where(named, weight, -1.0).T[None]

    heads, tails = (w_pair[:hid], w_down[:depth]), (w_pair[hid:], w_down[depth:])
    far, near, across_0, beside_0, table_far, late_tail = tie(
        hop(tokens, "z", 2),
        hop(tokens, "z", 1),
        hop(tokens, "dp"),
        hop(tokens, "y"),
        hop(table, "z", 2),
        tails[0],
    )
    table = jnp.concatenate([table, table_far])
    lane_pair = jnp.where(own, heads[0], hop(late_tail, "core"))
    apart, across_2, beside_2, table_near, lane_pair = tie(
        hop(far, "z", 1),
        hop(far, "dp"),
        hop(far, "y"),
        hop(table, "z", 1),
        lane_pair,
    )
    table = jnp.concatenate([table, table_near])
    mark = 2 * hid // 3
    arrived_first = hop(lane_pair[:mark], "z", 2)

    valid = placement[0] >= 0
    planes = (tokens, near, far, apart, across_0, beside_0, across_2, beside_2)
    *staged, counts, tail_down = guarded(valid, gather_stage, *planes, table, tails[1], w_pair)
    lane_down = jnp.where(own, heads[1], tail_down)
    *staged, arrived_first, lane_second, lane_down = tie(
        *staged, arrived_first, lane_pair[mark:], lane_down
    )
    arrived_second, arrived_down = hop(lane_second, "z", 2), hop(lane_down, "z", 2)
    handed_first = hop(arrived_first, "core")
    line, total = guarded(valid, expert_stage, *staged, w_pair, w_down)
    line, total, arrived_second, arrived_down = tie(line, total, arrived_second, arrived_down)
    line = (wide(line[0]) + wide(hop(line[1], "z", 1))).astype(jnp.bfloat16)
    closing = hop(total[1].astype(jnp.bfloat16), "z", 1)
    over, closing, *last = tie(hop(line, "z", 2), closing, *tails)
    handed_down, handed_second = hop(arrived_down, "core"), hop(arrived_second, "core")
    moe_out = (total[0] + wide(closing) + wide(over)).astype(jnp.bfloat16)
    partner = (slots + half * jnp.tile(swap_flag, 2)) % ncol
    column_load = jnp.sum(
        jnp.where(partner[:, None] == slots[None, :], counts[None, :], 0.0), axis=1
    ) / jnp.float32(rows * topk)

    rest = lax.cond(
        both, lambda a, b: (hop(a, "z", 2), hop(b, "z", 2)), lambda a, b: (a, b), *last
    )
    arrived = (jnp.concatenate([arrived_first, arrived_second]), arrived_down)
    handed = (jnp.concatenate([handed_first, handed_second]), handed_down)
    heads = [jnp.where(own, new, old) for new, old in zip(arrived, heads)]
    tails = [jnp.where(alone, new, old) for new, old in zip(handed, rest)]
    slot_gate_up = jnp.stack([heads[0], tails[0]])[None]
    slot_down = jnp.concatenate([heads[1], tails[1]])[None]
    return (moe_out, column_load, slot_gate_up, slot_down)


def from_behind(value, axis, steps):
    count = lax.axis_size(axis)
    pairs = [(source, (source + steps) % count) for source in range(count)]
    return lax.ppermute(value, axis, pairs)


def swapped_blocks(gate_up, down_weight, swap_flag, pair_index, half):
    incoming_pair = from_behind(gate_up, "expert", half)
    incoming_down = from_behind(down_weight, "expert", half)
    own_column = lax.axis_index("expert")
    own_flag = jnp.sum(jnp.where(pair_index == own_column % half, swap_flag, 0))
    pair_after = jnp.where(own_flag == 1, incoming_pair, gate_up)
    down_after = jnp.where(own_flag == 1, incoming_down, down_weight)
    return (pair_after, down_after)


def dispatched_body(tokens, expert_ids, route_weight, placement, swap_flag, gate_up, down_weight):
    ncol = lax.axis_size("expert")
    half = ncol // 2
    rows_here, feat_here = tokens.shape
    topk = expert_ids.shape[1]
    hid_here = gate_up.shape[2]
    width = gate_up.shape[3]
    capacity = max(4, rows_here * topk * 17 // (16 * ncol) + 2)
    experts_all = placement.shape[0]
    pair_index = jnp.arange(half, dtype=jnp.int32)
    hits = placement[:, None] % half == pair_index[None, :]
    flag_of = jnp.sum(jnp.where(hits, swap_flag[None, :], 0), axis=1)
    moved = (placement + half * flag_of) % ncol
    picks = expert_ids.reshape(-1)[:, None] == jnp.arange(experts_all, dtype=jnp.int32)[None, :]
    moved_dest = jnp.sum(jnp.where(picks, moved[None, :], 0), axis=1)
    columns = jnp.arange(ncol, dtype=jnp.int32)
    local_counts = jnp.sum((moved_dest[:, None] == columns[None, :]).astype(jnp.float32), axis=0)
    totals = lax.psum(local_counts, "expert")
    column_load = totals / jnp.float32(rows_here * topk)
    slot_gate_up, slot_down = swapped_blocks(gate_up, down_weight, swap_flag, pair_index, half)
    col_hits = moved_dest[:, None] == columns[None, :]
    order = jnp.cumsum(col_hits.astype(jnp.int32), axis=0) - 1
    position = jnp.sum(jnp.where(col_hits, order, 0), axis=1)
    slot_index = moved_dest * capacity + position
    w_pair = slot_gate_up.reshape(2 * hid_here, width)
    w_down = slot_down.reshape(slot_down.shape[1], feat_here)
    contract = (((1,), (1,)), ((), ()))
    whole = lax.all_gather(tokens, "dp", axis=1, tiled=True)
    repeated = jnp.repeat(whole, topk, axis=0)
    buffer = jnp.zeros((ncol * capacity, width), jnp.bfloat16).at[slot_index].set(repeated)
    buffer = buffer.reshape(ncol, capacity, width)
    received = lax.all_to_all(buffer, "expert", split_axis=0, concat_axis=0, tiled=True)
    blocks, count, wide = received.shape
    rows = received.reshape(blocks * count, wide)
    projected = lax.dot_general(rows, w_pair, contract, preferred_element_type=jnp.float32)
    hidden = (jax.nn.silu(projected[:, :hid_here]) * projected[:, hid_here:]).astype(jnp.bfloat16)
    mixed = jnp.dot(
        lax.all_gather(hidden, "dp", axis=1, tiled=True), w_down, preferred_element_type=jnp.float32
    )
    result = mixed.astype(jnp.bfloat16).reshape(blocks, count, feat_here)
    returned = lax.all_to_all(result, "expert", split_axis=0, concat_axis=0, tiled=True)
    flat_back = returned.reshape(ncol * capacity, feat_here)
    gathered = flat_back[slot_index].astype(jnp.float32).reshape(rows_here, topk, feat_here)
    moe_out = jnp.sum(gathered * route_weight[:, :, None], axis=1).astype(jnp.bfloat16)
    return (moe_out, column_load, slot_gate_up, slot_down)


def solution(mesh):
    expert = mesh.shape["expert"]
    if expert != 16 or mesh.shape["dp"] != 2:
        run, names, column = dispatched_body, mesh, "expert"
    else:
        shape = (mesh.shape["dp"], expert // 4, 2, 2)
        run, names, column = body, Mesh(mesh.devices.reshape(shape), ("dp", *COLUMN)), COLUMN
    return jax.shard_map(
        run,
        mesh=names,
        in_specs=(
            P(column, "dp"),
            P(column, None),
            P(column, None),
            P(),
            P(),
            P(column, None, "dp", None),
            P(column, None, "dp"),
        ),
        out_specs=(P(column, "dp"), P(), P(column, None, "dp", None), P(column, None, "dp")),
        check_vma=False,
    )
```

```python
import jax
import jax.numpy as jnp
from jax import lax
from jax.experimental import pallas as pl
from jax.experimental.pallas import tpu as pltpu
from jax.sharding import Mesh
from jax.sharding import PartitionSpec as P

COLUMN = ("z", "y", "core")


def project_kernel(part_ref, x_ref, own_w_ref, other_w_ref, out_ref):
    blocks, rows, feat = x_ref.shape[1:]
    hid = out_ref.shape[1]
    contract = (((1,), (1,)), ((), ()))
    total = lax.dot_general(
        x_ref[0].reshape(blocks * rows, feat),
        own_w_ref[...],
        contract,
        preferred_element_type=jnp.float32,
    )
    total += lax.dot_general(
        x_ref[1].reshape(blocks * rows, feat),
        other_w_ref[...],
        contract,
        preferred_element_type=jnp.float32,
    )
    gate, up = total[:, :hid], total[:, hid:]
    out_ref[...] = (gate / (1.0 + jnp.exp(-gate)) * up).astype(jnp.bfloat16)


def project(part, x_all, w_pair, step):
    blocks, rows, feat = x_all.shape[1:]
    hid2, width = w_pair.shape
    hid = hid2 // 2
    return pl.pallas_call(
        project_kernel,
        grid_spec=pltpu.PrefetchScalarGridSpec(
            num_scalar_prefetch=1,
            grid=(blocks // step,),
            in_specs=[
                pl.BlockSpec((2, step, rows, feat), lambda i, part: (0, i, 0, 0)),
                pl.BlockSpec((hid2, feat), lambda i, part: (0, part[0])),
                pl.BlockSpec((hid2, feat), lambda i, part: (0, 1 - part[0])),
            ],
            out_specs=pl.BlockSpec((step * rows, hid), lambda i, part: (i, 0)),
        ),
        out_shape=jax.ShapeDtypeStruct((blocks * rows, hid), jnp.bfloat16),
        compiler_params=pltpu.CompilerParams(vmem_limit_bytes=48 << 20),
        cost_estimate=pl.CostEstimate(
            flops=2 * blocks * rows * hid2 * width,
            bytes_accessed=2 * (blocks * rows * width + hid2 * width),
            transcendentals=blocks * rows * hid,
        ),
        name="project",
    )(part, x_all, w_pair, w_pair)


def down_kernel(part_ref, own_ref, other_ref, own_w_ref, other_w_ref, scale_ref, out_ref):
    result = jnp.dot(own_ref[...], own_w_ref[...], preferred_element_type=jnp.float32)
    result += jnp.dot(other_ref[...], other_w_ref[...], preferred_element_type=jnp.float32)
    result = result.astype(jnp.bfloat16).astype(jnp.float32)
    out_ref[...] = (result * scale_ref[...]).astype(out_ref.dtype)


def down(part, own, other, w_down, scale, block):
    rows, hid = own.shape
    depth, feat = w_down.shape
    return pl.pallas_call(
        down_kernel,
        grid_spec=pltpu.PrefetchScalarGridSpec(
            num_scalar_prefetch=1,
            grid=(rows // block,),
            in_specs=[
                pl.BlockSpec((block, hid), lambda i, part: (i, 0)),
                pl.BlockSpec((block, hid), lambda i, part: (i, 0)),
                pl.BlockSpec((hid, feat), lambda i, part: (part[0], 0)),
                pl.BlockSpec((hid, feat), lambda i, part: (1 - part[0], 0)),
                pl.BlockSpec((block, 1), lambda i, part: (i, 0)),
            ],
            out_specs=pl.BlockSpec((block, feat), lambda i, part: (i, 0)),
        ),
        out_shape=jax.ShapeDtypeStruct((rows, feat), jnp.bfloat16),
        compiler_params=pltpu.CompilerParams(vmem_limit_bytes=48 << 20),
        cost_estimate=pl.CostEstimate(
            flops=2 * rows * depth * feat,
            bytes_accessed=2 * (rows * depth + depth * feat + rows * feat),
            transcendentals=0,
        ),
        name="down",
    )(part, own, other, w_down, w_down, scale)


def hop(value, axis, mask=1):
    return lax.ppermute(value, axis, [(p, p ^ mask) for p in range(lax.axis_size(axis))])


def tie(*values):
    return lax.optimization_barrier(values)


def wide(value):
    return value.astype(jnp.float32)


def serve(hidden_own, cross_own, hidden_other, cross_other, w_down, scale):
    part = lax.axis_index("dp").astype(jnp.int32).reshape(1)
    rows = hidden_own.shape[0] // 4
    feat = w_down.shape[1]
    sent = down(part, hidden_other, cross_other, w_down, scale[1], 2 * rows)
    received = hop(sent, "core")
    kept = down(part, hidden_own, cross_own, w_down, scale[0], 2 * rows)
    return [v.reshape(2, 2, rows, feat) for v in (kept, received)]


def across_y(kept, received):
    leave = (wide(kept[1]) + wide(received[1])).astype(jnp.bfloat16)
    return wide(kept[0]) + wide(received[0]), hop(leave, "y")


def gather_stage(tokens, near, far, apart, across_0, beside_0, across_2, beside_2, table, tail, w_pair):
    rows = tokens.shape[0]
    part = lax.axis_index("dp").astype(jnp.int32).reshape(1)
    mine = jnp.arange(table.shape[1], dtype=jnp.int32) == lax.axis_index(COLUMN)
    across_3, beside_3, corner_2, table_y, near = tie(
        hop(apart, "dp"), hop(apart, "y"), hop(beside_2, "dp"), hop(table, "y"), near
    )
    table = jnp.concatenate([table, table_y])
    corner_3, across_1, beside_1, table_core, across_0, tail = tie(
        hop(across_3, "y"), hop(near, "dp"), hop(near, "y"), hop(table, "core"), across_0, tail
    )
    table = jnp.concatenate([table, table_core])
    own = jnp.stack([far, apart, beside_2, beside_3])
    x_late = jnp.stack([own, jnp.stack([across_2, across_3, corner_2, corner_3])])
    x_late_other = hop(x_late, "core")
    counts = jnp.sum((table >= 0).astype(jnp.float32), axis=(0, 2))
    scale = jnp.sum(jnp.where(mine[None, :, None], jnp.maximum(table, 0.0), 0.0), axis=1)
    scale = scale.reshape(2, 2, 2, 2, rows).transpose(0, 3, 1, 2, 4)
    scale = scale.reshape(2, 2, 4 * rows, 1)
    corner_0, corner_1 = hop(across_0, "y"), hop(beside_1, "dp")
    late_own = project(part, x_late, w_pair, 4)
    late_other = project(part, x_late_other, w_pair, 4)
    corner_0, corner_1, late_own, late_other, scale, tail = tie(
        corner_0, corner_1, late_own, late_other, scale, hop(tail, "core")
    )
    own = jnp.stack([tokens, near, beside_0, beside_1])
    x_early = jnp.stack([own, jnp.stack([across_0, across_1, corner_0, corner_1])])
    return x_early, late_own, hop(late_own, "dp"), late_other, scale, counts, tail


def expert_stage(x_early, late_own, late_own_cross, late_other, scale, w_pair, w_down):
    part = lax.axis_index("dp").astype(jnp.int32).reshape(1)
    late_other_cross = hop(late_other, "dp")
    x_early_other = hop(x_early, "core")
    early_own = project(part, x_early, w_pair, 4)
    early_own_cross = hop(early_own, "dp")
    late_other, early_own = tie(late_other, early_own)
    late = serve(late_own, late_own_cross, late_other, late_other_cross, w_down, scale[:, 1])
    early_other = project(part, x_early_other, w_pair, 4)
    early_other_cross = hop(early_other, "dp")
    line, line_y = across_y(*late)
    line = (line + wide(line_y)).astype(jnp.bfloat16)
    early = serve(early_own, early_own_cross, early_other, early_other_cross, w_down, scale[:, 0])
    line = (wide(line[0]) + wide(hop(line[1], "z", 1))).astype(jnp.bfloat16)
    total, total_y = across_y(*early)
    total = total + wide(total_y)
    return line, total[0], total[1].astype(jnp.bfloat16)


def guarded(valid, stage, *operands):
    shapes = jax.eval_shape(stage, *operands)
    empty = lambda *_: jax.tree.map(lambda leaf: jnp.zeros(leaf.shape, leaf.dtype), shapes)
    return lax.cond(valid, stage, empty, *operands)


def body(tokens, expert_ids, route_weight, placement, swap_flag, gate_up, down_weight):
    ncol = lax.axis_size(COLUMN)
    half = ncol // 2
    rows = tokens.shape[0]
    topk = expert_ids.shape[1]
    hid = gate_up.shape[2]
    width = gate_up.shape[3]
    me = lax.axis_index(COLUMN)
    core = lax.axis_index("core")
    w_pair = gate_up.reshape(2 * hid, width)
    w_down = down_weight.reshape(down_weight.shape[1:])
    depth = w_down.shape[0] // 2

    slots = jnp.arange(ncol, dtype=jnp.int32)
    own = jnp.sum(jnp.where(slots[:half] == me % half, swap_flag, 0)) == 1
    sibling = jnp.sum(jnp.where(slots[:half] == (me + 1 - 2 * core) % half, swap_flag, 0)) == 1
    alone = own & ~sibling
    both = own & sibling

    picks = expert_ids[:, :, None] == jnp.arange(placement.shape[0], dtype=jnp.int32)
    slot = jnp.sum(jnp.where(picks, placement, 0), axis=2)
    here = slot[:, :, None] == slots
    named = jnp.any(here, axis=1)
    weight = jnp.sum(jnp.where(here, route_weight[:, :, None], 0.0), axis=1)
    table = jnp.where(named, weight, -1.0).T[None]

    heads, tails = (w_pair[:hid], w_down[:depth]), (w_pair[hid:], w_down[depth:])
    far, near, across_0, beside_0, table_far, late_tail = tie(
        hop(tokens, "z", 2),
        hop(tokens, "z", 1),
        hop(tokens, "dp"),
        hop(tokens, "y"),
        hop(table, "z", 2),
        tails[0],
    )
    table = jnp.concatenate([table, table_far])
    lane_pair = jnp.where(own, heads[0], hop(late_tail, "core"))
    apart, across_2, beside_2, table_near, lane_pair = tie(
        hop(far, "z", 1),
        hop(far, "dp"),
        hop(far, "y"),
        hop(table, "z", 1),
        lane_pair,
    )
    table = jnp.concatenate([table, table_near])
    mark = 2 * hid // 3
    arrived_first = hop(lane_pair[:mark], "z", 2)

    valid = placement[0] >= 0
    planes = (tokens, near, far, apart, across_0, beside_0, across_2, beside_2)
    *staged, counts, tail_down = guarded(valid, gather_stage, *planes, table, tails[1], w_pair)
    lane_down = jnp.where(own, heads[1], tail_down)
    *staged, arrived_first, lane_second, lane_down = tie(
        *staged, arrived_first, lane_pair[mark:], lane_down
    )
    arrived_second, arrived_down = hop(lane_second, "z", 2), hop(lane_down, "z", 2)
    handed_first = hop(arrived_first, "core")
    line, total, leave = guarded(valid, expert_stage, *staged, w_pair, w_down)
    line, total, leave, arrived_second, arrived_down = tie(
        line, total, leave, arrived_second, arrived_down
    )
    over, closing = hop(line, "z", 2), hop(leave, "z", 1)
    handed_first, handed_second, handed_down, *last = tie(
        handed_first, hop(arrived_second, "core"), hop(arrived_down, "core"), *tails
    )
    partner = (slots + half * jnp.tile(swap_flag, 2)) % ncol
    column_load = jnp.sum(
        jnp.where(partner[:, None] == slots[None, :], counts[None, :], 0.0), axis=1
    ) / jnp.float32(rows * topk)

    rest = lax.cond(
        both, lambda a, b: (hop(a, "z", 2), hop(b, "z", 2)), lambda a, b: (a, b), *last
    )
    arrived = (jnp.concatenate([arrived_first, arrived_second]), arrived_down)
    handed = (jnp.concatenate([handed_first, handed_second]), handed_down)
    heads = [jnp.where(own, new, old) for new, old in zip(arrived, heads)]
    tails = [jnp.where(alone, new, old) for new, old in zip(handed, rest)]
    slot_gate_up = jnp.stack([heads[0], tails[0]])[None]
    slot_down = jnp.concatenate([heads[1], tails[1]])[None]
    over, closing, slot_gate_up, slot_down = tie(over, closing, slot_gate_up, slot_down)
    moe_out = (total + wide(closing) + wide(over)).astype(jnp.bfloat16)
    return (moe_out, column_load, slot_gate_up, slot_down)


def from_behind(value, axis, steps):
    count = lax.axis_size(axis)
    pairs = [(source, (source + steps) % count) for source in range(count)]
    return lax.ppermute(value, axis, pairs)


def swapped_blocks(gate_up, down_weight, swap_flag, pair_index, half):
    incoming_pair = from_behind(gate_up, "expert", half)
    incoming_down = from_behind(down_weight, "expert", half)
    own_column = lax.axis_index("expert")
    own_flag = jnp.sum(jnp.where(pair_index == own_column % half, swap_flag, 0))
    pair_after = jnp.where(own_flag == 1, incoming_pair, gate_up)
    down_after = jnp.where(own_flag == 1, incoming_down, down_weight)
    return (pair_after, down_after)


def dispatched_body(tokens, expert_ids, route_weight, placement, swap_flag, gate_up, down_weight):
    ncol = lax.axis_size("expert")
    half = ncol // 2
    rows_here, feat_here = tokens.shape
    topk = expert_ids.shape[1]
    hid_here = gate_up.shape[2]
    width = gate_up.shape[3]
    capacity = max(4, rows_here * topk * 17 // (16 * ncol) + 2)
    experts_all = placement.shape[0]
    pair_index = jnp.arange(half, dtype=jnp.int32)
    hits = placement[:, None] % half == pair_index[None, :]
    flag_of = jnp.sum(jnp.where(hits, swap_flag[None, :], 0), axis=1)
    moved = (placement + half * flag_of) % ncol
    picks = expert_ids.reshape(-1)[:, None] == jnp.arange(experts_all, dtype=jnp.int32)[None, :]
    moved_dest = jnp.sum(jnp.where(picks, moved[None, :], 0), axis=1)
    columns = jnp.arange(ncol, dtype=jnp.int32)
    local_counts = jnp.sum((moved_dest[:, None] == columns[None, :]).astype(jnp.float32), axis=0)
    totals = lax.psum(local_counts, "expert")
    column_load = totals / jnp.float32(rows_here * topk)
    slot_gate_up, slot_down = swapped_blocks(gate_up, down_weight, swap_flag, pair_index, half)
    col_hits = moved_dest[:, None] == columns[None, :]
    order = jnp.cumsum(col_hits.astype(jnp.int32), axis=0) - 1
    position = jnp.sum(jnp.where(col_hits, order, 0), axis=1)
    slot_index = moved_dest * capacity + position
    w_pair = slot_gate_up.reshape(2 * hid_here, width)
    w_down = slot_down.reshape(slot_down.shape[1], feat_here)
    contract = (((1,), (1,)), ((), ()))
    whole = lax.all_gather(tokens, "dp", axis=1, tiled=True)
    repeated = jnp.repeat(whole, topk, axis=0)
    buffer = jnp.zeros((ncol * capacity, width), jnp.bfloat16).at[slot_index].set(repeated)
    buffer = buffer.reshape(ncol, capacity, width)
    received = lax.all_to_all(buffer, "expert", split_axis=0, concat_axis=0, tiled=True)
    blocks, count, wide = received.shape
    rows = received.reshape(blocks * count, wide)
    projected = lax.dot_general(rows, w_pair, contract, preferred_element_type=jnp.float32)
    hidden = (jax.nn.silu(projected[:, :hid_here]) * projected[:, hid_here:]).astype(jnp.bfloat16)
    mixed = jnp.dot(
        lax.all_gather(hidden, "dp", axis=1, tiled=True), w_down, preferred_element_type=jnp.float32
    )
    result = mixed.astype(jnp.bfloat16).reshape(blocks, count, feat_here)
    returned = lax.all_to_all(result, "expert", split_axis=0, concat_axis=0, tiled=True)
    flat_back = returned.reshape(ncol * capacity, feat_here)
    gathered = flat_back[slot_index].astype(jnp.float32).reshape(rows_here, topk, feat_here)
    moe_out = jnp.sum(gathered * route_weight[:, :, None], axis=1).astype(jnp.bfloat16)
    return (moe_out, column_load, slot_gate_up, slot_down)


def solution(mesh):
    expert = mesh.shape["expert"]
    if expert != 16 or mesh.shape["dp"] != 2:
        run, names, column = dispatched_body, mesh, "expert"
    else:
        shape = (mesh.shape["dp"], expert // 4, 2, 2)
        run, names, column = body, Mesh(mesh.devices.reshape(shape), ("dp", *COLUMN)), COLUMN
    return jax.shard_map(
        run,
        mesh=names,
        in_specs=(
            P(column, "dp"),
            P(column, None),
            P(column, None),
            P(),
            P(),
            P(column, None, "dp", None),
            P(column, None, "dp"),
        ),
        out_specs=(P(column, "dp"), P(), P(column, None, "dp", None), P(column, None, "dp")),
        check_vma=False,
    )
```

```python
import jax
import jax.numpy as jnp
from jax import lax
from jax.experimental import pallas as pl
from jax.experimental.pallas import tpu as pltpu
from jax.sharding import Mesh
from jax.sharding import PartitionSpec as P

COLUMN = ("z", "y", "core")


def project_kernel(part_ref, x_ref, own_w_ref, other_w_ref, out_ref):
    blocks, rows, feat = x_ref.shape[1:]
    hid = out_ref.shape[1]
    contract = (((1,), (1,)), ((), ()))
    total = lax.dot_general(
        x_ref[0].reshape(blocks * rows, feat),
        own_w_ref[...],
        contract,
        preferred_element_type=jnp.float32,
    )
    total += lax.dot_general(
        x_ref[1].reshape(blocks * rows, feat),
        other_w_ref[...],
        contract,
        preferred_element_type=jnp.float32,
    )
    gate, up = total[:, :hid], total[:, hid:]
    out_ref[...] = (gate / (1.0 + jnp.exp(-gate)) * up).astype(jnp.bfloat16)


def project(part, x_all, w_pair, step):
    blocks, rows, feat = x_all.shape[1:]
    hid2, width = w_pair.shape
    hid = hid2 // 2
    return pl.pallas_call(
        project_kernel,
        grid_spec=pltpu.PrefetchScalarGridSpec(
            num_scalar_prefetch=1,
            grid=(blocks // step,),
            in_specs=[
                pl.BlockSpec((2, step, rows, feat), lambda i, part: (0, i, 0, 0)),
                pl.BlockSpec((hid2, feat), lambda i, part: (0, part[0])),
                pl.BlockSpec((hid2, feat), lambda i, part: (0, 1 - part[0])),
            ],
            out_specs=pl.BlockSpec((step * rows, hid), lambda i, part: (i, 0)),
        ),
        out_shape=jax.ShapeDtypeStruct((blocks * rows, hid), jnp.bfloat16),
        compiler_params=pltpu.CompilerParams(vmem_limit_bytes=48 << 20),
        cost_estimate=pl.CostEstimate(
            flops=2 * blocks * rows * hid2 * width,
            bytes_accessed=2 * (blocks * rows * width + hid2 * width),
            transcendentals=blocks * rows * hid,
        ),
        name="project",
    )(part, x_all, w_pair, w_pair)


def down_kernel(part_ref, own_ref, other_ref, own_w_ref, other_w_ref, scale_ref, out_ref):
    result = jnp.dot(own_ref[...], own_w_ref[...], preferred_element_type=jnp.float32)
    result += jnp.dot(other_ref[...], other_w_ref[...], preferred_element_type=jnp.float32)
    result = result.astype(jnp.bfloat16).astype(jnp.float32)
    out_ref[...] = (result * scale_ref[...]).astype(out_ref.dtype)


def down(part, own, other, w_down, scale, block):
    rows, hid = own.shape
    depth, feat = w_down.shape
    return pl.pallas_call(
        down_kernel,
        grid_spec=pltpu.PrefetchScalarGridSpec(
            num_scalar_prefetch=1,
            grid=(rows // block,),
            in_specs=[
                pl.BlockSpec((block, hid), lambda i, part: (i, 0)),
                pl.BlockSpec((block, hid), lambda i, part: (i, 0)),
                pl.BlockSpec((hid, feat), lambda i, part: (part[0], 0)),
                pl.BlockSpec((hid, feat), lambda i, part: (1 - part[0], 0)),
                pl.BlockSpec((block, 1), lambda i, part: (i, 0)),
            ],
            out_specs=pl.BlockSpec((block, feat), lambda i, part: (i, 0)),
        ),
        out_shape=jax.ShapeDtypeStruct((rows, feat), jnp.bfloat16),
        compiler_params=pltpu.CompilerParams(vmem_limit_bytes=48 << 20),
        cost_estimate=pl.CostEstimate(
            flops=2 * rows * depth * feat,
            bytes_accessed=2 * (rows * depth + depth * feat + rows * feat),
            transcendentals=0,
        ),
        name="down",
    )(part, own, other, w_down, w_down, scale)


def hop(value, axis, mask=1):
    return lax.ppermute(value, axis, [(p, p ^ mask) for p in range(lax.axis_size(axis))])


def tie(*values):
    return lax.optimization_barrier(values)


def wide(value):
    return value.astype(jnp.float32)


def serve(hidden_own, cross_own, hidden_other, cross_other, w_down, scale):
    part = lax.axis_index("dp").astype(jnp.int32).reshape(1)
    rows = hidden_own.shape[0] // 4
    feat = w_down.shape[1]
    sent = down(part, hidden_other, cross_other, w_down, scale[1], 2 * rows)
    received = hop(sent, "core")
    kept = down(part, hidden_own, cross_own, w_down, scale[0], 2 * rows)
    return [v.reshape(2, 2, rows, feat) for v in (kept, received)]


def across_y(kept, received):
    leave = (wide(kept[1]) + wide(received[1])).astype(jnp.bfloat16)
    return wide(kept[0]) + wide(received[0]), hop(leave, "y")


def gather_stage(tokens, near, far, apart, across_0, across_2, beside_2, table, w_pair):
    rows = tokens.shape[0]
    part = lax.axis_index("dp").astype(jnp.int32).reshape(1)
    mine = jnp.arange(table.shape[1], dtype=jnp.int32) == lax.axis_index(COLUMN)
    across_3, beside_3, corner_2, table_y, near = tie(
        hop(apart, "dp"), hop(apart, "y"), hop(beside_2, "dp"), hop(table, "y"), near
    )
    table = jnp.concatenate([table, table_y])
    corner_3, across_1, beside_1, table_core, across_0, tokens = tie(
        hop(across_3, "y"), hop(near, "dp"), hop(near, "y"), hop(table, "core"), across_0, tokens
    )
    beside_0 = hop(tokens, "y")
    table = jnp.concatenate([table, table_core])
    own = jnp.stack([far, apart, beside_2, beside_3])
    x_late = jnp.stack([own, jnp.stack([across_2, across_3, corner_2, corner_3])])
    x_late_other = hop(x_late, "core")
    corner_0, corner_1 = hop(across_0, "y"), hop(beside_1, "dp")
    late_own = project(part, x_late, w_pair, 4)
    late_other = project(part, x_late_other, w_pair, 4)
    counts = jnp.sum((table >= 0).astype(jnp.float32), axis=(0, 2))
    scale = jnp.sum(jnp.where(mine[None, :, None], jnp.maximum(table, 0.0), 0.0), axis=1)
    scale = scale.reshape(2, 2, 2, 2, rows).transpose(0, 3, 1, 2, 4)
    scale = scale.reshape(2, 2, 4 * rows, 1)
    corner_0, corner_1, late_own, late_other, scale = tie(
        corner_0, corner_1, late_own, late_other, scale
    )
    own = jnp.stack([tokens, near, beside_0, beside_1])
    x_early = jnp.stack([own, jnp.stack([across_0, across_1, corner_0, corner_1])])
    return x_early, late_own, hop(late_own, "dp"), late_other, scale, counts


def expert_stage(x_early, late_own, late_own_cross, late_other, scale, w_pair, w_down):
    part = lax.axis_index("dp").astype(jnp.int32).reshape(1)
    late_other_cross = hop(late_other, "dp")
    x_early_other = hop(x_early, "core")
    early_own = project(part, x_early, w_pair, 4)
    early_own_cross = hop(early_own, "dp")
    late_other, early_own = tie(late_other, early_own)
    late = serve(late_own, late_own_cross, late_other, late_other_cross, w_down, scale[:, 1])
    early_other = project(part, x_early_other, w_pair, 4)
    early_other_cross = hop(early_other, "dp")
    line, line_y = across_y(*late)
    line = (line + wide(line_y)).astype(jnp.bfloat16)
    early = serve(early_own, early_own_cross, early_other, early_other_cross, w_down, scale[:, 0])
    line = (wide(line[0]) + wide(hop(line[1], "z", 1))).astype(jnp.bfloat16)
    total, total_y = across_y(*early)
    total = total + wide(total_y)
    return line, total[0], total[1].astype(jnp.bfloat16)


def guarded(valid, stage, *operands):
    shapes = jax.eval_shape(stage, *operands)
    empty = lambda *_: jax.tree.map(lambda leaf: jnp.zeros(leaf.shape, leaf.dtype), shapes)
    return lax.cond(valid, stage, empty, *operands)


def body(tokens, expert_ids, route_weight, placement, swap_flag, gate_up, down_weight):
    ncol = lax.axis_size(COLUMN)
    half = ncol // 2
    rows = tokens.shape[0]
    topk = expert_ids.shape[1]
    hid = gate_up.shape[2]
    width = gate_up.shape[3]
    me = lax.axis_index(COLUMN)
    core = lax.axis_index("core")
    w_pair = gate_up.reshape(2 * hid, width)
    w_down = down_weight.reshape(down_weight.shape[1:])
    depth = w_down.shape[0] // 2

    slots = jnp.arange(ncol, dtype=jnp.int32)
    own = jnp.sum(jnp.where(slots[:half] == me % half, swap_flag, 0)) == 1
    sibling = jnp.sum(jnp.where(slots[:half] == (me + 1 - 2 * core) % half, swap_flag, 0)) == 1
    alone = own & ~sibling
    both = own & sibling

    picks = expert_ids[:, :, None] == jnp.arange(placement.shape[0], dtype=jnp.int32)
    slot = jnp.sum(jnp.where(picks, placement, 0), axis=2)
    here = slot[:, :, None] == slots
    named = jnp.any(here, axis=1)
    weight = jnp.sum(jnp.where(here, route_weight[:, :, None], 0.0), axis=1)
    table = jnp.where(named, weight, -1.0).T[None]

    heads, tails = (w_pair[:hid], w_down[:depth]), (w_pair[hid:], w_down[depth:])
    far, near, across_0, table_far, crossed, tail_down = tie(
        hop(tokens, "z", 2),
        hop(tokens, "z", 1),
        hop(tokens, "dp"),
        hop(table, "z", 2),
        hop(tails[0], "core"),
        tails[1],
    )
    table = jnp.concatenate([table, table_far])
    mark, middle = hid // 8, 17 * hid // 24
    lane_first = jnp.where(own, heads[0][:mark], crossed[:mark])
    lane_second = jnp.where(own, heads[0][mark:], crossed[mark:])
    lane_second, lane_third = lane_second[: middle - mark], lane_second[middle - mark :]
    apart, across_2, beside_2, table_near, arrived_first, crossed_down, lane_second = tie(
        hop(far, "z", 1),
        hop(far, "dp"),
        hop(far, "y"),
        hop(table, "z", 1),
        hop(lane_first, "z", 2),
        hop(tail_down, "core"),
        lane_second,
    )
    table = jnp.concatenate([table, table_near])
    arrived_second = hop(lane_second, "z", 2)

    valid = placement[0] >= 0
    planes = (tokens, near, far, apart, across_0, across_2, beside_2)
    *staged, counts = guarded(valid, gather_stage, *planes, table, w_pair)
    lane_down = jnp.where(own, heads[1], crossed_down)
    *staged, arrived_second, lane_third, lane_down = tie(
        *staged, arrived_second, lane_third, lane_down
    )
    arrived_third = hop(lane_third, "z", 2)
    arrived_down = hop(lane_down, "z", 2)
    arrived_early = jnp.concatenate([arrived_first, arrived_second])
    handed_early = hop(arrived_early, "core")
    line, total, leave = guarded(valid, expert_stage, *staged, w_pair, w_down)
    line, total, leave, arrived_third, arrived_down = tie(
        line, total, leave, arrived_third, arrived_down
    )
    over, closing = hop(line, "z", 2), hop(leave, "z", 1)
    handed_early, handed_third, handed_down, *last = tie(
        handed_early, hop(arrived_third, "core"), hop(arrived_down, "core"), *tails
    )
    partner = (slots + half * jnp.tile(swap_flag, 2)) % ncol
    column_load = jnp.sum(
        jnp.where(partner[:, None] == slots[None, :], counts[None, :], 0.0), axis=1
    ) / jnp.float32(rows * topk)

    rest = lax.cond(
        both, lambda a, b: (hop(a, "z", 2), hop(b, "z", 2)), lambda a, b: (a, b), *last
    )
    arrived = (jnp.concatenate([arrived_early, arrived_third]), arrived_down)
    handed = (jnp.concatenate([handed_early, handed_third]), handed_down)
    heads = [jnp.where(own, new, old) for new, old in zip(arrived, heads)]
    tails = [jnp.where(alone, new, old) for new, old in zip(handed, rest)]
    slot_gate_up = jnp.stack([heads[0], tails[0]])[None]
    slot_down = jnp.concatenate([heads[1], tails[1]])[None]
    over, closing, slot_gate_up, slot_down = tie(over, closing, slot_gate_up, slot_down)
    moe_out = (total + wide(closing) + wide(over)).astype(jnp.bfloat16)
    return (moe_out, column_load, slot_gate_up, slot_down)


def from_behind(value, axis, steps):
    count = lax.axis_size(axis)
    pairs = [(source, (source + steps) % count) for source in range(count)]
    return lax.ppermute(value, axis, pairs)


def swapped_blocks(gate_up, down_weight, swap_flag, pair_index, half):
    incoming_pair = from_behind(gate_up, "expert", half)
    incoming_down = from_behind(down_weight, "expert", half)
    own_column = lax.axis_index("expert")
    own_flag = jnp.sum(jnp.where(pair_index == own_column % half, swap_flag, 0))
    pair_after = jnp.where(own_flag == 1, incoming_pair, gate_up)
    down_after = jnp.where(own_flag == 1, incoming_down, down_weight)
    return (pair_after, down_after)


def dispatched_body(tokens, expert_ids, route_weight, placement, swap_flag, gate_up, down_weight):
    ncol = lax.axis_size("expert")
    half = ncol // 2
    rows_here, feat_here = tokens.shape
    topk = expert_ids.shape[1]
    hid_here = gate_up.shape[2]
    width = gate_up.shape[3]
    capacity = max(4, rows_here * topk * 17 // (16 * ncol) + 2)
    experts_all = placement.shape[0]
    pair_index = jnp.arange(half, dtype=jnp.int32)
    hits = placement[:, None] % half == pair_index[None, :]
    flag_of = jnp.sum(jnp.where(hits, swap_flag[None, :], 0), axis=1)
    moved = (placement + half * flag_of) % ncol
    picks = expert_ids.reshape(-1)[:, None] == jnp.arange(experts_all, dtype=jnp.int32)[None, :]
    moved_dest = jnp.sum(jnp.where(picks, moved[None, :], 0), axis=1)
    columns = jnp.arange(ncol, dtype=jnp.int32)
    local_counts = jnp.sum((moved_dest[:, None] == columns[None, :]).astype(jnp.float32), axis=0)
    totals = lax.psum(local_counts, "expert")
    column_load = totals / jnp.float32(rows_here * topk)
    slot_gate_up, slot_down = swapped_blocks(gate_up, down_weight, swap_flag, pair_index, half)
    col_hits = moved_dest[:, None] == columns[None, :]
    order = jnp.cumsum(col_hits.astype(jnp.int32), axis=0) - 1
    position = jnp.sum(jnp.where(col_hits, order, 0), axis=1)
    slot_index = moved_dest * capacity + position
    w_pair = slot_gate_up.reshape(2 * hid_here, width)
    w_down = slot_down.reshape(slot_down.shape[1], feat_here)
    contract = (((1,), (1,)), ((), ()))
    whole = lax.all_gather(tokens, "dp", axis=1, tiled=True)
    repeated = jnp.repeat(whole, topk, axis=0)
    buffer = jnp.zeros((ncol * capacity, width), jnp.bfloat16).at[slot_index].set(repeated)
    buffer = buffer.reshape(ncol, capacity, width)
    received = lax.all_to_all(buffer, "expert", split_axis=0, concat_axis=0, tiled=True)
    blocks, count, wide = received.shape
    rows = received.reshape(blocks * count, wide)
    projected = lax.dot_general(rows, w_pair, contract, preferred_element_type=jnp.float32)
    hidden = (jax.nn.silu(projected[:, :hid_here]) * projected[:, hid_here:]).astype(jnp.bfloat16)
    mixed = jnp.dot(
        lax.all_gather(hidden, "dp", axis=1, tiled=True), w_down, preferred_element_type=jnp.float32
    )
    result = mixed.astype(jnp.bfloat16).reshape(blocks, count, feat_here)
    returned = lax.all_to_all(result, "expert", split_axis=0, concat_axis=0, tiled=True)
    flat_back = returned.reshape(ncol * capacity, feat_here)
    gathered = flat_back[slot_index].astype(jnp.float32).reshape(rows_here, topk, feat_here)
    moe_out = jnp.sum(gathered * route_weight[:, :, None], axis=1).astype(jnp.bfloat16)
    return (moe_out, column_load, slot_gate_up, slot_down)


def solution(mesh):
    expert = mesh.shape["expert"]
    if expert != 16 or mesh.shape["dp"] != 2:
        run, names, column = dispatched_body, mesh, "expert"
    else:
        shape = (mesh.shape["dp"], expert // 4, 2, 2)
        run, names, column = body, Mesh(mesh.devices.reshape(shape), ("dp", *COLUMN)), COLUMN
    return jax.shard_map(
        run,
        mesh=names,
        in_specs=(
            P(column, "dp"),
            P(column, None),
            P(column, None),
            P(),
            P(),
            P(column, None, "dp", None),
            P(column, None, "dp"),
        ),
        out_specs=(P(column, "dp"), P(), P(column, None, "dp", None), P(column, None, "dp")),
        check_vma=False,
    )
```

```python
import jax
import jax.numpy as jnp
from jax import lax
from jax.experimental import pallas as pl
from jax.experimental.pallas import tpu as pltpu
from jax.sharding import Mesh
from jax.sharding import PartitionSpec as P

COLUMN = ("z", "y", "core")


def project_kernel(part_ref, x_ref, own_w_ref, other_w_ref, out_ref):
    blocks, rows, feat = x_ref.shape[1:]
    hid = out_ref.shape[1]
    contract = (((1,), (1,)), ((), ()))
    total = lax.dot_general(
        x_ref[0].reshape(blocks * rows, feat),
        own_w_ref[...],
        contract,
        preferred_element_type=jnp.float32,
    )
    total += lax.dot_general(
        x_ref[1].reshape(blocks * rows, feat),
        other_w_ref[...],
        contract,
        preferred_element_type=jnp.float32,
    )
    gate, up = total[:, :hid], total[:, hid:]
    out_ref[...] = (gate / (1.0 + jnp.exp(-gate)) * up).astype(jnp.bfloat16)


def project(part, x_all, w_pair, step):
    blocks, rows, feat = x_all.shape[1:]
    hid2, width = w_pair.shape
    hid = hid2 // 2
    return pl.pallas_call(
        project_kernel,
        grid_spec=pltpu.PrefetchScalarGridSpec(
            num_scalar_prefetch=1,
            grid=(blocks // step,),
            in_specs=[
                pl.BlockSpec((2, step, rows, feat), lambda i, part: (0, i, 0, 0)),
                pl.BlockSpec((hid2, feat), lambda i, part: (0, part[0])),
                pl.BlockSpec((hid2, feat), lambda i, part: (0, 1 - part[0])),
            ],
            out_specs=pl.BlockSpec((step * rows, hid), lambda i, part: (i, 0)),
        ),
        out_shape=jax.ShapeDtypeStruct((blocks * rows, hid), jnp.bfloat16),
        compiler_params=pltpu.CompilerParams(vmem_limit_bytes=48 << 20),
        cost_estimate=pl.CostEstimate(
            flops=2 * blocks * rows * hid2 * width,
            bytes_accessed=2 * (blocks * rows * width + hid2 * width),
            transcendentals=blocks * rows * hid,
        ),
        name="project",
    )(part, x_all, w_pair, w_pair)


def down_kernel(part_ref, own_ref, other_ref, own_w_ref, other_w_ref, scale_ref, out_ref):
    result = jnp.dot(own_ref[...], own_w_ref[...], preferred_element_type=jnp.float32)
    result += jnp.dot(other_ref[...], other_w_ref[...], preferred_element_type=jnp.float32)
    result = result.astype(jnp.bfloat16).astype(jnp.float32)
    out_ref[...] = (result * scale_ref[...]).astype(out_ref.dtype)


def down(part, own, other, w_down, scale, block):
    rows, hid = own.shape
    depth, feat = w_down.shape
    return pl.pallas_call(
        down_kernel,
        grid_spec=pltpu.PrefetchScalarGridSpec(
            num_scalar_prefetch=1,
            grid=(rows // block,),
            in_specs=[
                pl.BlockSpec((block, hid), lambda i, part: (i, 0)),
                pl.BlockSpec((block, hid), lambda i, part: (i, 0)),
                pl.BlockSpec((hid, feat), lambda i, part: (part[0], 0)),
                pl.BlockSpec((hid, feat), lambda i, part: (1 - part[0], 0)),
                pl.BlockSpec((block, 1), lambda i, part: (i, 0)),
            ],
            out_specs=pl.BlockSpec((block, feat), lambda i, part: (i, 0)),
        ),
        out_shape=jax.ShapeDtypeStruct((rows, feat), jnp.bfloat16),
        compiler_params=pltpu.CompilerParams(vmem_limit_bytes=48 << 20),
        cost_estimate=pl.CostEstimate(
            flops=2 * rows * depth * feat,
            bytes_accessed=2 * (rows * depth + depth * feat + rows * feat),
            transcendentals=0,
        ),
        name="down",
    )(part, own, other, w_down, w_down, scale)


def hop(value, axis, mask=1):
    return lax.ppermute(value, axis, [(p, p ^ mask) for p in range(lax.axis_size(axis))])


def tie(*values):
    return lax.optimization_barrier(values)


def wide(value):
    return value.astype(jnp.float32)


def serve(hidden_own, cross_own, hidden_other, cross_other, w_down, scale):
    part = lax.axis_index("dp").astype(jnp.int32).reshape(1)
    rows = hidden_own.shape[0] // 4
    feat = w_down.shape[1]
    sent = down(part, hidden_other, cross_other, w_down, scale[1], 2 * rows)
    received = hop(sent, "core")
    kept = down(part, hidden_own, cross_own, w_down, scale[0], 2 * rows)
    return [v.reshape(2, 2, rows, feat) for v in (kept, received)]


def across_y(kept, received):
    leave = (wide(kept[1]) + wide(received[1])).astype(jnp.bfloat16)
    return wide(kept[0]) + wide(received[0]), hop(leave, "y")


def gather_stage(tokens, near, far, apart, tail, w_pair):
    part = lax.axis_index("dp").astype(jnp.int32).reshape(1)
    across_2, beside_2, across_3, beside_3, near = tie(
        hop(far, "dp"), hop(far, "y"), hop(apart, "dp"), hop(apart, "y"), near
    )
    corner_2, corner_3, across_1, beside_1, tokens, tail = tie(
        hop(beside_2, "dp"), hop(across_3, "y"), hop(near, "dp"), hop(near, "y"), tokens, tail
    )
    across_0, beside_0, tail = hop(tokens, "dp"), hop(tokens, "y"), hop(tail, "core")
    own = jnp.stack([far, apart, beside_2, beside_3])
    x_late = jnp.stack([own, jnp.stack([across_2, across_3, corner_2, corner_3])])
    x_late_other = hop(x_late, "core")
    late_own = project(part, x_late, w_pair, 4)
    across_0, beside_0, tail, late_own, beside_1 = tie(across_0, beside_0, tail, late_own, beside_1)
    corner_0, corner_1 = hop(across_0, "y"), hop(beside_1, "dp")
    late_other = project(part, x_late_other, w_pair, 4)
    corner_0, corner_1, late_own, late_other = tie(corner_0, corner_1, late_own, late_other)
    own = jnp.stack([tokens, near, beside_0, beside_1])
    x_early = jnp.stack([own, jnp.stack([across_0, across_1, corner_0, corner_1])])
    return x_early, late_own, hop(late_own, "dp"), late_other, tail


def expert_stage(x_early, late_own, late_own_cross, late_other, table, w_pair, w_down):
    rows = x_early.shape[2]
    part = lax.axis_index("dp").astype(jnp.int32).reshape(1)
    mine = jnp.arange(table.shape[1], dtype=jnp.int32) == lax.axis_index(COLUMN)
    for axis in ("y", "core"):
        table = jnp.concatenate([table, hop(table, axis)])
    counts = jnp.sum((table >= 0).astype(jnp.float32), axis=(0, 2))
    scale = jnp.sum(jnp.where(mine[None, :, None], jnp.maximum(table, 0.0), 0.0), axis=1)
    scale = scale.reshape(2, 2, 2, 2, rows).transpose(0, 3, 1, 2, 4)
    scale = scale.reshape(2, 2, 4 * rows, 1)
    late_other_cross = hop(late_other, "dp")
    x_early_other = hop(x_early, "core")
    early_own = project(part, x_early, w_pair, 4)
    early_own_cross = hop(early_own, "dp")
    late_other, early_own = tie(late_other, early_own)
    late = serve(late_own, late_own_cross, late_other, late_other_cross, w_down, scale[:, 1])
    early_other = project(part, x_early_other, w_pair, 4)
    early_other_cross = hop(early_other, "dp")
    line, line_y = across_y(*late)
    line = (line + wide(line_y)).astype(jnp.bfloat16)
    early = serve(early_own, early_own_cross, early_other, early_other_cross, w_down, scale[:, 0])
    line = (wide(line[0]) + wide(hop(line[1], "z", 1))).astype(jnp.bfloat16)
    total, total_y = across_y(*early)
    total = total + wide(total_y)
    return line, total[0], total[1].astype(jnp.bfloat16), counts


def guarded(valid, stage, *operands):
    shapes = jax.eval_shape(stage, *operands)
    empty = lambda *_: jax.tree.map(lambda leaf: jnp.zeros(leaf.shape, leaf.dtype), shapes)
    return lax.cond(valid, stage, empty, *operands)


def body(tokens, expert_ids, route_weight, placement, swap_flag, gate_up, down_weight):
    ncol = lax.axis_size(COLUMN)
    half = ncol // 2
    rows = tokens.shape[0]
    topk = expert_ids.shape[1]
    hid = gate_up.shape[2]
    width = gate_up.shape[3]
    me = lax.axis_index(COLUMN)
    core = lax.axis_index("core")
    w_pair = gate_up.reshape(2 * hid, width)
    w_down = down_weight.reshape(down_weight.shape[1:])
    depth = w_down.shape[0] // 2

    slots = jnp.arange(ncol, dtype=jnp.int32)
    own = jnp.sum(jnp.where(slots[:half] == me % half, swap_flag, 0)) == 1
    sibling = jnp.sum(jnp.where(slots[:half] == (me + 1 - 2 * core) % half, swap_flag, 0)) == 1
    alone = own & ~sibling
    both = own & sibling

    picks = expert_ids[:, :, None] == jnp.arange(placement.shape[0], dtype=jnp.int32)
    slot = jnp.sum(jnp.where(picks, placement, 0), axis=2)
    here = slot[:, :, None] == slots
    named = jnp.any(here, axis=1)
    weight = jnp.sum(jnp.where(here, route_weight[:, :, None], 0.0), axis=1)
    table = jnp.where(named, weight, -1.0).T[None]

    heads, tails = (w_pair[:hid], w_down[:depth]), (w_pair[hid:], w_down[depth:])
    far, near, table_far, crossed = tie(
        hop(tokens, "z", 2), hop(tokens, "z", 1), hop(table, "z", 2), hop(w_pair, "core")
    )
    crossed = crossed[hid:]
    table = jnp.concatenate([table, table_far])
    mark = 19 * hid // 24
    lane_first = jnp.where(own, heads[0][:mark], crossed[:mark])
    lane_second = jnp.where(own, heads[0][mark:], crossed[mark:])
    apart, table_near, lane_first, lane_second = tie(
        hop(far, "z", 1), hop(table, "z", 1), lane_first, lane_second
    )
    table = jnp.concatenate([table, table_near])
    arrived_first = hop(lane_first, "z", 2)

    valid = placement[0] >= 0
    *staged, tail_down = guarded(
        valid, gather_stage, tokens, near, far, apart, tails[1], w_pair
    )
    lane_down = jnp.where(own, heads[1], tail_down)
    *staged, arrived_first, lane_second, lane_down = tie(
        *staged, arrived_first, lane_second, lane_down
    )
    arrived_second, arrived_down = hop(lane_second, "z", 2), hop(lane_down, "z", 2)
    line, total, leave, counts = guarded(valid, expert_stage, *staged, table, w_pair, w_down)
    line, total, leave, arrived_first, arrived_second, arrived_down = tie(
        line, total, leave, arrived_first, arrived_second, arrived_down
    )
    over, closing = hop(line, "z", 2), hop(leave, "z", 1)
    handed_first, handed_second, handed_down, *last = tie(
        *(hop(value, "core") for value in (arrived_first, arrived_second, arrived_down)), w_pair, w_down
    )
    partner = (slots + half * jnp.tile(swap_flag, 2)) % ncol
    column_load = jnp.sum(
        jnp.where(partner[:, None] == slots[None, :], counts[None, :], 0.0), axis=1
    ) / jnp.float32(rows * topk)

    rest = lax.cond(
        both,
        lambda a, b: (hop(a[hid:], "z", 2), hop(b[depth:], "z", 2)),
        lambda a, b: (a[hid:], b[depth:]),
        *last,
    )
    arrived = (jnp.concatenate([arrived_first, arrived_second]), arrived_down)
    handed = (jnp.concatenate([handed_first, handed_second]), handed_down)
    heads = [jnp.where(own, new, old) for new, old in zip(arrived, heads)]
    tails = [jnp.where(alone, new, old) for new, old in zip(handed, rest)]
    slot_gate_up = jnp.stack([heads[0], tails[0]])[None]
    slot_down = jnp.concatenate([heads[1], tails[1]])[None]
    over, closing, slot_gate_up, slot_down = tie(over, closing, slot_gate_up, slot_down)
    moe_out = (total + wide(closing) + wide(over)).astype(jnp.bfloat16)
    return (moe_out, column_load, slot_gate_up, slot_down)


def from_behind(value, axis, steps):
    count = lax.axis_size(axis)
    pairs = [(source, (source + steps) % count) for source in range(count)]
    return lax.ppermute(value, axis, pairs)


def swapped_blocks(gate_up, down_weight, swap_flag, pair_index, half):
    incoming_pair = from_behind(gate_up, "expert", half)
    incoming_down = from_behind(down_weight, "expert", half)
    own_column = lax.axis_index("expert")
    own_flag = jnp.sum(jnp.where(pair_index == own_column % half, swap_flag, 0))
    pair_after = jnp.where(own_flag == 1, incoming_pair, gate_up)
    down_after = jnp.where(own_flag == 1, incoming_down, down_weight)
    return (pair_after, down_after)


def dispatched_body(tokens, expert_ids, route_weight, placement, swap_flag, gate_up, down_weight):
    ncol = lax.axis_size("expert")
    half = ncol // 2
    rows_here, feat_here = tokens.shape
    topk = expert_ids.shape[1]
    hid_here = gate_up.shape[2]
    width = gate_up.shape[3]
    capacity = max(4, rows_here * topk * 17 // (16 * ncol) + 2)
    experts_all = placement.shape[0]
    pair_index = jnp.arange(half, dtype=jnp.int32)
    hits = placement[:, None] % half == pair_index[None, :]
    flag_of = jnp.sum(jnp.where(hits, swap_flag[None, :], 0), axis=1)
    moved = (placement + half * flag_of) % ncol
    picks = expert_ids.reshape(-1)[:, None] == jnp.arange(experts_all, dtype=jnp.int32)[None, :]
    moved_dest = jnp.sum(jnp.where(picks, moved[None, :], 0), axis=1)
    columns = jnp.arange(ncol, dtype=jnp.int32)
    local_counts = jnp.sum((moved_dest[:, None] == columns[None, :]).astype(jnp.float32), axis=0)
    totals = lax.psum(local_counts, "expert")
    column_load = totals / jnp.float32(rows_here * topk)
    slot_gate_up, slot_down = swapped_blocks(gate_up, down_weight, swap_flag, pair_index, half)
    col_hits = moved_dest[:, None] == columns[None, :]
    order = jnp.cumsum(col_hits.astype(jnp.int32), axis=0) - 1
    position = jnp.sum(jnp.where(col_hits, order, 0), axis=1)
    slot_index = moved_dest * capacity + position
    w_pair = slot_gate_up.reshape(2 * hid_here, width)
    w_down = slot_down.reshape(slot_down.shape[1], feat_here)
    contract = (((1,), (1,)), ((), ()))
    whole = lax.all_gather(tokens, "dp", axis=1, tiled=True)
    repeated = jnp.repeat(whole, topk, axis=0)
    buffer = jnp.zeros((ncol * capacity, width), jnp.bfloat16).at[slot_index].set(repeated)
    buffer = buffer.reshape(ncol, capacity, width)
    received = lax.all_to_all(buffer, "expert", split_axis=0, concat_axis=0, tiled=True)
    blocks, count, wide = received.shape
    rows = received.reshape(blocks * count, wide)
    projected = lax.dot_general(rows, w_pair, contract, preferred_element_type=jnp.float32)
    hidden = (jax.nn.silu(projected[:, :hid_here]) * projected[:, hid_here:]).astype(jnp.bfloat16)
    mixed = jnp.dot(
        lax.all_gather(hidden, "dp", axis=1, tiled=True), w_down, preferred_element_type=jnp.float32
    )
    result = mixed.astype(jnp.bfloat16).reshape(blocks, count, feat_here)
    returned = lax.all_to_all(result, "expert", split_axis=0, concat_axis=0, tiled=True)
    flat_back = returned.reshape(ncol * capacity, feat_here)
    gathered = flat_back[slot_index].astype(jnp.float32).reshape(rows_here, topk, feat_here)
    moe_out = jnp.sum(gathered * route_weight[:, :, None], axis=1).astype(jnp.bfloat16)
    return (moe_out, column_load, slot_gate_up, slot_down)


def solution(mesh):
    expert = mesh.shape["expert"]
    if expert != 16 or mesh.shape["dp"] != 2:
        run, names, column = dispatched_body, mesh, "expert"
    else:
        shape = (mesh.shape["dp"], expert // 4, 2, 2)
        run, names, column = body, Mesh(mesh.devices.reshape(shape), ("dp", *COLUMN)), COLUMN
    return jax.shard_map(
        run,
        mesh=names,
        in_specs=(
            P(column, "dp"),
            P(column, None),
            P(column, None),
            P(),
            P(),
            P(column, None, "dp", None),
            P(column, None, "dp"),
        ),
        out_specs=(P(column, "dp"), P(), P(column, None, "dp", None), P(column, None, "dp")),
        check_vma=False,
    )
```

```python
import jax
import jax.numpy as jnp
from jax import lax
from jax.experimental import pallas as pl
from jax.experimental.pallas import tpu as pltpu
from jax.sharding import Mesh
from jax.sharding import PartitionSpec as P

COLUMN = ("z", "y", "core")


def project_kernel(part_ref, x_ref, own_w_ref, other_w_ref, out_ref):
    blocks, rows, feat = x_ref.shape[1:]
    hid = out_ref.shape[1]
    contract = (((1,), (1,)), ((), ()))
    total = lax.dot_general(
        x_ref[0].reshape(blocks * rows, feat),
        own_w_ref[...],
        contract,
        preferred_element_type=jnp.float32,
    )
    total += lax.dot_general(
        x_ref[1].reshape(blocks * rows, feat),
        other_w_ref[...],
        contract,
        preferred_element_type=jnp.float32,
    )
    gate, up = total[:, :hid], total[:, hid:]
    out_ref[...] = (gate / (1.0 + jnp.exp(-gate)) * up).astype(jnp.bfloat16)


def project(part, x_all, w_pair, step):
    blocks, rows, feat = x_all.shape[1:]
    hid2, width = w_pair.shape
    hid = hid2 // 2
    return pl.pallas_call(
        project_kernel,
        grid_spec=pltpu.PrefetchScalarGridSpec(
            num_scalar_prefetch=1,
            grid=(blocks // step,),
            in_specs=[
                pl.BlockSpec((2, step, rows, feat), lambda i, part: (0, i, 0, 0)),
                pl.BlockSpec((hid2, feat), lambda i, part: (0, part[0])),
                pl.BlockSpec((hid2, feat), lambda i, part: (0, 1 - part[0])),
            ],
            out_specs=pl.BlockSpec((step * rows, hid), lambda i, part: (i, 0)),
        ),
        out_shape=jax.ShapeDtypeStruct((blocks * rows, hid), jnp.bfloat16),
        compiler_params=pltpu.CompilerParams(vmem_limit_bytes=48 << 20),
        cost_estimate=pl.CostEstimate(
            flops=2 * blocks * rows * hid2 * width,
            bytes_accessed=2 * (blocks * rows * width + hid2 * width),
            transcendentals=blocks * rows * hid,
        ),
        name="project",
    )(part, x_all, w_pair, w_pair)


def down_kernel(part_ref, own_ref, other_ref, own_w_ref, other_w_ref, scale_ref, out_ref):
    result = jnp.dot(own_ref[...], own_w_ref[...], preferred_element_type=jnp.float32)
    result += jnp.dot(other_ref[...], other_w_ref[...], preferred_element_type=jnp.float32)
    result = result.astype(jnp.bfloat16).astype(jnp.float32)
    out_ref[...] = (result * scale_ref[...]).astype(out_ref.dtype)


def down(part, own, other, w_down, scale, block):
    rows, hid = own.shape
    depth, feat = w_down.shape
    return pl.pallas_call(
        down_kernel,
        grid_spec=pltpu.PrefetchScalarGridSpec(
            num_scalar_prefetch=1,
            grid=(rows // block,),
            in_specs=[
                pl.BlockSpec((block, hid), lambda i, part: (i, 0)),
                pl.BlockSpec((block, hid), lambda i, part: (i, 0)),
                pl.BlockSpec((hid, feat), lambda i, part: (part[0], 0)),
                pl.BlockSpec((hid, feat), lambda i, part: (1 - part[0], 0)),
                pl.BlockSpec((block, 1), lambda i, part: (i, 0)),
            ],
            out_specs=pl.BlockSpec((block, feat), lambda i, part: (i, 0)),
        ),
        out_shape=jax.ShapeDtypeStruct((rows, feat), jnp.bfloat16),
        compiler_params=pltpu.CompilerParams(vmem_limit_bytes=48 << 20),
        cost_estimate=pl.CostEstimate(
            flops=2 * rows * depth * feat,
            bytes_accessed=2 * (rows * depth + depth * feat + rows * feat),
            transcendentals=0,
        ),
        name="down",
    )(part, own, other, w_down, w_down, scale)


def assemble_kernel(flags_ref, *refs):
    sources, out_ref = refs[:-1], refs[-1]
    choice = source_of(pl.program_id(0), flags_ref)
    for number, source in enumerate(sources):

        @pl.when(choice == number)
        def _():
            out_ref[...] = source[...]


def source_of(step, flags):
    late = step % 4 == 3
    arrived = jnp.where(flags[0] == 1, jnp.where(late, 1, 0), 5)
    handed = jnp.where(flags[1] == 1, jnp.where(late, 3, 2), 4)
    return jnp.where(step < 4, arrived, handed)


def assemble(flags, sources):
    rows, width = sources[-1].shape
    block = rows // 8

    def spec(number):
        def place(step, flags):
            used = source_of(step, flags) == number
            row = step if number == 5 else step % 4 if number in (0, 2, 4) else 0
            return jnp.where(used, row, 0), 0

        return pl.BlockSpec((block, width), place)

    return pl.pallas_call(
        assemble_kernel,
        grid_spec=pltpu.PrefetchScalarGridSpec(
            num_scalar_prefetch=1,
            grid=(8,),
            in_specs=[spec(number) for number in range(6)],
            out_specs=pl.BlockSpec((block, width), lambda step, flags: (step, 0)),
        ),
        out_shape=jax.ShapeDtypeStruct((rows, width), jnp.bfloat16),
        compiler_params=pltpu.CompilerParams(vmem_limit_bytes=48 << 20),
        cost_estimate=pl.CostEstimate(
            flops=0, bytes_accessed=4 * rows * width, transcendentals=0
        ),
        name="assemble",
    )(flags, *sources)


def hop(value, axis, mask=1):
    return lax.ppermute(value, axis, [(p, p ^ mask) for p in range(lax.axis_size(axis))])


def tie(*values):
    return lax.optimization_barrier(values)


def wide(value):
    return value.astype(jnp.float32)


def serve(hidden_own, cross_own, hidden_other, cross_other, w_down, scale):
    part = lax.axis_index("dp").astype(jnp.int32).reshape(1)
    rows = hidden_own.shape[0] // 4
    feat = w_down.shape[1]
    sent = down(part, hidden_other, cross_other, w_down, scale[1], 2 * rows)
    received = hop(sent, "core")
    kept = down(part, hidden_own, cross_own, w_down, scale[0], 2 * rows)
    return [v.reshape(2, 2, rows, feat) for v in (kept, received)]


def across_y(kept, received):
    leave = (wide(kept[1]) + wide(received[1])).astype(jnp.bfloat16)
    return wide(kept[0]) + wide(received[0]), hop(leave, "y")


def gather_stage(tokens, near, far, apart, tail, w_pair):
    part = lax.axis_index("dp").astype(jnp.int32).reshape(1)
    across_2, beside_2, across_3, beside_3, near = tie(
        hop(far, "dp"), hop(far, "y"), hop(apart, "dp"), hop(apart, "y"), near
    )
    corner_2, corner_3, across_1, beside_1, tokens, tail = tie(
        hop(beside_2, "dp"), hop(across_3, "y"), hop(near, "dp"), hop(near, "y"), tokens, tail
    )
    across_0, beside_0, tail = hop(tokens, "dp"), hop(tokens, "y"), hop(tail, "core")
    own = jnp.stack([far, apart, beside_2, beside_3])
    x_late = jnp.stack([own, jnp.stack([across_2, across_3, corner_2, corner_3])])
    x_late_other = hop(x_late, "core")
    late_own = project(part, x_late, w_pair, 4)
    across_0, beside_0, tail, late_own, beside_1 = tie(across_0, beside_0, tail, late_own, beside_1)
    corner_0, corner_1 = hop(across_0, "y"), hop(beside_1, "dp")
    late_other = project(part, x_late_other, w_pair, 4)
    corner_0, corner_1, late_own, late_other = tie(corner_0, corner_1, late_own, late_other)
    own = jnp.stack([tokens, near, beside_0, beside_1])
    x_early = jnp.stack([own, jnp.stack([across_0, across_1, corner_0, corner_1])])
    return x_early, late_own, hop(late_own, "dp"), late_other, tail


def expert_stage(x_early, late_own, late_own_cross, late_other, table, w_pair, w_down):
    rows = x_early.shape[2]
    part = lax.axis_index("dp").astype(jnp.int32).reshape(1)
    mine = jnp.arange(table.shape[1], dtype=jnp.int32) == lax.axis_index(COLUMN)
    for axis in ("y", "core"):
        table = jnp.concatenate([table, hop(table, axis)])
    counts = jnp.sum((table >= 0).astype(jnp.float32), axis=(0, 2))
    scale = jnp.sum(jnp.where(mine[None, :, None], jnp.maximum(table, 0.0), 0.0), axis=1)
    scale = scale.reshape(2, 2, 2, 2, rows).transpose(0, 3, 1, 2, 4)
    scale = scale.reshape(2, 2, 4 * rows, 1)
    late_other_cross = hop(late_other, "dp")
    x_early_other = hop(x_early, "core")
    early_own = project(part, x_early, w_pair, 4)
    early_own_cross = hop(early_own, "dp")
    late_other, early_own = tie(late_other, early_own)
    late = serve(late_own, late_own_cross, late_other, late_other_cross, w_down, scale[:, 1])
    early_other = project(part, x_early_other, w_pair, 4)
    early_other_cross = hop(early_other, "dp")
    line, line_y = across_y(*late)
    line = (line + wide(line_y)).astype(jnp.bfloat16)
    early = serve(early_own, early_own_cross, early_other, early_other_cross, w_down, scale[:, 0])
    line = (wide(line[0]) + wide(hop(line[1], "z", 1))).astype(jnp.bfloat16)
    total, total_y = across_y(*early)
    total = total + wide(total_y)
    return line, total[0], total[1].astype(jnp.bfloat16), counts


def guarded(valid, stage, *operands):
    shapes = jax.eval_shape(stage, *operands)
    empty = lambda *_: jax.tree.map(lambda leaf: jnp.zeros(leaf.shape, leaf.dtype), shapes)
    return lax.cond(valid, stage, empty, *operands)


def body(tokens, expert_ids, route_weight, placement, swap_flag, gate_up, down_weight):
    ncol = lax.axis_size(COLUMN)
    half = ncol // 2
    rows = tokens.shape[0]
    topk = expert_ids.shape[1]
    hid = gate_up.shape[2]
    width = gate_up.shape[3]
    me = lax.axis_index(COLUMN)
    core = lax.axis_index("core")
    w_pair = gate_up.reshape(2 * hid, width)
    w_down = down_weight.reshape(down_weight.shape[1:])
    depth = w_down.shape[0] // 2

    slots = jnp.arange(ncol, dtype=jnp.int32)
    own = jnp.sum(jnp.where(slots[:half] == me % half, swap_flag, 0)) == 1
    sibling = jnp.sum(jnp.where(slots[:half] == (me + 1 - 2 * core) % half, swap_flag, 0)) == 1
    alone = own & ~sibling
    both = own & sibling

    picks = expert_ids[:, :, None] == jnp.arange(placement.shape[0], dtype=jnp.int32)
    slot = jnp.sum(jnp.where(picks, placement, 0), axis=2)
    here = slot[:, :, None] == slots
    named = jnp.any(here, axis=1)
    weight = jnp.sum(jnp.where(here, route_weight[:, :, None], 0.0), axis=1)
    table = jnp.where(named, weight, -1.0).T[None]

    heads, tails = (w_pair[:hid], w_down[:depth]), (w_pair[hid:], w_down[depth:])
    far, near, table_far, crossed, *tails = tie(
        hop(tokens, "z", 2), hop(tokens, "z", 1), hop(table, "z", 2), hop(w_pair, "core"), *tails
    )
    crossed = crossed[hid:]
    table = jnp.concatenate([table, table_far])
    mark = 3 * hid // 4
    lane_first = jnp.where(own, heads[0][:mark], crossed[:mark])
    lane_second = jnp.where(own, heads[0][mark:], crossed[mark:])
    apart, table_near, lane_first, lane_second = tie(
        hop(far, "z", 1), hop(table, "z", 1), lane_first, lane_second
    )
    table = jnp.concatenate([table, table_near])
    arrived_first = hop(lane_first, "z", 2)

    valid = placement[0] >= 0
    *staged, tail_down = guarded(
        valid, gather_stage, tokens, near, far, apart, tails[1], w_pair
    )
    lane_down = jnp.where(own, heads[1], tail_down)
    *staged, arrived_first, lane_second, lane_down = tie(
        *staged, arrived_first, lane_second, lane_down
    )
    arrived_second, arrived_down = hop(lane_second, "z", 2), hop(lane_down, "z", 2)
    line, total, leave, counts = guarded(valid, expert_stage, *staged, table, w_pair, w_down)
    line, total, leave, arrived_first, arrived_second, arrived_down = tie(
        line, total, leave, arrived_first, arrived_second, arrived_down
    )
    over, closing = hop(line, "z", 2), hop(leave, "z", 1)
    handed_first, handed_second, handed_down, *last = tie(
        *(hop(value, "core") for value in (arrived_first, arrived_second, arrived_down)), *tails
    )
    partner = (slots + half * jnp.tile(swap_flag, 2)) % ncol
    column_load = jnp.sum(
        jnp.where(partner[:, None] == slots[None, :], counts[None, :], 0.0), axis=1
    ) / jnp.float32(rows * topk)

    rest_pair, rest_down = lax.cond(
        both, lambda a, b: (hop(a, "z", 2), hop(b, "z", 2)), lambda a, b: (a, b), *last
    )
    sources = (arrived_first, arrived_second, handed_first, handed_second, rest_pair, w_pair)
    flags = jnp.stack([own, alone]).astype(jnp.int32)
    slot_gate_up = assemble(flags, sources).reshape(gate_up.shape)
    slot_down = jnp.concatenate(
        [
            jnp.where(own, arrived_down, heads[1]),
            jnp.where(alone, handed_down, rest_down),
        ]
    )[None]
    over, closing, slot_gate_up, slot_down = tie(over, closing, slot_gate_up, slot_down)
    moe_out = (total + wide(closing) + wide(over)).astype(jnp.bfloat16)
    return (moe_out, column_load, slot_gate_up, slot_down)


def from_behind(value, axis, steps):
    count = lax.axis_size(axis)
    pairs = [(source, (source + steps) % count) for source in range(count)]
    return lax.ppermute(value, axis, pairs)


def swapped_blocks(gate_up, down_weight, swap_flag, pair_index, half):
    incoming_pair = from_behind(gate_up, "expert", half)
    incoming_down = from_behind(down_weight, "expert", half)
    own_column = lax.axis_index("expert")
    own_flag = jnp.sum(jnp.where(pair_index == own_column % half, swap_flag, 0))
    pair_after = jnp.where(own_flag == 1, incoming_pair, gate_up)
    down_after = jnp.where(own_flag == 1, incoming_down, down_weight)
    return (pair_after, down_after)


def dispatched_body(tokens, expert_ids, route_weight, placement, swap_flag, gate_up, down_weight):
    ncol = lax.axis_size("expert")
    half = ncol // 2
    rows_here, feat_here = tokens.shape
    topk = expert_ids.shape[1]
    hid_here = gate_up.shape[2]
    width = gate_up.shape[3]
    capacity = max(4, rows_here * topk * 17 // (16 * ncol) + 2)
    experts_all = placement.shape[0]
    pair_index = jnp.arange(half, dtype=jnp.int32)
    hits = placement[:, None] % half == pair_index[None, :]
    flag_of = jnp.sum(jnp.where(hits, swap_flag[None, :], 0), axis=1)
    moved = (placement + half * flag_of) % ncol
    picks = expert_ids.reshape(-1)[:, None] == jnp.arange(experts_all, dtype=jnp.int32)[None, :]
    moved_dest = jnp.sum(jnp.where(picks, moved[None, :], 0), axis=1)
    columns = jnp.arange(ncol, dtype=jnp.int32)
    local_counts = jnp.sum((moved_dest[:, None] == columns[None, :]).astype(jnp.float32), axis=0)
    totals = lax.psum(local_counts, "expert")
    column_load = totals / jnp.float32(rows_here * topk)
    slot_gate_up, slot_down = swapped_blocks(gate_up, down_weight, swap_flag, pair_index, half)
    col_hits = moved_dest[:, None] == columns[None, :]
    order = jnp.cumsum(col_hits.astype(jnp.int32), axis=0) - 1
    position = jnp.sum(jnp.where(col_hits, order, 0), axis=1)
    slot_index = moved_dest * capacity + position
    w_pair = slot_gate_up.reshape(2 * hid_here, width)
    w_down = slot_down.reshape(slot_down.shape[1], feat_here)
    contract = (((1,), (1,)), ((), ()))
    whole = lax.all_gather(tokens, "dp", axis=1, tiled=True)
    repeated = jnp.repeat(whole, topk, axis=0)
    buffer = jnp.zeros((ncol * capacity, width), jnp.bfloat16).at[slot_index].set(repeated)
    buffer = buffer.reshape(ncol, capacity, width)
    received = lax.all_to_all(buffer, "expert", split_axis=0, concat_axis=0, tiled=True)
    blocks, count, wide = received.shape
    rows = received.reshape(blocks * count, wide)
    projected = lax.dot_general(rows, w_pair, contract, preferred_element_type=jnp.float32)
    hidden = (jax.nn.silu(projected[:, :hid_here]) * projected[:, hid_here:]).astype(jnp.bfloat16)
    mixed = jnp.dot(
        lax.all_gather(hidden, "dp", axis=1, tiled=True), w_down, preferred_element_type=jnp.float32
    )
    result = mixed.astype(jnp.bfloat16).reshape(blocks, count, feat_here)
    returned = lax.all_to_all(result, "expert", split_axis=0, concat_axis=0, tiled=True)
    flat_back = returned.reshape(ncol * capacity, feat_here)
    gathered = flat_back[slot_index].astype(jnp.float32).reshape(rows_here, topk, feat_here)
    moe_out = jnp.sum(gathered * route_weight[:, :, None], axis=1).astype(jnp.bfloat16)
    return (moe_out, column_load, slot_gate_up, slot_down)


def solution(mesh):
    expert = mesh.shape["expert"]
    if expert != 16 or mesh.shape["dp"] != 2:
        run, names, column = dispatched_body, mesh, "expert"
    else:
        shape = (mesh.shape["dp"], expert // 4, 2, 2)
        run, names, column = body, Mesh(mesh.devices.reshape(shape), ("dp", *COLUMN)), COLUMN
    return jax.shard_map(
        run,
        mesh=names,
        in_specs=(
            P(column, "dp"),
            P(column, None),
            P(column, None),
            P(),
            P(),
            P(column, None, "dp", None),
            P(column, None, "dp"),
        ),
        out_specs=(P(column, "dp"), P(), P(column, None, "dp", None), P(column, None, "dp")),
        check_vma=False,
    )
```

```python
import jax
import jax.numpy as jnp
from jax import lax
from jax.experimental import pallas as pl
from jax.experimental.pallas import tpu as pltpu
from jax.sharding import Mesh
from jax.sharding import PartitionSpec as P

COLUMN = ("z", "y", "core")


def project_kernel(part_ref, x_ref, own_w_ref, other_w_ref, out_ref):
    blocks, rows, feat = x_ref.shape[1:]
    hid = out_ref.shape[1]
    contract = (((1,), (1,)), ((), ()))
    total = lax.dot_general(
        x_ref[0].reshape(blocks * rows, feat),
        own_w_ref[...],
        contract,
        preferred_element_type=jnp.float32,
    )
    total += lax.dot_general(
        x_ref[1].reshape(blocks * rows, feat),
        other_w_ref[...],
        contract,
        preferred_element_type=jnp.float32,
    )
    gate, up = total[:, :hid], total[:, hid:]
    out_ref[...] = (gate / (1.0 + jnp.exp(-gate)) * up).astype(jnp.bfloat16)


def project(part, x_all, w_pair, step):
    blocks, rows, feat = x_all.shape[1:]
    hid2, width = w_pair.shape
    hid = hid2 // 2
    return pl.pallas_call(
        project_kernel,
        grid_spec=pltpu.PrefetchScalarGridSpec(
            num_scalar_prefetch=1,
            grid=(blocks // step,),
            in_specs=[
                pl.BlockSpec((2, step, rows, feat), lambda i, part: (0, i, 0, 0)),
                pl.BlockSpec((hid2, feat), lambda i, part: (0, part[0])),
                pl.BlockSpec((hid2, feat), lambda i, part: (0, 1 - part[0])),
            ],
            out_specs=pl.BlockSpec((step * rows, hid), lambda i, part: (i, 0)),
        ),
        out_shape=jax.ShapeDtypeStruct((blocks * rows, hid), jnp.bfloat16),
        compiler_params=pltpu.CompilerParams(vmem_limit_bytes=48 << 20),
        cost_estimate=pl.CostEstimate(
            flops=2 * blocks * rows * hid2 * width,
            bytes_accessed=2 * (blocks * rows * width + hid2 * width),
            transcendentals=blocks * rows * hid,
        ),
        name="project",
    )(part, x_all, w_pair, w_pair)


def down_kernel(part_ref, own_ref, other_ref, own_w_ref, other_w_ref, scale_ref, out_ref):
    result = jnp.dot(own_ref[...], own_w_ref[...], preferred_element_type=jnp.float32)
    result += jnp.dot(other_ref[...], other_w_ref[...], preferred_element_type=jnp.float32)
    result = result.astype(jnp.bfloat16).astype(jnp.float32)
    out_ref[...] = (result * scale_ref[...]).astype(out_ref.dtype)


def down(part, own, other, w_down, scale, block):
    rows, hid = own.shape
    depth, feat = w_down.shape
    return pl.pallas_call(
        down_kernel,
        grid_spec=pltpu.PrefetchScalarGridSpec(
            num_scalar_prefetch=1,
            grid=(rows // block,),
            in_specs=[
                pl.BlockSpec((block, hid), lambda i, part: (i, 0)),
                pl.BlockSpec((block, hid), lambda i, part: (i, 0)),
                pl.BlockSpec((hid, feat), lambda i, part: (part[0], 0)),
                pl.BlockSpec((hid, feat), lambda i, part: (1 - part[0], 0)),
                pl.BlockSpec((block, 1), lambda i, part: (i, 0)),
            ],
            out_specs=pl.BlockSpec((block, feat), lambda i, part: (i, 0)),
        ),
        out_shape=jax.ShapeDtypeStruct((rows, feat), jnp.bfloat16),
        compiler_params=pltpu.CompilerParams(vmem_limit_bytes=48 << 20),
        cost_estimate=pl.CostEstimate(
            flops=2 * rows * depth * feat,
            bytes_accessed=2 * (rows * depth + depth * feat + rows * feat),
            transcendentals=0,
        ),
        name="down",
    )(part, own, other, w_down, w_down, scale)


def assemble_kernel(flags_ref, *refs):
    sources, out_ref = refs[:-1], refs[-1]
    choice = source_of(pl.program_id(0), flags_ref)
    for number, source in enumerate(sources):

        @pl.when(choice == number)
        def _():
            out_ref[...] = source[...]


def source_of(step, flags):
    arrived = jnp.where(flags[0] == 1, 0, 3)
    handed = jnp.where(flags[1] == 1, 1, 2)
    return jnp.where(step < 4, arrived, handed)


def assemble(flags, sources):
    rows, width = sources[-1].shape
    block = rows // 8

    def spec(number):
        def place(step, flags):
            used = source_of(step, flags) == number
            row = step if number == 3 else step % 4
            return jnp.where(used, row, 0), 0

        return pl.BlockSpec((block, width), place)

    return pl.pallas_call(
        assemble_kernel,
        grid_spec=pltpu.PrefetchScalarGridSpec(
            num_scalar_prefetch=1,
            grid=(8,),
            in_specs=[spec(number) for number in range(4)],
            out_specs=pl.BlockSpec((block, width), lambda step, flags: (step, 0)),
        ),
        out_shape=jax.ShapeDtypeStruct((rows, width), jnp.bfloat16),
        compiler_params=pltpu.CompilerParams(vmem_limit_bytes=48 << 20),
        cost_estimate=pl.CostEstimate(
            flops=0, bytes_accessed=4 * rows * width, transcendentals=0
        ),
        name="assemble",
    )(flags, *sources)


def hop(value, axis, mask=1):
    return lax.ppermute(value, axis, [(p, p ^ mask) for p in range(lax.axis_size(axis))])


def tie(*values):
    return lax.optimization_barrier(values)


def wide(value):
    return value.astype(jnp.float32)


def serve(hidden_own, cross_own, hidden_other, cross_other, w_down, scale):
    part = lax.axis_index("dp").astype(jnp.int32).reshape(1)
    rows = hidden_own.shape[0] // 4
    feat = w_down.shape[1]
    sent = down(part, hidden_other, cross_other, w_down, scale[1], 2 * rows)
    received = hop(sent, "core")
    kept = down(part, hidden_own, cross_own, w_down, scale[0], 2 * rows)
    return [v.reshape(2, 2, rows, feat) for v in (kept, received)]


def across_y(kept, received):
    leave = (wide(kept[1]) + wide(received[1])).astype(jnp.bfloat16)
    return wide(kept[0]) + wide(received[0]), hop(leave, "y")


def gather_stage(tokens, near, far, apart, tail, table, w_pair):
    rows = tokens.shape[0]
    part = lax.axis_index("dp").astype(jnp.int32).reshape(1)
    across_2, beside_2, across_3, beside_3, near = tie(
        hop(far, "dp"), hop(far, "y"), hop(apart, "dp"), hop(apart, "y"), near
    )
    corner_2, corner_3, across_1, beside_1, tokens, tail = tie(
        hop(beside_2, "dp"), hop(across_3, "y"), hop(near, "dp"), hop(near, "y"), tokens, tail
    )
    across_0, beside_0, tail = hop(tokens, "dp"), hop(tokens, "y"), hop(tail, "core")
    own = jnp.stack([far, apart, beside_2, beside_3])
    x_late = jnp.stack([own, jnp.stack([across_2, across_3, corner_2, corner_3])])
    x_late_other = hop(x_late, "core")
    late_own = project(part, x_late, w_pair, 4)
    across_0, beside_0, tail, late_own, beside_1 = tie(across_0, beside_0, tail, late_own, beside_1)
    corner_0, corner_1 = hop(across_0, "y"), hop(beside_1, "dp")
    late_other = project(part, x_late_other, w_pair, 4)
    corner_0, corner_1, late_own, late_other, table = tie(
        corner_0, corner_1, late_own, late_other, table
    )
    own = jnp.stack([tokens, near, beside_0, beside_1])
    x_early = jnp.stack([own, jnp.stack([across_0, across_1, corner_0, corner_1])])
    x_early, late_own_cross, late_other_cross, table_y = tie(
        x_early, hop(late_own, "dp"), hop(late_other, "dp"), hop(table, "y")
    )
    table = jnp.concatenate([table, table_y])
    table = jnp.concatenate([table, hop(table, "core")])
    mine = jnp.arange(table.shape[1], dtype=jnp.int32) == lax.axis_index(COLUMN)
    counts = jnp.sum((table >= 0).astype(jnp.float32), axis=(0, 2))
    scale = jnp.sum(jnp.where(mine[None, :, None], jnp.maximum(table, 0.0), 0.0), axis=1)
    scale = scale.reshape(2, 2, 2, 2, rows).transpose(0, 3, 1, 2, 4)
    scale = scale.reshape(2, 2, 4 * rows, 1)
    x_early_other = hop(x_early, "core")
    early_own = project(part, x_early, w_pair, 4)
    late = (late_own, late_own_cross, late_other, late_other_cross)
    early = (early_own, hop(early_own, "dp"), x_early_other)
    return late, early, scale, tail, counts


def expert_stage(late, early, scale, w_pair, w_down):
    part = lax.axis_index("dp").astype(jnp.int32).reshape(1)
    early_own, early_own_cross, x_early_other = early
    late = serve(*late, w_down, scale[:, 1])
    early_other = project(part, x_early_other, w_pair, 4)
    early_other_cross = hop(early_other, "dp")
    line, line_y = across_y(*late)
    line = (line + wide(line_y)).astype(jnp.bfloat16)
    early = serve(early_own, early_own_cross, early_other, early_other_cross, w_down, scale[:, 0])
    line = (wide(line[0]) + wide(hop(line[1], "z", 1))).astype(jnp.bfloat16)
    total, total_y = across_y(*early)
    total = total + wide(total_y)
    return line, total[0], total[1].astype(jnp.bfloat16)


def guarded(valid, stage, *operands):
    shapes = jax.eval_shape(stage, *operands)
    empty = lambda *_: jax.tree.map(lambda leaf: jnp.zeros(leaf.shape, leaf.dtype), shapes)
    return lax.cond(valid, stage, empty, *operands)


def body(tokens, expert_ids, route_weight, placement, swap_flag, gate_up, down_weight):
    ncol = lax.axis_size(COLUMN)
    half = ncol // 2
    rows = tokens.shape[0]
    topk = expert_ids.shape[1]
    hid = gate_up.shape[2]
    width = gate_up.shape[3]
    me = lax.axis_index(COLUMN)
    core = lax.axis_index("core")
    w_pair = gate_up.reshape(2 * hid, width)
    w_down = down_weight.reshape(down_weight.shape[1:])
    depth = w_down.shape[0] // 2

    slots = jnp.arange(ncol, dtype=jnp.int32)
    own = jnp.sum(jnp.where(slots[:half] == me % half, swap_flag, 0)) == 1
    sibling = jnp.sum(jnp.where(slots[:half] == (me + 1 - 2 * core) % half, swap_flag, 0)) == 1
    alone = own & ~sibling
    both = own & sibling

    picks = expert_ids[:, :, None] == jnp.arange(placement.shape[0], dtype=jnp.int32)
    slot = jnp.sum(jnp.where(picks, placement, 0), axis=2)
    here = slot[:, :, None] == slots
    named = jnp.any(here, axis=1)
    weight = jnp.sum(jnp.where(here, route_weight[:, :, None], 0.0), axis=1)
    table = jnp.where(named, weight, -1.0).T[None]

    heads, tails = (w_pair[:hid], w_down[:depth]), (w_pair[hid:], w_down[depth:])
    far, near, table_far, crossed, *tails = tie(
        hop(tokens, "z", 2), hop(tokens, "z", 1), hop(table, "z", 2), hop(w_pair, "core"), *tails
    )
    crossed = crossed[hid:]
    table = jnp.concatenate([table, table_far])
    lane_pair = jnp.where(own, heads[0], crossed)
    apart, table_near, lane_pair = tie(hop(far, "z", 1), hop(table, "z", 1), lane_pair)
    table = jnp.concatenate([table, table_near])
    arrived_pair = hop(lane_pair, "z", 2)

    valid = placement[0] >= 0
    *staged, tail_down, counts = guarded(
        valid, gather_stage, tokens, near, far, apart, tails[1], table, w_pair
    )
    lane_down = jnp.where(own, heads[1], tail_down)
    (*late, early_own, early_cross, x_other, scale, arrived_pair, lane_down) = tie(
        *staged[0], *staged[1], staged[2], arrived_pair, lane_down
    )
    arrived_down = hop(lane_down, "z", 2)
    handed_pair = hop(arrived_pair, "core")
    line, total, leave = guarded(
        valid, expert_stage, late, (early_own, early_cross, x_other), scale, w_pair, w_down
    )
    line, total, leave, arrived_down = tie(line, total, leave, arrived_down)
    over, closing = hop(line, "z", 2), hop(leave, "z", 1)
    handed_pair, handed_down, *last = tie(handed_pair, hop(arrived_down, "core"), *tails)
    partner = (slots + half * jnp.tile(swap_flag, 2)) % ncol
    column_load = jnp.sum(
        jnp.where(partner[:, None] == slots[None, :], counts[None, :], 0.0), axis=1
    ) / jnp.float32(rows * topk)

    rest_pair, rest_down = lax.cond(
        both, lambda a, b: (hop(a, "z", 2), hop(b, "z", 2)), lambda a, b: (a, b), *last
    )
    sources = (arrived_pair, handed_pair, rest_pair, w_pair)
    flags = jnp.stack([own, alone]).astype(jnp.int32)
    slot_gate_up = assemble(flags, sources).reshape(gate_up.shape)
    slot_down = jnp.concatenate(
        [
            jnp.where(own, arrived_down, heads[1]),
            jnp.where(alone, handed_down, rest_down),
        ]
    )[None]
    over, closing, slot_gate_up, slot_down = tie(over, closing, slot_gate_up, slot_down)
    moe_out = (total + wide(closing) + wide(over)).astype(jnp.bfloat16)
    return (moe_out, column_load, slot_gate_up, slot_down)


def from_behind(value, axis, steps):
    count = lax.axis_size(axis)
    pairs = [(source, (source + steps) % count) for source in range(count)]
    return lax.ppermute(value, axis, pairs)


def swapped_blocks(gate_up, down_weight, swap_flag, pair_index, half):
    incoming_pair = from_behind(gate_up, "expert", half)
    incoming_down = from_behind(down_weight, "expert", half)
    own_column = lax.axis_index("expert")
    own_flag = jnp.sum(jnp.where(pair_index == own_column % half, swap_flag, 0))
    pair_after = jnp.where(own_flag == 1, incoming_pair, gate_up)
    down_after = jnp.where(own_flag == 1, incoming_down, down_weight)
    return (pair_after, down_after)


def dispatched_body(tokens, expert_ids, route_weight, placement, swap_flag, gate_up, down_weight):
    ncol = lax.axis_size("expert")
    half = ncol // 2
    rows_here, feat_here = tokens.shape
    topk = expert_ids.shape[1]
    hid_here = gate_up.shape[2]
    width = gate_up.shape[3]
    capacity = max(4, rows_here * topk * 17 // (16 * ncol) + 2)
    experts_all = placement.shape[0]
    pair_index = jnp.arange(half, dtype=jnp.int32)
    hits = placement[:, None] % half == pair_index[None, :]
    flag_of = jnp.sum(jnp.where(hits, swap_flag[None, :], 0), axis=1)
    moved = (placement + half * flag_of) % ncol
    picks = expert_ids.reshape(-1)[:, None] == jnp.arange(experts_all, dtype=jnp.int32)[None, :]
    moved_dest = jnp.sum(jnp.where(picks, moved[None, :], 0), axis=1)
    columns = jnp.arange(ncol, dtype=jnp.int32)
    local_counts = jnp.sum((moved_dest[:, None] == columns[None, :]).astype(jnp.float32), axis=0)
    totals = lax.psum(local_counts, "expert")
    column_load = totals / jnp.float32(rows_here * topk)
    slot_gate_up, slot_down = swapped_blocks(gate_up, down_weight, swap_flag, pair_index, half)
    col_hits = moved_dest[:, None] == columns[None, :]
    order = jnp.cumsum(col_hits.astype(jnp.int32), axis=0) - 1
    position = jnp.sum(jnp.where(col_hits, order, 0), axis=1)
    slot_index = moved_dest * capacity + position
    w_pair = slot_gate_up.reshape(2 * hid_here, width)
    w_down = slot_down.reshape(slot_down.shape[1], feat_here)
    contract = (((1,), (1,)), ((), ()))
    whole = lax.all_gather(tokens, "dp", axis=1, tiled=True)
    repeated = jnp.repeat(whole, topk, axis=0)
    buffer = jnp.zeros((ncol * capacity, width), jnp.bfloat16).at[slot_index].set(repeated)
    buffer = buffer.reshape(ncol, capacity, width)
    received = lax.all_to_all(buffer, "expert", split_axis=0, concat_axis=0, tiled=True)
    blocks, count, wide = received.shape
    rows = received.reshape(blocks * count, wide)
    projected = lax.dot_general(rows, w_pair, contract, preferred_element_type=jnp.float32)
    hidden = (jax.nn.silu(projected[:, :hid_here]) * projected[:, hid_here:]).astype(jnp.bfloat16)
    mixed = jnp.dot(
        lax.all_gather(hidden, "dp", axis=1, tiled=True), w_down, preferred_element_type=jnp.float32
    )
    result = mixed.astype(jnp.bfloat16).reshape(blocks, count, feat_here)
    returned = lax.all_to_all(result, "expert", split_axis=0, concat_axis=0, tiled=True)
    flat_back = returned.reshape(ncol * capacity, feat_here)
    gathered = flat_back[slot_index].astype(jnp.float32).reshape(rows_here, topk, feat_here)
    moe_out = jnp.sum(gathered * route_weight[:, :, None], axis=1).astype(jnp.bfloat16)
    return (moe_out, column_load, slot_gate_up, slot_down)


def solution(mesh):
    expert = mesh.shape["expert"]
    if expert != 16 or mesh.shape["dp"] != 2:
        run, names, column = dispatched_body, mesh, "expert"
    else:
        shape = (mesh.shape["dp"], expert // 4, 2, 2)
        run, names, column = body, Mesh(mesh.devices.reshape(shape), ("dp", *COLUMN)), COLUMN
    return jax.shard_map(
        run,
        mesh=names,
        in_specs=(
            P(column, "dp"),
            P(column, None),
            P(column, None),
            P(),
            P(),
            P(column, None, "dp", None),
            P(column, None, "dp"),
        ),
        out_specs=(P(column, "dp"), P(), P(column, None, "dp", None), P(column, None, "dp")),
        check_vma=False,
    )
```

```python
import jax
import jax.numpy as jnp
from jax import lax
from jax.experimental import pallas as pl
from jax.experimental.pallas import tpu as pltpu
from jax.sharding import Mesh
from jax.sharding import PartitionSpec as P

COLUMN = ("z", "y", "core")


def project_kernel(part_ref, x_ref, own_w_ref, other_w_ref, out_ref):
    blocks, rows, feat = x_ref.shape[1:]
    hid = out_ref.shape[1]
    contract = (((1,), (1,)), ((), ()))
    total = lax.dot_general(
        x_ref[0].reshape(blocks * rows, feat),
        own_w_ref[...],
        contract,
        preferred_element_type=jnp.float32,
    )
    total += lax.dot_general(
        x_ref[1].reshape(blocks * rows, feat),
        other_w_ref[...],
        contract,
        preferred_element_type=jnp.float32,
    )
    gate, up = total[:, :hid], total[:, hid:]
    out_ref[...] = (gate / (1.0 + jnp.exp(-gate)) * up).astype(jnp.bfloat16)


def project(part, x_all, w_pair, step):
    blocks, rows, feat = x_all.shape[1:]
    hid2, width = w_pair.shape
    hid = hid2 // 2
    return pl.pallas_call(
        project_kernel,
        grid_spec=pltpu.PrefetchScalarGridSpec(
            num_scalar_prefetch=1,
            grid=(blocks // step,),
            in_specs=[
                pl.BlockSpec((2, step, rows, feat), lambda i, part: (0, i, 0, 0)),
                pl.BlockSpec((hid2, feat), lambda i, part: (0, part[0])),
                pl.BlockSpec((hid2, feat), lambda i, part: (0, 1 - part[0])),
            ],
            out_specs=pl.BlockSpec((step * rows, hid), lambda i, part: (i, 0)),
        ),
        out_shape=jax.ShapeDtypeStruct((blocks * rows, hid), jnp.bfloat16),
        compiler_params=pltpu.CompilerParams(vmem_limit_bytes=48 << 20),
        cost_estimate=pl.CostEstimate(
            flops=2 * blocks * rows * hid2 * width,
            bytes_accessed=2 * (blocks * rows * width + hid2 * width),
            transcendentals=blocks * rows * hid,
        ),
        name="project",
    )(part, x_all, w_pair, w_pair)


def down_kernel(part_ref, own_ref, other_ref, own_w_ref, other_w_ref, scale_ref, out_ref):
    result = jnp.dot(own_ref[...], own_w_ref[...], preferred_element_type=jnp.float32)
    result += jnp.dot(other_ref[...], other_w_ref[...], preferred_element_type=jnp.float32)
    result = result.astype(jnp.bfloat16).astype(jnp.float32)
    out_ref[...] = (result * scale_ref[...]).astype(out_ref.dtype)


def down(part, own, other, w_down, scale, block):
    rows, hid = own.shape
    depth, feat = w_down.shape
    return pl.pallas_call(
        down_kernel,
        grid_spec=pltpu.PrefetchScalarGridSpec(
            num_scalar_prefetch=1,
            grid=(rows // block,),
            in_specs=[
                pl.BlockSpec((block, hid), lambda i, part: (i, 0)),
                pl.BlockSpec((block, hid), lambda i, part: (i, 0)),
                pl.BlockSpec((hid, feat), lambda i, part: (part[0], 0)),
                pl.BlockSpec((hid, feat), lambda i, part: (1 - part[0], 0)),
                pl.BlockSpec((block, 1), lambda i, part: (i, 0)),
            ],
            out_specs=pl.BlockSpec((block, feat), lambda i, part: (i, 0)),
        ),
        out_shape=jax.ShapeDtypeStruct((rows, feat), jnp.bfloat16),
        compiler_params=pltpu.CompilerParams(vmem_limit_bytes=48 << 20),
        cost_estimate=pl.CostEstimate(
            flops=2 * rows * depth * feat,
            bytes_accessed=2 * (rows * depth + depth * feat + rows * feat),
            transcendentals=0,
        ),
        name="down",
    )(part, own, other, w_down, w_down, scale)


def assemble_kernel(flags_ref, *refs):
    sources, out_ref = refs[:-1], refs[-1]
    choice = source_of(pl.program_id(0), flags_ref)
    for number, source in enumerate(sources):

        @pl.when(choice == number)
        def _():
            out_ref[...] = source[...]


def source_of(step, flags):
    arrived = jnp.where(flags[0] == 1, 0, 3)
    handed = jnp.where(flags[1] == 1, 1, 2)
    return jnp.where(step < 4, arrived, handed)


def assemble(flags, sources):
    rows, width = sources[-1].shape
    block = rows // 8

    def spec(number):
        def place(step, flags):
            used = source_of(step, flags) == number
            row = step if number == 3 else step % 4
            return jnp.where(used, row, 0), 0

        return pl.BlockSpec((block, width), place)

    return pl.pallas_call(
        assemble_kernel,
        grid_spec=pltpu.PrefetchScalarGridSpec(
            num_scalar_prefetch=1,
            grid=(8,),
            in_specs=[spec(number) for number in range(4)],
            out_specs=pl.BlockSpec((block, width), lambda step, flags: (step, 0)),
        ),
        out_shape=jax.ShapeDtypeStruct((rows, width), jnp.bfloat16),
        compiler_params=pltpu.CompilerParams(vmem_limit_bytes=48 << 20),
        cost_estimate=pl.CostEstimate(
            flops=0, bytes_accessed=4 * rows * width, transcendentals=0
        ),
        name="assemble",
    )(flags, *sources)


def hop(value, axis, mask=1):
    return lax.ppermute(value, axis, [(p, p ^ mask) for p in range(lax.axis_size(axis))])


def tie(*values):
    return lax.optimization_barrier(values)


def wide(value):
    return value.astype(jnp.float32)


def serve(hidden_own, cross_own, hidden_other, cross_other, w_down, scale):
    part = lax.axis_index("dp").astype(jnp.int32).reshape(1)
    rows = hidden_own.shape[0] // 4
    feat = w_down.shape[1]
    sent = down(part, hidden_other, cross_other, w_down, scale[1], 2 * rows)
    received = hop(sent, "core")
    kept = down(part, hidden_own, cross_own, w_down, scale[0], 2 * rows)
    return [v.reshape(2, 2, rows, feat) for v in (kept, received)]


def across_y(kept, received):
    leave = (wide(kept[1]) + wide(received[1])).astype(jnp.bfloat16)
    return wide(kept[0]) + wide(received[0]), hop(leave, "y")


def gather_stage(tokens, near, far, apart, tail, table, w_pair):
    rows = tokens.shape[0]
    part = lax.axis_index("dp").astype(jnp.int32).reshape(1)
    across_2, beside_2, across_3, beside_3, near = tie(
        hop(far, "dp"), hop(far, "y"), hop(apart, "dp"), hop(apart, "y"), near
    )
    corner_2, corner_3, across_1, beside_1, tokens, tail = tie(
        hop(beside_2, "dp"), hop(across_3, "y"), hop(near, "dp"), hop(near, "y"), tokens, tail
    )
    across_0, beside_0, tail = hop(tokens, "dp"), hop(tokens, "y"), hop(tail, "core")
    own = jnp.stack([far, apart, beside_2, beside_3])
    x_late = jnp.stack([own, jnp.stack([across_2, across_3, corner_2, corner_3])])
    x_late_other = hop(x_late, "core")
    late_own = project(part, x_late, w_pair, 4)
    across_0, beside_0, tail, late_own, beside_1 = tie(across_0, beside_0, tail, late_own, beside_1)
    corner_0, corner_1 = hop(across_0, "y"), hop(beside_1, "dp")
    late_other = project(part, x_late_other, w_pair, 4)
    corner_0, corner_1, late_own, late_other, table = tie(
        corner_0, corner_1, late_own, late_other, table
    )
    own = jnp.stack([tokens, near, beside_0, beside_1])
    x_early = jnp.stack([own, jnp.stack([across_0, across_1, corner_0, corner_1])])
    x_early, late_own_cross, late_other_cross, table_y = tie(
        x_early, hop(late_own, "dp"), hop(late_other, "dp"), hop(table, "y")
    )
    table = jnp.concatenate([table, table_y])
    table = jnp.concatenate([table, hop(table, "core")])
    mine = jnp.arange(table.shape[1], dtype=jnp.int32) == lax.axis_index(COLUMN)
    counts = jnp.sum((table >= 0).astype(jnp.float32), axis=(0, 2))
    scale = jnp.sum(jnp.where(mine[None, :, None], jnp.maximum(table, 0.0), 0.0), axis=1)
    scale = scale.reshape(2, 2, 2, 2, rows).transpose(0, 3, 1, 2, 4)
    scale = scale.reshape(2, 2, 4 * rows, 1)
    x_early_other = hop(x_early, "core")
    early_own = project(part, x_early, w_pair, 4)
    late = (late_own, late_own_cross, late_other, late_other_cross)
    early = (early_own, hop(early_own, "dp"), x_early_other)
    return late, early, scale, tail, counts


def expert_stage(late, early, scale, w_pair, w_down):
    part = lax.axis_index("dp").astype(jnp.int32).reshape(1)
    early_own, early_own_cross, x_early_other = early
    kept, received = serve(*late, w_down, scale[:, 1])
    leave = (wide(kept[1]) + wide(received[1])).astype(jnp.bfloat16)
    leave, x_early_other = tie(leave, x_early_other)
    line, line_y = wide(kept[0]) + wide(received[0]), hop(leave, "y")
    early_other = project(part, x_early_other, w_pair, 4)
    early_other_cross, line_y = tie(hop(early_other, "dp"), line_y)
    line = (line + wide(line_y)).astype(jnp.bfloat16)
    early = serve(early_own, early_own_cross, early_other, early_other_cross, w_down, scale[:, 0])
    line = (wide(line[0]) + wide(hop(line[1], "z", 1))).astype(jnp.bfloat16)
    total, total_y = across_y(*early)
    total = total + wide(total_y)
    return line, total[0], total[1].astype(jnp.bfloat16)


def guarded(valid, stage, *operands):
    shapes = jax.eval_shape(stage, *operands)
    empty = lambda *_: jax.tree.map(lambda leaf: jnp.zeros(leaf.shape, leaf.dtype), shapes)
    return lax.cond(valid, stage, empty, *operands)


def body(tokens, expert_ids, route_weight, placement, swap_flag, gate_up, down_weight):
    ncol = lax.axis_size(COLUMN)
    half = ncol // 2
    rows = tokens.shape[0]
    topk = expert_ids.shape[1]
    hid = gate_up.shape[2]
    width = gate_up.shape[3]
    me = lax.axis_index(COLUMN)
    core = lax.axis_index("core")
    w_pair = gate_up.reshape(2 * hid, width)
    w_down = down_weight.reshape(down_weight.shape[1:])
    depth = w_down.shape[0] // 2

    slots = jnp.arange(ncol, dtype=jnp.int32)
    own = jnp.sum(jnp.where(slots[:half] == me % half, swap_flag, 0)) == 1
    sibling = jnp.sum(jnp.where(slots[:half] == (me + 1 - 2 * core) % half, swap_flag, 0)) == 1
    alone = own & ~sibling
    both = own & sibling

    picks = expert_ids[:, :, None] == jnp.arange(placement.shape[0], dtype=jnp.int32)
    slot = jnp.sum(jnp.where(picks, placement, 0), axis=2)
    here = slot[:, :, None] == slots
    named = jnp.any(here, axis=1)
    weight = jnp.sum(jnp.where(here, route_weight[:, :, None], 0.0), axis=1)
    table = jnp.where(named, weight, -1.0).T[None]

    heads, tails = (w_pair[:hid], w_down[:depth]), (w_pair[hid:], w_down[depth:])
    far, near, table_far, crossed, *tails = tie(
        hop(tokens, "z", 2), hop(tokens, "z", 1), hop(table, "z", 2), hop(w_pair, "core"), *tails
    )
    crossed = crossed[hid:]
    table = jnp.concatenate([table, table_far])
    lane_pair = jnp.where(own, heads[0], crossed)
    apart, table_near, lane_pair = tie(hop(far, "z", 1), hop(table, "z", 1), lane_pair)
    table = jnp.concatenate([table, table_near])
    arrived_pair = hop(lane_pair, "z", 2)

    valid = placement[0] >= 0
    *staged, tail_down, counts = guarded(
        valid, gather_stage, tokens, near, far, apart, tails[1], table, w_pair
    )
    lane_down = jnp.where(own, heads[1], tail_down)
    (*late, early_own, early_cross, x_other, scale, arrived_pair, lane_down) = tie(
        *staged[0], *staged[1], staged[2], arrived_pair, lane_down
    )
    arrived_down = hop(lane_down, "z", 2)
    handed_pair = hop(arrived_pair, "core")
    line, total, leave = guarded(
        valid, expert_stage, late, (early_own, early_cross, x_other), scale, w_pair, w_down
    )
    line, total, leave, arrived_down = tie(line, total, leave, arrived_down)
    over, closing = hop(line, "z", 2), hop(leave, "z", 1)
    handed_pair, handed_down, *last = tie(handed_pair, hop(arrived_down, "core"), *tails)
    partner = (slots + half * jnp.tile(swap_flag, 2)) % ncol
    column_load = jnp.sum(
        jnp.where(partner[:, None] == slots[None, :], counts[None, :], 0.0), axis=1
    ) / jnp.float32(rows * topk)

    rest_pair, rest_down = lax.cond(
        both, lambda a, b: (hop(a, "z", 2), hop(b, "z", 2)), lambda a, b: (a, b), *last
    )
    sources = (arrived_pair, handed_pair, rest_pair, w_pair)
    flags = jnp.stack([own, alone]).astype(jnp.int32)
    slot_gate_up = assemble(flags, sources).reshape(gate_up.shape)
    slot_down = jnp.concatenate(
        [
            jnp.where(own, arrived_down, heads[1]),
            jnp.where(alone, handed_down, rest_down),
        ]
    )[None]
    over, closing, slot_gate_up, slot_down = tie(over, closing, slot_gate_up, slot_down)
    moe_out = (total + wide(closing) + wide(over)).astype(jnp.bfloat16)
    return (moe_out, column_load, slot_gate_up, slot_down)


def from_behind(value, axis, steps):
    count = lax.axis_size(axis)
    pairs = [(source, (source + steps) % count) for source in range(count)]
    return lax.ppermute(value, axis, pairs)


def swapped_blocks(gate_up, down_weight, swap_flag, pair_index, half):
    incoming_pair = from_behind(gate_up, "expert", half)
    incoming_down = from_behind(down_weight, "expert", half)
    own_column = lax.axis_index("expert")
    own_flag = jnp.sum(jnp.where(pair_index == own_column % half, swap_flag, 0))
    pair_after = jnp.where(own_flag == 1, incoming_pair, gate_up)
    down_after = jnp.where(own_flag == 1, incoming_down, down_weight)
    return (pair_after, down_after)


def dispatched_body(tokens, expert_ids, route_weight, placement, swap_flag, gate_up, down_weight):
    ncol = lax.axis_size("expert")
    half = ncol // 2
    rows_here, feat_here = tokens.shape
    topk = expert_ids.shape[1]
    hid_here = gate_up.shape[2]
    width = gate_up.shape[3]
    capacity = max(4, rows_here * topk * 17 // (16 * ncol) + 2)
    experts_all = placement.shape[0]
    pair_index = jnp.arange(half, dtype=jnp.int32)
    hits = placement[:, None] % half == pair_index[None, :]
    flag_of = jnp.sum(jnp.where(hits, swap_flag[None, :], 0), axis=1)
    moved = (placement + half * flag_of) % ncol
    picks = expert_ids.reshape(-1)[:, None] == jnp.arange(experts_all, dtype=jnp.int32)[None, :]
    moved_dest = jnp.sum(jnp.where(picks, moved[None, :], 0), axis=1)
    columns = jnp.arange(ncol, dtype=jnp.int32)
    local_counts = jnp.sum((moved_dest[:, None] == columns[None, :]).astype(jnp.float32), axis=0)
    totals = lax.psum(local_counts, "expert")
    column_load = totals / jnp.float32(rows_here * topk)
    slot_gate_up, slot_down = swapped_blocks(gate_up, down_weight, swap_flag, pair_index, half)
    col_hits = moved_dest[:, None] == columns[None, :]
    order = jnp.cumsum(col_hits.astype(jnp.int32), axis=0) - 1
    position = jnp.sum(jnp.where(col_hits, order, 0), axis=1)
    slot_index = moved_dest * capacity + position
    w_pair = slot_gate_up.reshape(2 * hid_here, width)
    w_down = slot_down.reshape(slot_down.shape[1], feat_here)
    contract = (((1,), (1,)), ((), ()))
    whole = lax.all_gather(tokens, "dp", axis=1, tiled=True)
    repeated = jnp.repeat(whole, topk, axis=0)
    buffer = jnp.zeros((ncol * capacity, width), jnp.bfloat16).at[slot_index].set(repeated)
    buffer = buffer.reshape(ncol, capacity, width)
    received = lax.all_to_all(buffer, "expert", split_axis=0, concat_axis=0, tiled=True)
    blocks, count, wide = received.shape
    rows = received.reshape(blocks * count, wide)
    projected = lax.dot_general(rows, w_pair, contract, preferred_element_type=jnp.float32)
    hidden = (jax.nn.silu(projected[:, :hid_here]) * projected[:, hid_here:]).astype(jnp.bfloat16)
    mixed = jnp.dot(
        lax.all_gather(hidden, "dp", axis=1, tiled=True), w_down, preferred_element_type=jnp.float32
    )
    result = mixed.astype(jnp.bfloat16).reshape(blocks, count, feat_here)
    returned = lax.all_to_all(result, "expert", split_axis=0, concat_axis=0, tiled=True)
    flat_back = returned.reshape(ncol * capacity, feat_here)
    gathered = flat_back[slot_index].astype(jnp.float32).reshape(rows_here, topk, feat_here)
    moe_out = jnp.sum(gathered * route_weight[:, :, None], axis=1).astype(jnp.bfloat16)
    return (moe_out, column_load, slot_gate_up, slot_down)


def solution(mesh):
    expert = mesh.shape["expert"]
    if expert != 16 or mesh.shape["dp"] != 2:
        run, names, column = dispatched_body, mesh, "expert"
    else:
        shape = (mesh.shape["dp"], expert // 4, 2, 2)
        run, names, column = body, Mesh(mesh.devices.reshape(shape), ("dp", *COLUMN)), COLUMN
    return jax.shard_map(
        run,
        mesh=names,
        in_specs=(
            P(column, "dp"),
            P(column, None),
            P(column, None),
            P(),
            P(),
            P(column, None, "dp", None),
            P(column, None, "dp"),
        ),
        out_specs=(P(column, "dp"), P(), P(column, None, "dp", None), P(column, None, "dp")),
        check_vma=False,
    )
```
